32 devices in a mesh: parts: 2 (over y), ta: 4 (over z), gz: 2 (over x), sa: 2 (over core).
Axes of the slice: x: 2, y: 2, z: 4, core: 2. Of those that a mesh axis runs over, the one named last changes fastest.
Arguments:
- iterate: float32 [4, 4, 3, 24, 4, 2, 256], P('parts', None, None, 'sa', 'ta', 'gz'), parts along dimension 0, may hold values from -1.2 to 1.2
- source: float32 [4, 4, 3, 24, 4, 2, 256], P('parts', None, None, 'sa', 'ta', 'gz'), parts along dimension 0, may hold values from -6 to 6
- gauge_links: float32 [8, 18, 4, 2, 256], P('parts', None, 'ta', 'gz'), parts along dimension 0, may hold values from -1 to 1, as said below
Outputs:
- residual: float32 [4, 4, 3, 24, 4, 2, 256], P('parts', None, None, 'sa', 'ta', 'gz'), parts along dimension 0
- corrected: float32 [4, 4, 3, 24, 4, 2, 256], P('parts', None, None, 'sa', 'ta', 'gz'), parts along dimension 0
The draws below stay inside these ranges and needn't reach their ends.
There are 2 independent parts, one for each index of `parts`. The reference program is written for one: setup_inputs(seed, part) draws one part's arguments, and reference() takes and returns one part's arrays. A program takes and returns all parts, laid end to end along the dimension named above; each array names one. Nothing has to cross between parts.
Inputs may be any that keep to these rules, and one draw needn't show every extreme that they name: `gauge_links`: each 3 x 3 complex link matrix is special unitary.
All inputs are finite; a program needn't handle non-finite values.
Results may differ from the reference program's by a relative error of at most 0.00026.
Values sent between devices are 32-bit elements; how exact they have to be, the bound alone decides.
No kernel may reach another device: no remote copies, remote signals or barrier semaphores. Data moves between devices by JAX's collectives and lax.ppermute only.
A program may use at most 192 MiB of HBM per device.

```python
import jax
import jax.numpy as jnp
import numpy as np
from jax import lax

NX = 32
NY = 8
LS = 24
LS8 = 8
ITERS = 3
NT = 4
NZ = 2


def normalized(rows_block):
    length = jnp.sqrt(jnp.sum(rows_block * rows_block, axis=(1, 2), keepdims=True))
    return rows_block / length


def draw_gauge_links(key, part):
    key = jax.random.fold_in(key, 11)
    site_shape = (NT, NZ, NY * NX)
    raw_links = jax.random.normal(key, (4, 2, 3, 3) + site_shape, jnp.float32)
    first_row = normalized(raw_links[:, :, 0])
    second_raw = raw_links[:, :, 1]
    proj_real = jnp.sum(first_row[:, 0] * second_raw[:, 0] + first_row[:, 1] * second_raw[:, 1], axis=1, keepdims=True)
    proj_imag = jnp.sum(first_row[:, 0] * second_raw[:, 1] - first_row[:, 1] * second_raw[:, 0], axis=1, keepdims=True)
    second_row = normalized(jnp.stack([second_raw[:, 0] - (proj_real * first_row[:, 0] - proj_imag * first_row[:, 1]), second_raw[:, 1] - (proj_real * first_row[:, 1] + proj_imag * first_row[:, 0])], axis=1))
    first_real, first_imag = (first_row[:, 0], first_row[:, 1])
    second_real, second_imag = (second_row[:, 0], second_row[:, 1])
    third_real = []
    third_imag = []
    for component in range(3):
        next_one = (component + 1) % 3
        next_two = (component + 2) % 3
        cross_real = first_real[:, next_one] * second_real[:, next_two] - first_imag[:, next_one] * second_imag[:, next_two] - first_real[:, next_two] * second_real[:, next_one] + first_imag[:, next_two] * second_imag[:, next_one]
        cross_imag = first_real[:, next_one] * second_imag[:, next_two] + first_imag[:, next_one] * second_real[:, next_two] - first_real[:, next_two] * second_imag[:, next_one] - first_imag[:, next_two] * second_real[:, next_one]
        third_real.append(cross_real)
        third_imag.append(-cross_imag)
    third_row = jnp.stack([jnp.stack(third_real, axis=1), jnp.stack(third_imag, axis=1)], axis=1)
    matrix = jnp.stack([first_row, second_row, third_row], axis=2)
    return matrix.reshape((4, 18) + site_shape)


def block_levels(own_key, extent, split, low, top_value):
    def one(axis_at, blocks):
        heights = jax.random.uniform(jax.random.fold_in(jax.random.fold_in(own_key, 6), axis_at), (blocks,), jnp.float32, low / len(split), top_value / len(split))
        return jnp.repeat(jnp.exp(heights), extent[axis_at] // blocks).reshape((-1,) + (1,) * (len(extent) - axis_at - 1))

    loudness = one(*split[0])
    for cut in split[1:]:
        loudness = loudness * one(*cut)
    return loudness


def centred(stream_key, dims, deviation, most, shards=(), held_as=jnp.bfloat16):
    drawn = deviation * jax.random.normal(stream_key, dims, jnp.float32)
    if shards:
        drawn = drawn * block_levels(stream_key, dims, shards, -0.22, 0.18)
    return jnp.clip(drawn, -most, most).astype(held_as)


def setup_inputs(seed: int = 0, part: int = 0) -> dict:
    splits = jax.random.split(jax.random.key(seed), 4)
    own_keys = jax.random.split(jax.random.fold_in(splits[3], part), 4)
    iterate = centred(own_keys[0], (2, 4, 3, LS, NT, NZ, NY * NX), 0.2, 1.2, ((3, 2), (4, 4), (5, 2)), jnp.float32)
    source = centred(own_keys[1], (2, 4, 3, LS, NT, NZ, NY * NX), 1.0, 6.0, ((3, 2), (4, 4), (5, 2)), jnp.float32)
    gauge_links = draw_gauge_links(jax.random.fold_in(jax.random.fold_in(splits[3], part), 71), part)
    return {"iterate": iterate, "source": source, "gauge_links": gauge_links}


WALL_HEIGHT = 1.8
OUTER_SCALE = 1.5
OUTER_SHIFT = 0.5
INNER_SCALE = 1.25
INNER_SHIFT = 0.25
QUARK_MASS = 0.05
EPSILON = 1e-6
HIGHEST = lax.Precision.HIGHEST


def gamma_tables():
    pauli_list = [np.array([[0, 1], [1, 0]], complex), np.array([[0, -1j], [1j, 0]], complex), np.array([[1, 0], [0, -1]], complex)]
    gammas = []
    for pauli_matrix in pauli_list:
        matrix = np.zeros((4, 4), complex)
        matrix[0:2, 2:4] = -1j * pauli_matrix
        matrix[2:4, 0:2] = 1j * pauli_matrix
        gammas.append(matrix)
    fourth = np.zeros((4, 4), complex)
    fourth[0:2, 2:4] = np.eye(2)
    fourth[2:4, 0:2] = np.eye(2)
    gammas.append(fourth)
    tables = np.zeros((4, 2, 8, 8), np.float32)
    for direction in range(4):
        for sign_slot, sign_value in enumerate((-1.0, 1.0)):
            matrix = np.eye(4) + sign_value * gammas[direction]
            tables[direction, sign_slot, :4, :4] = matrix.real
            tables[direction, sign_slot, :4, 4:] = -matrix.imag
            tables[direction, sign_slot, 4:, :4] = matrix.imag
            tables[direction, sign_slot, 4:, 4:] = matrix.real
    return tables


def spin_apply(matrix, spinor):
    flattened = spinor.reshape((8,) + spinor.shape[2:])
    product = jnp.einsum("pq,q...->p...", jnp.asarray(matrix, spinor.dtype), flattened, precision=HIGHEST)
    return product.reshape(spinor.shape)


def color_apply(link_field, spinor, dagger):
    formula = "batzw,sbtzw->satzw" if dagger else "abtzw,sbtzw->satzw"

    def contract(matrix_part, spinor_part):
        return jnp.einsum(formula, matrix_part, spinor_part, precision=HIGHEST)

    if dagger:
        real_part = contract(link_field[0], spinor[0]) + contract(link_field[1], spinor[1])
        imag_part = contract(link_field[0], spinor[1]) - contract(link_field[1], spinor[0])
    else:
        real_part = contract(link_field[0], spinor[0]) - contract(link_field[1], spinor[1])
        imag_part = contract(link_field[0], spinor[1]) + contract(link_field[1], spinor[0])
    return jnp.stack([real_part, imag_part])


def shifted(spinor, direction, offset, antiperiodic):
    if direction == 3:
        rolled = jnp.roll(spinor, -offset, axis=-3)
        if antiperiodic:
            edge_slot = spinor.shape[-3] - 1 if offset > 0 else 0
            sign_table = jnp.ones((spinor.shape[-3], 1, 1), spinor.dtype).at[edge_slot].set(-1.0)
            rolled = rolled * sign_table
        return rolled
    if direction == 2:
        return jnp.roll(spinor, -offset, axis=-2)
    lattice = spinor.reshape(spinor.shape[:-1] + (NY, NX))
    return jnp.roll(lattice, -offset, axis=-2 if direction == 1 else -1).reshape(spinor.shape)


def wilson(spinor, link_set):
    tables = gamma_tables()
    total = (4.0 - WALL_HEIGHT) * spinor
    for direction in range(4):
        forward = color_apply(link_set[direction], shifted(spinor, direction, 1, True), False)
        backward = color_apply(shifted(link_set[direction], direction, -1, False), shifted(spinor, direction, -1, True), True)
        total = total - 0.5 * (spin_apply(tables[direction, 0], forward) + spin_apply(tables[direction, 1], backward))
    return total


def mobius(iterate, link_set, scale_weight, shift_weight):
    upper_slices = jnp.roll(iterate, -1, axis=3).at[:, :, :, -1].multiply(-QUARK_MASS)
    lower_slices = jnp.roll(iterate, 1, axis=3).at[:, :, :, 0].multiply(-QUARK_MASS)
    chiral_mix = jnp.concatenate([lower_slices[:, :2], upper_slices[:, 2:]], axis=1)
    blended = scale_weight * iterate + shift_weight * chiral_mix
    hopped = lax.map(lambda slab_piece: wilson(slab_piece, link_set), jnp.moveaxis(blended, 3, 0))
    return jnp.moveaxis(hopped, 0, 3) + iterate - chiral_mix


def project_plus(spinor):
    return jnp.concatenate([spinor[:, :2], jnp.zeros_like(spinor[:, 2:])], axis=1)


def project_minus(spinor):
    return jnp.concatenate([jnp.zeros_like(spinor[:, :2]), spinor[:, 2:]], axis=1)


def complex_scale(coef_real, coef_imag, spinor):
    return jnp.stack([coef_real * spinor[0] - coef_imag * spinor[1], coef_real * spinor[1] + coef_imag * spinor[0]])


def reference(iterate, source, gauge_links):
    link_set = gauge_links.reshape((4, 2, 3, 3) + gauge_links.shape[2:])
    residual = source - mobius(iterate, link_set, OUTER_SCALE, OUTER_SHIFT)
    blank = jnp.zeros(residual.shape[:3] + (LS8 - 2,) + residual.shape[4:], residual.dtype)
    inner_source = jnp.concatenate([project_minus(residual[:, :, :, :1]), blank, project_plus(residual[:, :, :, -1:])], axis=3)
    correction = jnp.zeros_like(inner_source)
    remainder = inner_source
    for iteration in range(ITERS):
        applied = mobius(remainder, link_set, INNER_SCALE, INNER_SHIFT)
        inner_real = jnp.sum(applied[0] * remainder[0] + applied[1] * remainder[1])
        inner_imag = jnp.sum(applied[0] * remainder[1] - applied[1] * remainder[0])
        weight = jnp.sum(applied * applied) + EPSILON
        alpha_real = inner_real / weight
        alpha_imag = inner_imag / weight
        correction = correction + complex_scale(alpha_real, alpha_imag, remainder)
        remainder = remainder - complex_scale(alpha_real, alpha_imag, applied)
    corrected = iterate.at[:, :, :, :1].add(project_minus(correction[:, :, :, :1]))
    corrected = corrected.at[:, :, :, -1:].add(project_plus(correction[:, :, :, -1:]))
    return residual, corrected
```

```python
import jax
import jax.numpy as jnp
import numpy as np
from jax import lax
from jax.experimental import pallas as pl
from jax.experimental.pallas import tpu as pltpu
from jax.sharding import PartitionSpec as P

NX = 32
LS = 24
LS8 = 8
ITERS = 3


WALL_HEIGHT = 1.8
OUTER_SCALE = 1.5
OUTER_SHIFT = 0.5
INNER_SCALE = 1.25
INNER_SHIFT = 0.25
QUARK_MASS = 0.05
EPSILON = 1e-06
HIGHEST = lax.Precision.HIGHEST


def padded_2(array, sides, width):
    for axis, dim in sides:
        count, length = (lax.axis_size(axis), array.shape[dim])
        up = [(i, (i + 1) % count) for i in range(count)]
        down = [(j, i) for i, j in up]
        last = lax.slice_in_dim(array, length - width, length, axis=dim)
        first = lax.slice_in_dim(array, 0, width, axis=dim)
        before = lax.ppermute(last, axis, up)
        after = lax.ppermute(first, axis, down)
        array = jnp.concatenate([before, array, after], axis=dim)
    return array


def shifted(block, axis, distance):
    devices = range(lax.axis_size(axis))
    route = [((i - distance) % len(devices), i) for i in devices]
    return lax.ppermute(block, axis, route)


def gamma_tables():
    pauli_list = [
        np.array([[0, 1], [1, 0]], complex),
        np.array([[0, -1j], [1j, 0]], complex),
        np.array([[1, 0], [0, -1]], complex),
    ]
    gammas = []
    for pauli_matrix in pauli_list:
        matrix = np.zeros((4, 4), complex)
        matrix[0:2, 2:4] = -1j * pauli_matrix
        matrix[2:4, 0:2] = 1j * pauli_matrix
        gammas.append(matrix)
    fourth = np.zeros((4, 4), complex)
    fourth[0:2, 2:4] = np.eye(2)
    fourth[2:4, 0:2] = np.eye(2)
    gammas.append(fourth)
    tables = np.zeros((4, 2, 8, 8), np.float32)
    for direction in range(4):
        for sign_slot, sign_value in enumerate((-1.0, 1.0)):
            matrix = np.eye(4) + sign_value * gammas[direction]
            tables[direction, sign_slot, :4, :4] = matrix.real
            tables[direction, sign_slot, :4, 4:] = -matrix.imag
            tables[direction, sign_slot, 4:, :4] = matrix.imag
            tables[direction, sign_slot, 4:, 4:] = matrix.real
    return tables


def spin_apply(matrix, spinor):
    flattened = spinor.reshape((8,) + spinor.shape[2:])
    product = jnp.einsum(
        "pq,q...->p...", jnp.asarray(matrix, spinor.dtype), flattened, precision=HIGHEST
    )
    return product.reshape(spinor.shape)


def color_apply(link_field, spinor, dagger):
    formula = "batzw,sbltzw->saltzw" if dagger else "abtzw,sbltzw->saltzw"

    def contract(matrix_part, spinor_part):
        return jnp.einsum(formula, matrix_part, spinor_part, precision=HIGHEST)

    if dagger:
        real_part = contract(link_field[0], spinor[0]) + contract(link_field[1], spinor[1])
        imag_part = contract(link_field[0], spinor[1]) - contract(link_field[1], spinor[0])
    else:
        real_part = contract(link_field[0], spinor[0]) - contract(link_field[1], spinor[1])
        imag_part = contract(link_field[0], spinor[1]) + contract(link_field[1], spinor[0])
    return jnp.stack([real_part, imag_part])


def along_x(spinor, offset):
    lattice = spinor.reshape(spinor.shape[:-1] + (spinor.shape[-1] // NX, NX))
    return jnp.roll(lattice, -offset, axis=-1).reshape(spinor.shape)


def along_y(spinor, offset):
    lattice = spinor.reshape(spinor.shape[:-1] + (spinor.shape[-1] // NX, NX))
    return jnp.roll(lattice, -offset, axis=-2).reshape(spinor.shape)


def project_plus(spinor):
    return jnp.concatenate([spinor[:, :2], jnp.zeros_like(spinor[:, 2:])], axis=1)


def project_minus(spinor):
    return jnp.concatenate([jnp.zeros_like(spinor[:, :2]), spinor[:, 2:]], axis=1)


def complex_scale(coef_real, coef_imag, spinor):
    return jnp.stack(
        [
            coef_real * spinor[0] - coef_imag * spinor[1],
            coef_real * spinor[1] + coef_imag * spinor[0],
        ]
    )


def padded_rims(padded):
    return (
        padded[:, :, :, :, :1, 1:-1],
        padded[:, :, :, :, -1:, 1:-1],
        padded[:, :, :, :, 1:-1, :1],
        padded[:, :, :, :, 1:-1, -1:],
    )


def time_signs():
    position = lax.axis_index("ta")
    sign_low = jnp.where(position == 0, -1.0, 1.0).astype(jnp.float32)
    sign_high = jnp.where(position == lax.axis_size("ta") - 1, -1.0, 1.0).astype(jnp.float32)
    return (sign_low, sign_high)


def slice_masses():
    position = lax.axis_index("sa")
    mass_low = jnp.where(position == 0, -QUARK_MASS, 1.0).astype(jnp.float32)
    mass_high = jnp.where(position == lax.axis_size("sa") - 1, -QUARK_MASS, 1.0).astype(jnp.float32)
    return (mass_low, mass_high)


def slice_mix(spinor, low_rim, high_rim, mass_low, mass_high):
    lower_part = jnp.concatenate([mass_low * low_rim, spinor[:, :2, :, :-1]], axis=3)
    upper_part = jnp.concatenate([spinor[:, 2:, :, 1:], mass_high * high_rim], axis=3)
    return jnp.concatenate([lower_part, upper_part], axis=1)


def hopping(centre, rims, here_links, down_links, y_forward, y_backward):
    tables = gamma_tables()
    sign_low, sign_high = time_signs()
    low_time, high_time, low_depth, high_depth = rims
    forward = [
        along_x(centre, 1),
        y_forward,
        jnp.concatenate([centre[:, :, :, :, :, 1:], high_depth], axis=5),
        jnp.concatenate([centre[:, :, :, :, 1:], sign_high * high_time], axis=4),
    ]
    backward = [
        along_x(centre, -1),
        y_backward,
        jnp.concatenate([low_depth, centre[:, :, :, :, :, :-1]], axis=5),
        jnp.concatenate([sign_low * low_time, centre[:, :, :, :, :-1]], axis=4),
    ]
    total = (4.0 - WALL_HEIGHT) * centre
    for direction in range(4):
        going = color_apply(here_links[direction], forward[direction], False)
        coming = color_apply(down_links[direction], backward[direction], True)
        total = total - 0.5 * (
            spin_apply(tables[direction, 0], going) + spin_apply(tables[direction, 1], coming)
        )
    return total


def outer_operator(iterate, here_links, down_links):
    mass_low, mass_high = slice_masses()
    with_rims = padded_2(iterate, (("sa", 3),), 1)
    low_rim = with_rims[:, :2, :, :1]
    high_rim = with_rims[:, 2:, :, -1:]
    chiral_mix = slice_mix(iterate, low_rim, high_rim, mass_low, mass_high)
    blended = OUTER_SCALE * iterate + OUTER_SHIFT * chiral_mix
    rims = padded_rims(padded_2(blended, (("ta", 4), ("gz", 5)), 1))
    hopped = hopping(
        blended, rims, here_links, down_links, along_y(blended, 1), along_y(blended, -1)
    )
    return hopped + iterate - chiral_mix


def inner_rows_operator(remainder, here_links, down_links):
    chiral_mix = slice_mix(
        remainder, remainder[:, :2, :, -1:], remainder[:, 2:, :, :1], -QUARK_MASS, -QUARK_MASS
    )
    blended = INNER_SCALE * remainder + INNER_SHIFT * chiral_mix
    rims = padded_rims(padded_2(blended, (("ta", 4), ("gz", 5)), 1))
    row_rims = padded_2(blended, (("sa", 6),), NX)
    y_forward = row_rims[..., 2 * NX :]
    y_backward = row_rims[..., : -2 * NX]
    hopped = hopping(blended, rims, here_links, down_links, y_forward, y_backward)
    return hopped + remainder - chiral_mix


def minimal_residual(inner_source, operator, here_links, down_links):
    correction = jnp.zeros_like(inner_source)
    remainder = inner_source
    for iteration in range(ITERS):
        applied = operator(remainder, here_links, down_links)
        inner_real, inner_imag, weight = lax.psum(
            (
                jnp.sum(applied[0] * remainder[0] + applied[1] * remainder[1]),
                jnp.sum(applied[0] * remainder[1] - applied[1] * remainder[0]),
                jnp.sum(applied * applied),
            ),
            ("ta", "gz", "sa"),
        )
        weight = weight + EPSILON
        alpha_real = inner_real / weight
        alpha_imag = inner_imag / weight
        correction = correction + complex_scale(alpha_real, alpha_imag, remainder)
        remainder = remainder - complex_scale(alpha_real, alpha_imag, applied)
    return correction


def body(iterate, source, gauge_links):
    span = gauge_links.shape[-1]
    link_set = gauge_links.reshape((4, 2, 3, 3) + gauge_links.shape[2:])
    rim_time = shifted(gauge_links[3, :, -1:], "ta", 1)
    rim_depth = shifted(gauge_links[2, :, :, -1:], "gz", 1)
    down_time = jnp.concatenate([rim_time, gauge_links[3, :, :-1]], axis=1).reshape(
        link_set.shape[1:]
    )
    down_depth = jnp.concatenate([rim_depth, gauge_links[2, :, :, :-1]], axis=2).reshape(
        link_set.shape[1:]
    )
    here_links = [link_set[0], link_set[1], link_set[2], link_set[3]]
    down_links = [along_x(link_set[0], -1), along_y(link_set[1], -1), down_depth, down_time]
    residual = source - outer_operator(iterate, here_links, down_links)
    core_index = lax.axis_index("sa")
    local_slices = iterate.shape[3]
    global_slice = core_index * local_slices + jnp.arange(local_slices)
    first_mask = (global_slice == 0).astype(jnp.float32).reshape(-1, 1, 1, 1)
    last_mask = (global_slice == LS - 1).astype(jnp.float32).reshape(-1, 1, 1, 1)
    surface_piece = jnp.where(
        core_index == 0, project_minus(residual[:, :, :, :1]), project_plus(residual[:, :, :, -1:])
    )
    surface_slots = lax.all_to_all(surface_piece, "sa", split_axis=6, concat_axis=3, tiled=True)
    blank = jnp.zeros(surface_slots.shape[:3] + (LS8 - 2,) + surface_slots.shape[4:], jnp.float32)
    inner_source = jnp.concatenate(
        [surface_slots[:, :, :, :1], blank, surface_slots[:, :, :, 1:]], axis=3
    )
    row_width = span // lax.axis_size("sa")
    row_start = core_index * row_width
    here_rows = [
        lax.dynamic_slice_in_dim(link_field, row_start, row_width, 5) for link_field in here_links
    ]
    down_rows = [
        lax.dynamic_slice_in_dim(link_field, row_start, row_width, 5) for link_field in down_links
    ]
    correction = minimal_residual(inner_source, inner_rows_operator, here_rows, down_rows)
    returned = jnp.concatenate(
        [project_minus(correction[:, :, :, :1]), project_plus(correction[:, :, :, -1:])], axis=3
    )
    received = lax.all_to_all(returned, "sa", split_axis=3, concat_axis=6, tiled=True)
    corrected = iterate + received * (first_mask + last_mask)
    return (residual, corrected)


UPPER = [ri * 12 + sp * 3 + c for ri in range(2) for sp in (0, 1) for c in range(3)]
LOWER = [ri * 12 + sp * 3 + c for ri in range(2) for sp in (2, 3) for c in range(3)]
RE, IM = 0, 1
SPIN = (
    (((1, 1, IM), (-1, 1, RE)), ((1, 0, IM), (-1, 0, RE))),
    (((-1, 1, RE), (-1, 1, IM)), ((1, 0, RE), (1, 0, IM))),
    (((1, 0, IM), (-1, 0, RE)), ((-1, 1, IM), (1, 1, RE))),
    (((1, 0, RE), (1, 0, IM)), ((1, 1, RE), (1, 1, IM))),
)
ROWS = 24
FIELD = 576
LINKS = 72
BLOCK = 144
MESSAGE = 2 * BLOCK
VMEM_LIMIT = 48 * 1024 * 1024


def number(part, spin, color):
    return part * 12 + spin * 3 + color


def half_spinor(get, direction, side):
    out = {}
    for spin in range(2):
        for part in range(2):
            sign, from_spin, from_part = SPIN[direction][spin][part]
            for color in range(3):
                up = get(number(part, spin, color))
                low = get(number(from_part, 2 + from_spin, color))
                out[spin, part, color] = up + low if sign * side > 0 else up - low
    return out


def link_times(link, half, dagger):
    out = {}
    for row in range(3):
        for spin in range(2):
            real, imag = (None, None)
            for col in range(3):
                a, b = (col, row) if dagger else (row, col)
                ur, ui = (link(RE, a, b), link(IM, a, b))
                hr, hi = (half[spin, RE, col], half[spin, IM, col])
                if dagger:
                    re_new, im_new = (ur * hr + ui * hi, ur * hi - ui * hr)
                else:
                    re_new, im_new = (ur * hr - ui * hi, ur * hi + ui * hr)
                real = re_new if real is None else real + re_new
                imag = im_new if imag is None else imag + im_new
            out[spin, RE, row] = real
            out[spin, IM, row] = imag
    return out


def add_hop(acc, half, direction, side):
    flip = 1 if direction == 3 else -1
    for spin in range(2):
        for part in range(2):
            sign, from_spin, from_part = SPIN[direction][spin][part]
            for color in range(3):
                up = number(part, spin, color)
                acc[up] = acc[up] + half[spin, part, color]
                low = number(part, 2 + spin, color)
                g = half[from_spin, from_part, color]
                acc[low] = acc[low] + g if sign * side * flip > 0 else acc[low] - g
    return acc


def roll(x, shift, axis):
    return pltpu.roll(x, shift % x.shape[axis], axis)


def lane():
    return lax.broadcasted_iota(jnp.int32, (8, 128), 1)


def sublane():
    return lax.broadcasted_iota(jnp.int32, (8, 128), 0)


def move_x(x, offset):
    edge = lane() % NX == (NX - 1 if offset > 0 else 0)
    return jnp.where(edge, roll(x, offset * (NX - 1), 1), roll(x, -offset, 1))


def move_y(x, offset):
    near = roll(x, -offset * NX, 1)
    far = jnp.where(sublane() % 2 == 0, roll(near, -1, 0), roll(near, 1, 0))
    edge = lane() // NX == (3 if offset > 0 else 0)
    return jnp.where(edge, far, near)


def move_t(x, offset):
    return roll(x, -offset * 2, 0)


def pairs(x):
    return jnp.concatenate([x, x, x, x], axis=0)


def scaled_links(gauge_ref, tile_ref, slot, direction, scale):
    for entry in range(18):
        row = (direction * 18 + entry) * 2
        tile_ref[slot * 18 + entry] = pairs(gauge_ref[row : row + 2, :]) * scale


def tile_link(tile_ref, slot):
    return lambda part, a, b: tile_ref[slot * 18 + part * 9 + a * 3 + b]


def blend_rows(out_ref, here_ref, there_ref, mass_low, mass_high):
    row = lax.broadcasted_iota(jnp.int32, (ROWS, 128), 0)
    for comp in range(24):
        rows = slice(comp * ROWS, (comp + 1) * ROWS)
        v, other = (here_ref[rows, :], there_ref[rows, :])
        if comp in UPPER:
            chi = jnp.where(row < 2, roll(other, 2, 0) * mass_low, roll(v, 2, 0))
        else:
            chi = jnp.where(row >= ROWS - 2, roll(other, -2, 0) * mass_high, roll(v, -2, 0))
        out_ref[rows, :] = OUTER_SCALE * v + OUTER_SHIFT * chi


def send_kernel(own_ref, oth_ref, src_own_ref, src_oth_ref, gauge_ref, mt_ref, mz_ref, blk_ref, bl_ref, blo_ref, tile_ref):
    core = lax.axis_index("sa")
    last_time = lax.axis_index("ta") == lax.axis_size("ta") - 1
    time_scale = jnp.where(last_time, 0.5, -0.5).astype(jnp.float32)
    first = jnp.where(core == 0, -QUARK_MASS, 1.0).astype(jnp.float32)
    last = jnp.where(core == 0, 1.0, -QUARK_MASS).astype(jnp.float32)
    blend_rows(bl_ref, own_ref, oth_ref, first, last)
    blend_rows(blo_ref, oth_ref, own_ref, last, first)

    sign_row = lax.broadcasted_iota(jnp.int32, (LINKS, 128), 0) >= 54
    link_sign = jnp.where(jnp.logical_and(sign_row, last_time), 0.5, -0.5).astype(jnp.float32)
    for h in range(2):
        base = h * BLOCK
        blk_ref[base : base + LINKS, :] = gauge_ref[pl.ds(h, LINKS, stride=2), :] * link_sign

    def surfaces(bl0_ref, it0_ref, src0_ref, bl1_ref, it1_ref, src1_ref):
        for h in range(2):
            base = h * BLOCK + LINKS
            blk_ref[base : base + 24, :] = bl0_ref[pl.ds(h, 24, stride=ROWS), :]
            blk_ref[base + 24 : base + 48, :] = bl1_ref[pl.ds(22 + h, 24, stride=ROWS), :]
            for part in range(2):
                start = (part * 12 + 6) * ROWS + h
                value = (
                    src0_ref[pl.ds(start, 6, stride=ROWS), :]
                    - it0_ref[pl.ds(start, 6, stride=ROWS), :]
                    + it0_ref[pl.ds(start + 2, 6, stride=ROWS), :]
                )
                blk_ref[base + 48 + part * 6 : base + 54 + part * 6, :] = value
                start = part * 12 * ROWS + 22 + h
                value = (
                    src1_ref[pl.ds(start, 6, stride=ROWS), :]
                    - it1_ref[pl.ds(start, 6, stride=ROWS), :]
                    + it1_ref[pl.ds(start - 2, 6, stride=ROWS), :]
                )
                blk_ref[base + 60 + part * 6 : base + 66 + part * 6, :] = value

    pl.when(core == 0)(lambda: surfaces(bl_ref, own_ref, src_own_ref, blo_ref, oth_ref, src_oth_ref))
    pl.when(core == 1)(lambda: surfaces(blo_ref, oth_ref, src_oth_ref, bl_ref, own_ref, src_own_ref))

    scaled_links(gauge_ref, tile_ref, 0, 2, -0.5)
    scaled_links(gauge_ref, tile_ref, 1, 3, time_scale)

    def store(ref, half, offset, g):
        for (spin, part, color), value in half.items():
            ref[pl.ds(offset + (part * 6 + spin * 3 + color) * ROWS + g * 8, 8), :] = value

    def getter(ref, g):
        return lambda comp: ref[pl.ds(comp * ROWS + g * 8, 8), :]

    for g in range(3):
        get = getter(bl_ref, g)
        store(mz_ref, half_spinor(get, 2, -1), 0, g)
        store(mz_ref, link_times(tile_link(tile_ref, 0), half_spinor(get, 2, 1), True), 288, g)

    def time_up(first_ref, second_ref):
        for which, ref in enumerate((first_ref, second_ref)):
            for g in range(3):
                half = half_spinor(getter(ref, g), 3, 1)
                store(mt_ref, link_times(tile_link(tile_ref, 1), half, True), which * 288, g)

    def time_down(first_ref, second_ref):
        for which, ref in enumerate((first_ref, second_ref)):
            for g in range(3):
                store(mt_ref, half_spinor(getter(ref, g), 3, -1), which * 288, g)

    pl.when(core == 0)(lambda: time_up(bl_ref, blo_ref))
    pl.when(core == 1)(lambda: time_down(blo_ref, bl_ref))
    mt_ref[FIELD : FIELD + MESSAGE, :] = blk_ref[...]
    mz_ref[FIELD : FIELD + MESSAGE, :] = blk_ref[...]


def local_kernel(own_ref, bl_ref, src_ref, gauge_ref, acc_ref, tile_ref):
    scaled_links(gauge_ref, tile_ref, 0, 0, -0.5)
    scaled_links(gauge_ref, tile_ref, 1, 1, -0.5)

    def group(g, carry):
        def rows(comp):
            return pl.ds(pl.multiple_of(comp * ROWS + g * 8, 8), 8)

        get = lambda comp: bl_ref[rows(comp), :]
        acc = [0.2 * get(comp) + 4.0 * own_ref[rows(comp), :] - src_ref[rows(comp), :] for comp in range(24)]
        for direction, move in ((0, move_x), (1, move_y)):
            link = tile_link(tile_ref, direction)
            half = {k: move(h, 1) for k, h in half_spinor(get, direction, -1).items()}
            acc = add_hop(acc, link_times(link, half, False), direction, -1)
            half = link_times(link, half_spinor(get, direction, 1), True)
            acc = add_hop(acc, {k: move(h, -1) for k, h in half.items()}, direction, 1)
        for comp in range(24):
            acc_ref[rows(comp), :] = acc[comp]
        return carry

    lax.fori_loop(0, 3, group, 0)


def inner_kernel(own_ref, x2_ref, x1a_ref, x1b_ref, x3a_ref, x3b_ref, x4a_ref, x4b_ref, out_ref, gather_ref, link_ref, base_ref, r_ref, a_ref, z_ref, sem):
    core = lax.axis_index("sa")
    pick = lambda zero, one: jnp.where(core == 0, zero, one)
    placed = (
        (own_ref, 0, 0),
        (x2_ref, FIELD, 4),
        (x1a_ref, FIELD, pick(3, 1)),
        (x1b_ref, FIELD, pick(1, 3)),
        (x3a_ref, 0, pick(2, 5)),
        (x3b_ref, 0, pick(5, 2)),
        (x4a_ref, 0, pick(7, 6)),
        (x4b_ref, 0, pick(6, 7)),
    )
    copies = []
    for i, (ref, start, slot) in enumerate(placed):
        to = gather_ref.at[pl.ds(pl.multiple_of(slot * MESSAGE, 8), MESSAGE), :]
        copies.append(pltpu.make_async_copy(ref.at[pl.ds(start, MESSAGE), :], to, sem.at[i]))
        copies[-1].start()
    zero = jnp.zeros((8, 128), jnp.float32)
    for s in range(8):
        for comp in range(24):
            for dz in range(2):
                r_ref[s, comp, dz] = zero
    for copy in copies:
        copy.wait()

    def gathered(comp, dz):
        return gather_ref[pl.ds(dz * 8 * BLOCK + comp, 8, stride=BLOCK), :]

    for dz in range(2):
        for entry in range(LINKS):
            link_ref[entry, dz] = gathered(entry, dz)
        for comp in range(24):
            z_ref[0, comp, dz] = gathered(LINKS + comp, dz)
            z_ref[1, comp, dz] = gathered(LINKS + 24 + comp, dz)
        for i in range(24):
            base_ref[i, dz] = gathered(LINKS + 48 + i, dz)

    def hops(slot, dz, acc):
        def link(direction, at):
            return lambda part, a, b: link_ref[direction * 18 + part * 9 + a * 3 + b, at]

        here = lambda comp: z_ref[slot, comp, dz]
        there = lambda comp: z_ref[slot, comp, 1 - dz]
        for direction, move in ((0, move_x), (1, move_y), (3, move_t)):
            half = {k: move(h, 1) for k, h in half_spinor(here, direction, -1).items()}
            acc = add_hop(acc, link_times(link(direction, dz), half, False), direction, -1)
            half = link_times(link(direction, dz), half_spinor(here, direction, 1), True)
            acc = add_hop(acc, {k: move(h, -1) for k, h in half.items()}, direction, 1)
        half = half_spinor(there, 2, -1)
        acc = add_hop(acc, link_times(link(2, dz), half, False), 2, -1)
        half = link_times(link(2, 1 - dz), half_spinor(there, 2, 1), True)
        return add_hop(acc, half, 2, 1)

    def surface(k, carry):
        for dz in range(2):
            acc = [2.2 * z_ref[k, comp, dz] for comp in range(24)]
            acc = hops(k, dz, acc)
            for comp in range(24):
                a_ref[k, comp, dz] = acc[comp]
        return carry

    lax.fori_loop(0, 2, surface, 0)
    for i, comp in enumerate(LOWER):
        for dz in range(2):
            r_ref[0, comp, dz] = base_ref[i, dz] - a_ref[0, comp, dz]
    for i, comp in enumerate(UPPER):
        for dz in range(2):
            r_ref[7, comp, dz] = base_ref[12 + i, dz] - a_ref[1, comp, dz]
    for i in range(24):
        out_ref[i] = zero

    def step(iteration, carry):
        def one(j, sums):
            s = jnp.where(j <= iteration, j, 8 + iteration - j)
            before = jnp.where(s == 0, 7, s - 1)
            after = jnp.where(s == 7, 0, s + 1)
            low = jnp.where(s == 0, -QUARK_MASS, 1.0).astype(jnp.float32)
            high = jnp.where(s == 7, -QUARK_MASS, 1.0).astype(jnp.float32)
            for dz in range(2):
                for comp in range(24):
                    chi = r_ref[before, comp, dz] * low if comp in UPPER else r_ref[after, comp, dz] * high
                    z_ref[0, comp, dz] = INNER_SCALE * r_ref[s, comp, dz] + INNER_SHIFT * chi
            real, imag, weight = sums
            for dz in range(2):
                acc = [6.0 * r_ref[s, comp, dz] - 1.8 * z_ref[0, comp, dz] for comp in range(24)]
                acc = hops(0, dz, acc)
                for i in range(12):
                    ar, ai = (acc[i], acc[i + 12])
                    rr, ri = (r_ref[s, i, dz], r_ref[s, i + 12, dz])
                    real = real + ar * rr + ai * ri
                    imag = imag + ar * ri - ai * rr
                    weight = weight + ar * ar + ai * ai
                for comp in range(24):
                    a_ref[s, comp, dz] = acc[comp]
            return (real, imag, weight)

        count = 2 * (iteration + 1)
        real, imag, weight = lax.fori_loop(0, count, one, (zero, zero, zero))
        total = lambda x: jnp.sum(x, axis=(0, 1), keepdims=True)
        scale = total(weight) + EPSILON
        alpha_real = jnp.broadcast_to(total(real) / scale, (8, 128))
        alpha_imag = jnp.broadcast_to(total(imag) / scale, (8, 128))
        for slot, (s, comps) in enumerate(((0, LOWER), (7, UPPER))):
            for i in range(6):
                rr, ri = (r_ref[s, comps[i], 0], r_ref[s, comps[i + 6], 0])
                at = slot * 12 + i
                out_ref[at] = out_ref[at] + alpha_real * rr - alpha_imag * ri
                out_ref[at + 6] = out_ref[at + 6] + alpha_real * ri + alpha_imag * rr

        def update(j, c):
            s = jnp.where(j <= iteration, j, 8 + iteration - j)
            for dz in range(2):
                for i in range(12):
                    ar, ai = (a_ref[s, i, dz], a_ref[s, i + 12, dz])
                    r_ref[s, i, dz] = r_ref[s, i, dz] - (alpha_real * ar - alpha_imag * ai)
                    r_ref[s, i + 12, dz] = r_ref[s, i + 12, dz] - (alpha_real * ai + alpha_imag * ar)
            return c

        lax.fori_loop(0, jnp.where(iteration == ITERS - 1, 0, count), update, 0)
        return carry

    lax.fori_loop(0, ITERS, step, 0)


def final_kernel(own_ref, acc_ref, gauge_ref, ta_ref, tb_ref, mz_ref, corr_ref, res_ref, cor_ref, tile_ref):
    core = lax.axis_index("sa")
    last_time = lax.axis_index("ta") == lax.axis_size("ta") - 1
    time_scale = jnp.where(last_time, 0.5, -0.5).astype(jnp.float32)
    scaled_links(gauge_ref, tile_ref, 0, 2, -0.5)
    scaled_links(gauge_ref, tile_ref, 1, 3, time_scale)

    def finish(up_ref, down_ref, offset):
        def group(g, carry):
            def rows(comp, start=0):
                return pl.ds(pl.multiple_of(start + comp * ROWS + g * 8, 8), 8)

            def half(ref, start):
                return {
                    (spin, part, color): ref[rows(part * 6 + spin * 3 + color, start), :]
                    for spin in range(2)
                    for part in range(2)
                    for color in range(3)
                }

            acc = [acc_ref[rows(comp), :] for comp in range(24)]
            acc = add_hop(acc, link_times(tile_link(tile_ref, 0), half(mz_ref, 0), False), 2, -1)
            acc = add_hop(acc, half(mz_ref, 288), 2, 1)
            acc = add_hop(acc, link_times(tile_link(tile_ref, 1), half(down_ref, offset), False), 3, -1)
            acc = add_hop(acc, half(up_ref, offset), 3, 1)
            for comp in range(24):
                res_ref[rows(comp), :] = -acc[comp]
            return carry

        lax.fori_loop(0, 3, group, 0)

    cor_ref[...] = own_ref[...]

    def add_surface(s, comps, first):
        for i, comp in enumerate(comps):
            rows = slice(comp * ROWS + 2 * s, comp * ROWS + 2 * s + 2)
            cor_ref[rows, :] = cor_ref[rows, :] + corr_ref[first + i, 0:2, :]

    @pl.when(core == 0)
    def _():
        finish(ta_ref, tb_ref, 0)
        add_surface(0, LOWER, 0)

    @pl.when(core == 1)
    def _():
        finish(tb_ref, ta_ref, 288)
        add_surface(11, UPPER, 12)


def cost(flops, moved):
    return pl.CostEstimate(flops=flops, bytes_accessed=moved, transcendentals=0)


def call(kernel, outs, scratch, in_specs, flops, moved, *args):
    shapes = [jax.ShapeDtypeStruct(s, jnp.float32) for s in outs]
    return pl.pallas_call(
        kernel,
        out_shape=shapes,
        in_specs=in_specs,
        out_specs=[pl.BlockSpec(memory_space=pltpu.VMEM)] * len(outs),
        scratch_shapes=scratch,
        cost_estimate=cost(flops, moved),
        compiler_params=pltpu.CompilerParams(vmem_limit_bytes=VMEM_LIMIT),
    )(*args)


def small_body(iterate, source, gauge_links):
    whole = iterate.shape
    own = iterate.reshape(FIELD, 128)
    src = source.reshape(FIELD, 128)
    gauge = gauge_links.reshape(2 * LINKS, 128)
    swap = [(0, 1), (1, 0)]
    oth = lax.ppermute(own, "sa", swap)
    src_oth = lax.ppermute(src, "sa", swap)
    vmem = pl.BlockSpec(memory_space=pltpu.VMEM)
    anywhere = pl.BlockSpec(memory_space=pl.ANY)
    f32 = jnp.float32
    mt, mz, blk, bl = call(
        send_kernel,
        [(FIELD + MESSAGE, 128), (FIELD + MESSAGE, 128), (MESSAGE, 128), (FIELD, 128)],
        [pltpu.VMEM((FIELD, 128), f32), pltpu.VMEM((36, 8, 128), f32)],
        [vmem] * 5,
        4_000_000,
        3_000_000,
        own, oth, src, src_oth, gauge,
    )

    def route(where):
        pairs_out = []
        for t in range(4):
            for z in range(2):
                for s in range(2):
                    dt, dz = where(s)
                    to = ((t + dt) % 4) * 4 + ((z + dz) % 2) * 2 + s
                    pairs_out.append((t * 4 + z * 2 + s, to))
        return pairs_out

    axes = ("ta", "gz", "sa")
    x1 = lax.ppermute(mt, axes, route(lambda s: (1, 0) if s == 0 else (-1, 0)))
    x4 = lax.ppermute(blk, axes, route(lambda s: (1, 1) if s == 0 else (2, 1)))
    x3 = lax.ppermute(blk, axes, route(lambda s: (2, 0) if s == 0 else (-1, 1)))
    x2 = lax.ppermute(mz, axes, route(lambda s: (0, 1)))
    x1b = lax.ppermute(x1, "sa", swap)
    x3b = lax.ppermute(x3, "sa", swap)
    x4b = lax.ppermute(x4, "sa", swap)
    acc = call(
        local_kernel,
        [(FIELD, 128)],
        [pltpu.VMEM((36, 8, 128), f32)],
        [vmem] * 4,
        4_000_000,
        2_000_000,
        own, bl, src, gauge,
    )[0]
    corr = call(
        inner_kernel,
        [(24, 8, 128)],
        [
            pltpu.VMEM((8 * MESSAGE, 128), f32),
            pltpu.VMEM((LINKS, 2, 8, 128), f32),
            pltpu.VMEM((24, 2, 8, 128), f32),
            pltpu.VMEM((8, 24, 2, 8, 128), f32),
            pltpu.VMEM((8, 24, 2, 8, 128), f32),
            pltpu.VMEM((2, 24, 2, 8, 128), f32),
            pltpu.SemaphoreType.DMA((8,)),
        ],
        [anywhere] * 8,
        40_000_000,
        2_000_000,
        blk, x2, x1, x1b, x3, x3b, x4, x4b,
    )[0]
    residual, corrected = call(
        final_kernel,
        [(FIELD, 128), (FIELD, 128)],
        [pltpu.VMEM((36, 8, 128), f32)],
        [vmem] * 7,
        4_000_000,
        3_000_000,
        own, acc, gauge, x1, x1b, x2, corr,
    )
    return (residual.reshape(whole), corrected.reshape(whole))


def solution(mesh):
    placed = (
        P("parts", None, None, "sa", "ta", "gz", None),
        P("parts", None, None, "sa", "ta", "gz", None),
        P("parts", None, "ta", "gz", None),
    )
    small = (mesh.shape["ta"], mesh.shape["gz"], mesh.shape["sa"]) == (4, 2, 2)

    def chosen(iterate, source, gauge_links):
        one_block = iterate.shape[3:] == (12, 1, 1, 256)
        return (small_body if small and one_block else body)(iterate, source, gauge_links)

    return jax.shard_map(
        chosen,
        mesh=mesh,
        in_specs=placed,
        out_specs=(
            P("parts", None, None, "sa", "ta", "gz", None),
            P("parts", None, None, "sa", "ta", "gz", None),
        ),
        check_vma=False,
    )
```

```python
import jax
import jax.numpy as jnp
import numpy as np
from jax import lax
from jax.experimental import pallas as pl
from jax.experimental.pallas import tpu as pltpu
from jax.sharding import PartitionSpec as P

NX = 32
LS = 24
LS8 = 8
ITERS = 3


WALL_HEIGHT = 1.8
OUTER_SCALE = 1.5
OUTER_SHIFT = 0.5
INNER_SCALE = 1.25
INNER_SHIFT = 0.25
QUARK_MASS = 0.05
EPSILON = 1e-06
HIGHEST = lax.Precision.HIGHEST


def padded_2(array, sides, width):
    for axis, dim in sides:
        count, length = (lax.axis_size(axis), array.shape[dim])
        up = [(i, (i + 1) % count) for i in range(count)]
        down = [(j, i) for i, j in up]
        last = lax.slice_in_dim(array, length - width, length, axis=dim)
        first = lax.slice_in_dim(array, 0, width, axis=dim)
        before = lax.ppermute(last, axis, up)
        after = lax.ppermute(first, axis, down)
        array = jnp.concatenate([before, array, after], axis=dim)
    return array


def shifted(block, axis, distance):
    devices = range(lax.axis_size(axis))
    route = [((i - distance) % len(devices), i) for i in devices]
    return lax.ppermute(block, axis, route)


def gamma_tables():
    pauli_list = [
        np.array([[0, 1], [1, 0]], complex),
        np.array([[0, -1j], [1j, 0]], complex),
        np.array([[1, 0], [0, -1]], complex),
    ]
    gammas = []
    for pauli_matrix in pauli_list:
        matrix = np.zeros((4, 4), complex)
        matrix[0:2, 2:4] = -1j * pauli_matrix
        matrix[2:4, 0:2] = 1j * pauli_matrix
        gammas.append(matrix)
    fourth = np.zeros((4, 4), complex)
    fourth[0:2, 2:4] = np.eye(2)
    fourth[2:4, 0:2] = np.eye(2)
    gammas.append(fourth)
    tables = np.zeros((4, 2, 8, 8), np.float32)
    for direction in range(4):
        for sign_slot, sign_value in enumerate((-1.0, 1.0)):
            matrix = np.eye(4) + sign_value * gammas[direction]
            tables[direction, sign_slot, :4, :4] = matrix.real
            tables[direction, sign_slot, :4, 4:] = -matrix.imag
            tables[direction, sign_slot, 4:, :4] = matrix.imag
            tables[direction, sign_slot, 4:, 4:] = matrix.real
    return tables


def spin_apply(matrix, spinor):
    flattened = spinor.reshape((8,) + spinor.shape[2:])
    product = jnp.einsum(
        "pq,q...->p...", jnp.asarray(matrix, spinor.dtype), flattened, precision=HIGHEST
    )
    return product.reshape(spinor.shape)


def color_apply(link_field, spinor, dagger):
    formula = "batzw,sbltzw->saltzw" if dagger else "abtzw,sbltzw->saltzw"

    def contract(matrix_part, spinor_part):
        return jnp.einsum(formula, matrix_part, spinor_part, precision=HIGHEST)

    if dagger:
        real_part = contract(link_field[0], spinor[0]) + contract(link_field[1], spinor[1])
        imag_part = contract(link_field[0], spinor[1]) - contract(link_field[1], spinor[0])
    else:
        real_part = contract(link_field[0], spinor[0]) - contract(link_field[1], spinor[1])
        imag_part = contract(link_field[0], spinor[1]) + contract(link_field[1], spinor[0])
    return jnp.stack([real_part, imag_part])


def along_x(spinor, offset):
    lattice = spinor.reshape(spinor.shape[:-1] + (spinor.shape[-1] // NX, NX))
    return jnp.roll(lattice, -offset, axis=-1).reshape(spinor.shape)


def along_y(spinor, offset):
    lattice = spinor.reshape(spinor.shape[:-1] + (spinor.shape[-1] // NX, NX))
    return jnp.roll(lattice, -offset, axis=-2).reshape(spinor.shape)


def project_plus(spinor):
    return jnp.concatenate([spinor[:, :2], jnp.zeros_like(spinor[:, 2:])], axis=1)


def project_minus(spinor):
    return jnp.concatenate([jnp.zeros_like(spinor[:, :2]), spinor[:, 2:]], axis=1)


def complex_scale(coef_real, coef_imag, spinor):
    return jnp.stack(
        [
            coef_real * spinor[0] - coef_imag * spinor[1],
            coef_real * spinor[1] + coef_imag * spinor[0],
        ]
    )


def padded_rims(padded):
    return (
        padded[:, :, :, :, :1, 1:-1],
        padded[:, :, :, :, -1:, 1:-1],
        padded[:, :, :, :, 1:-1, :1],
        padded[:, :, :, :, 1:-1, -1:],
    )


def time_signs():
    position = lax.axis_index("ta")
    sign_low = jnp.where(position == 0, -1.0, 1.0).astype(jnp.float32)
    sign_high = jnp.where(position == lax.axis_size("ta") - 1, -1.0, 1.0).astype(jnp.float32)
    return (sign_low, sign_high)


def slice_masses():
    position = lax.axis_index("sa")
    mass_low = jnp.where(position == 0, -QUARK_MASS, 1.0).astype(jnp.float32)
    mass_high = jnp.where(position == lax.axis_size("sa") - 1, -QUARK_MASS, 1.0).astype(jnp.float32)
    return (mass_low, mass_high)


def slice_mix(spinor, low_rim, high_rim, mass_low, mass_high):
    lower_part = jnp.concatenate([mass_low * low_rim, spinor[:, :2, :, :-1]], axis=3)
    upper_part = jnp.concatenate([spinor[:, 2:, :, 1:], mass_high * high_rim], axis=3)
    return jnp.concatenate([lower_part, upper_part], axis=1)


def hopping(centre, rims, here_links, down_links, y_forward, y_backward):
    tables = gamma_tables()
    sign_low, sign_high = time_signs()
    low_time, high_time, low_depth, high_depth = rims
    forward = [
        along_x(centre, 1),
        y_forward,
        jnp.concatenate([centre[:, :, :, :, :, 1:], high_depth], axis=5),
        jnp.concatenate([centre[:, :, :, :, 1:], sign_high * high_time], axis=4),
    ]
    backward = [
        along_x(centre, -1),
        y_backward,
        jnp.concatenate([low_depth, centre[:, :, :, :, :, :-1]], axis=5),
        jnp.concatenate([sign_low * low_time, centre[:, :, :, :, :-1]], axis=4),
    ]
    total = (4.0 - WALL_HEIGHT) * centre
    for direction in range(4):
        going = color_apply(here_links[direction], forward[direction], False)
        coming = color_apply(down_links[direction], backward[direction], True)
        total = total - 0.5 * (
            spin_apply(tables[direction, 0], going) + spin_apply(tables[direction, 1], coming)
        )
    return total


def outer_operator(iterate, here_links, down_links):
    mass_low, mass_high = slice_masses()
    with_rims = padded_2(iterate, (("sa", 3),), 1)
    low_rim = with_rims[:, :2, :, :1]
    high_rim = with_rims[:, 2:, :, -1:]
    chiral_mix = slice_mix(iterate, low_rim, high_rim, mass_low, mass_high)
    blended = OUTER_SCALE * iterate + OUTER_SHIFT * chiral_mix
    rims = padded_rims(padded_2(blended, (("ta", 4), ("gz", 5)), 1))
    hopped = hopping(
        blended, rims, here_links, down_links, along_y(blended, 1), along_y(blended, -1)
    )
    return hopped + iterate - chiral_mix


def inner_rows_operator(remainder, here_links, down_links):
    chiral_mix = slice_mix(
        remainder, remainder[:, :2, :, -1:], remainder[:, 2:, :, :1], -QUARK_MASS, -QUARK_MASS
    )
    blended = INNER_SCALE * remainder + INNER_SHIFT * chiral_mix
    rims = padded_rims(padded_2(blended, (("ta", 4), ("gz", 5)), 1))
    row_rims = padded_2(blended, (("sa", 6),), NX)
    y_forward = row_rims[..., 2 * NX :]
    y_backward = row_rims[..., : -2 * NX]
    hopped = hopping(blended, rims, here_links, down_links, y_forward, y_backward)
    return hopped + remainder - chiral_mix


def minimal_residual(inner_source, operator, here_links, down_links):
    correction = jnp.zeros_like(inner_source)
    remainder = inner_source
    for iteration in range(ITERS):
        applied = operator(remainder, here_links, down_links)
        inner_real, inner_imag, weight = lax.psum(
            (
                jnp.sum(applied[0] * remainder[0] + applied[1] * remainder[1]),
                jnp.sum(applied[0] * remainder[1] - applied[1] * remainder[0]),
                jnp.sum(applied * applied),
            ),
            ("ta", "gz", "sa"),
        )
        weight = weight + EPSILON
        alpha_real = inner_real / weight
        alpha_imag = inner_imag / weight
        correction = correction + complex_scale(alpha_real, alpha_imag, remainder)
        remainder = remainder - complex_scale(alpha_real, alpha_imag, applied)
    return correction


def body(iterate, source, gauge_links):
    span = gauge_links.shape[-1]
    link_set = gauge_links.reshape((4, 2, 3, 3) + gauge_links.shape[2:])
    rim_time = shifted(gauge_links[3, :, -1:], "ta", 1)
    rim_depth = shifted(gauge_links[2, :, :, -1:], "gz", 1)
    down_time = jnp.concatenate([rim_time, gauge_links[3, :, :-1]], axis=1).reshape(
        link_set.shape[1:]
    )
    down_depth = jnp.concatenate([rim_depth, gauge_links[2, :, :, :-1]], axis=2).reshape(
        link_set.shape[1:]
    )
    here_links = [link_set[0], link_set[1], link_set[2], link_set[3]]
    down_links = [along_x(link_set[0], -1), along_y(link_set[1], -1), down_depth, down_time]
    residual = source - outer_operator(iterate, here_links, down_links)
    core_index = lax.axis_index("sa")
    local_slices = iterate.shape[3]
    global_slice = core_index * local_slices + jnp.arange(local_slices)
    first_mask = (global_slice == 0).astype(jnp.float32).reshape(-1, 1, 1, 1)
    last_mask = (global_slice == LS - 1).astype(jnp.float32).reshape(-1, 1, 1, 1)
    surface_piece = jnp.where(
        core_index == 0, project_minus(residual[:, :, :, :1]), project_plus(residual[:, :, :, -1:])
    )
    surface_slots = lax.all_to_all(surface_piece, "sa", split_axis=6, concat_axis=3, tiled=True)
    blank = jnp.zeros(surface_slots.shape[:3] + (LS8 - 2,) + surface_slots.shape[4:], jnp.float32)
    inner_source = jnp.concatenate(
        [surface_slots[:, :, :, :1], blank, surface_slots[:, :, :, 1:]], axis=3
    )
    row_width = span // lax.axis_size("sa")
    row_start = core_index * row_width
    here_rows = [
        lax.dynamic_slice_in_dim(link_field, row_start, row_width, 5) for link_field in here_links
    ]
    down_rows = [
        lax.dynamic_slice_in_dim(link_field, row_start, row_width, 5) for link_field in down_links
    ]
    correction = minimal_residual(inner_source, inner_rows_operator, here_rows, down_rows)
    returned = jnp.concatenate(
        [project_minus(correction[:, :, :, :1]), project_plus(correction[:, :, :, -1:])], axis=3
    )
    received = lax.all_to_all(returned, "sa", split_axis=3, concat_axis=6, tiled=True)
    corrected = iterate + received * (first_mask + last_mask)
    return (residual, corrected)


UPPER = [ri * 12 + sp * 3 + c for ri in range(2) for sp in (0, 1) for c in range(3)]
LOWER = [ri * 12 + sp * 3 + c for ri in range(2) for sp in (2, 3) for c in range(3)]
RE, IM = 0, 1
SPIN = (
    (((1, 1, IM), (-1, 1, RE)), ((1, 0, IM), (-1, 0, RE))),
    (((-1, 1, RE), (-1, 1, IM)), ((1, 0, RE), (1, 0, IM))),
    (((1, 0, IM), (-1, 0, RE)), ((-1, 1, IM), (1, 1, RE))),
    (((1, 0, RE), (1, 0, IM)), ((1, 1, RE), (1, 1, IM))),
)
ROWS = 24
FIELD = 576
LINKS = 72
SENT = 48
BLOCK = SENT + 72
MESSAGE = 2 * BLOCK
VMEM_LIMIT = 48 * 1024 * 1024


def number(part, spin, color):
    return part * 12 + spin * 3 + color


def half_spinor(get, direction, side):
    out = {}
    for spin in range(2):
        for part in range(2):
            sign, from_spin, from_part = SPIN[direction][spin][part]
            for color in range(3):
                up = get(number(part, spin, color))
                low = get(number(from_part, 2 + from_spin, color))
                out[spin, part, color] = up + low if sign * side > 0 else up - low
    return out


def link_times(link, half, dagger):
    out = {}
    for row in range(3):
        for spin in range(2):
            real, imag = (None, None)
            for col in range(3):
                a, b = (col, row) if dagger else (row, col)
                ur, ui = (link(RE, a, b), link(IM, a, b))
                hr, hi = (half[spin, RE, col], half[spin, IM, col])
                if dagger:
                    re_new, im_new = (ur * hr + ui * hi, ur * hi - ui * hr)
                else:
                    re_new, im_new = (ur * hr - ui * hi, ur * hi + ui * hr)
                real = re_new if real is None else real + re_new
                imag = im_new if imag is None else imag + im_new
            out[spin, RE, row] = real
            out[spin, IM, row] = imag
    return out


def add_hop(acc, half, direction, side):
    flip = 1 if direction == 3 else -1
    for spin in range(2):
        for part in range(2):
            sign, from_spin, from_part = SPIN[direction][spin][part]
            for color in range(3):
                up = number(part, spin, color)
                acc[up] = acc[up] + half[spin, part, color]
                low = number(part, 2 + spin, color)
                g = half[from_spin, from_part, color]
                acc[low] = acc[low] + g if sign * side * flip > 0 else acc[low] - g
    return acc


def roll(x, shift, axis):
    return pltpu.roll(x, shift % x.shape[axis], axis)


def lane():
    return lax.broadcasted_iota(jnp.int32, (8, 128), 1)


def sublane():
    return lax.broadcasted_iota(jnp.int32, (8, 128), 0)


def move_x(x, offset):
    edge = lane() % NX == (NX - 1 if offset > 0 else 0)
    return jnp.where(edge, roll(x, offset * (NX - 1), 1), roll(x, -offset, 1))


def move_y(x, offset):
    near = roll(x, -offset * NX, 1)
    far = jnp.where(sublane() % 2 == 0, roll(near, -1, 0), roll(near, 1, 0))
    edge = lane() // NX == (3 if offset > 0 else 0)
    return jnp.where(edge, far, near)


def move_t(x, offset):
    return roll(x, -offset * 2, 0)


def pairs(x):
    return jnp.concatenate([x, x, x, x], axis=0)


def scaled_links(gauge_ref, tile_ref, slot, direction, scale):
    for entry in range(18):
        row = (direction * 18 + entry) * 2
        tile_ref[slot * 18 + entry] = pairs(gauge_ref[row : row + 2, :]) * scale


def tile_link(tile_ref, slot):
    return lambda part, a, b: tile_ref[slot * 18 + part * 9 + a * 3 + b]


def blend_rows(out_ref, here_ref, there_ref, mass_low, mass_high):
    row = lax.broadcasted_iota(jnp.int32, (ROWS, 128), 0)
    for comp in range(24):
        rows = slice(comp * ROWS, (comp + 1) * ROWS)
        v, other = (here_ref[rows, :], there_ref[rows, :])
        if comp in UPPER:
            chi = jnp.where(row < 2, roll(other, 2, 0) * mass_low, roll(v, 2, 0))
        else:
            chi = jnp.where(row >= ROWS - 2, roll(other, -2, 0) * mass_high, roll(v, -2, 0))
        out_ref[rows, :] = OUTER_SCALE * v + OUTER_SHIFT * chi


def stage_kernel(own_ref, src_ref, gauge_ref, own_out, src_out, gauge_out, sem):
    copies = []
    for i, (ref, out) in enumerate(((own_ref, own_out), (src_ref, src_out), (gauge_ref, gauge_out))):
        copies.append(pltpu.make_async_copy(ref, out, sem.at[i]))
        copies[-1].start()
    for copy in copies:
        copy.wait()


def send_kernel(own_ref, oth_ref, src_own_ref, src_oth_ref, gauge_ref, mt_ref, mz_ref, blk_ref, bl_ref, blo_ref, tile_ref):
    core = lax.axis_index("sa")
    last_time = lax.axis_index("ta") == lax.axis_size("ta") - 1
    time_scale = jnp.where(last_time, 0.5, -0.5).astype(jnp.float32)
    first = jnp.where(core == 0, -QUARK_MASS, 1.0).astype(jnp.float32)
    last = jnp.where(core == 0, 1.0, -QUARK_MASS).astype(jnp.float32)
    blend_rows(bl_ref, own_ref, oth_ref, first, last)
    blend_rows(blo_ref, oth_ref, own_ref, last, first)

    for h in range(2):
        for i in range(8):
            base = h * BLOCK + i * 6
            blk_ref[base : base + 6, :] = gauge_ref[pl.ds(i * 18 + h, 6, stride=2), :]

    def surfaces(bl0_ref, it0_ref, src0_ref, bl1_ref, it1_ref, src1_ref):
        for h in range(2):
            base = h * BLOCK + SENT
            blk_ref[base : base + 24, :] = bl0_ref[pl.ds(h, 24, stride=ROWS), :]
            blk_ref[base + 24 : base + 48, :] = bl1_ref[pl.ds(22 + h, 24, stride=ROWS), :]
            for part in range(2):
                start = (part * 12 + 6) * ROWS + h
                value = (
                    src0_ref[pl.ds(start, 6, stride=ROWS), :]
                    - it0_ref[pl.ds(start, 6, stride=ROWS), :]
                    + it0_ref[pl.ds(start + 2, 6, stride=ROWS), :]
                )
                blk_ref[base + 48 + part * 6 : base + 54 + part * 6, :] = value
                start = part * 12 * ROWS + 22 + h
                value = (
                    src1_ref[pl.ds(start, 6, stride=ROWS), :]
                    - it1_ref[pl.ds(start, 6, stride=ROWS), :]
                    + it1_ref[pl.ds(start - 2, 6, stride=ROWS), :]
                )
                blk_ref[base + 60 + part * 6 : base + 66 + part * 6, :] = value

    pl.when(core == 0)(lambda: surfaces(bl_ref, own_ref, src_own_ref, blo_ref, oth_ref, src_oth_ref))
    pl.when(core == 1)(lambda: surfaces(blo_ref, oth_ref, src_oth_ref, bl_ref, own_ref, src_own_ref))

    scaled_links(gauge_ref, tile_ref, 0, 2, -0.5)
    scaled_links(gauge_ref, tile_ref, 1, 3, time_scale)

    def store(ref, half, offset, g):
        for (spin, part, color), value in half.items():
            ref[pl.ds(offset + (part * 6 + spin * 3 + color) * ROWS + g * 8, 8), :] = value

    def getter(ref, g):
        return lambda comp: ref[pl.ds(comp * ROWS + g * 8, 8), :]

    for g in range(3):
        get = getter(bl_ref, g)
        store(mz_ref, half_spinor(get, 2, -1), 0, g)
        store(mz_ref, link_times(tile_link(tile_ref, 0), half_spinor(get, 2, 1), True), 288, g)

    def time_up(first_ref, second_ref):
        for which, ref in enumerate((first_ref, second_ref)):
            for g in range(3):
                half = half_spinor(getter(ref, g), 3, 1)
                store(mt_ref, link_times(tile_link(tile_ref, 1), half, True), which * 288, g)

    def time_down(first_ref, second_ref):
        for which, ref in enumerate((first_ref, second_ref)):
            for g in range(3):
                store(mt_ref, half_spinor(getter(ref, g), 3, -1), which * 288, g)

    pl.when(core == 0)(lambda: time_up(bl_ref, blo_ref))
    pl.when(core == 1)(lambda: time_down(blo_ref, bl_ref))


def halves(ref, rows, start):
    return {
        (spin, part, color): ref[rows(part * 6 + spin * 3 + color, start), :]
        for spin in range(2)
        for part in range(2)
        for color in range(3)
    }


def group_rows(g):
    return lambda comp, start=0: pl.ds(pl.multiple_of(start + comp * ROWS + g * 8, 8), 8)


def local_kernel(own_ref, bl_ref, src_ref, gauge_ref, mz_ref, corr_ref, acc_ref, cor_ref, tile_ref):
    core = lax.axis_index("sa")
    for direction in range(3):
        scaled_links(gauge_ref, tile_ref, direction, direction, -0.5)

    def group(g, carry):
        rows = group_rows(g)
        get = lambda comp: bl_ref[rows(comp), :]
        acc = [0.2 * get(comp) + 4.0 * own_ref[rows(comp), :] - src_ref[rows(comp), :] for comp in range(24)]
        for direction, move in ((0, move_x), (1, move_y)):
            link = tile_link(tile_ref, direction)
            half = {k: move(h, 1) for k, h in half_spinor(get, direction, -1).items()}
            acc = add_hop(acc, link_times(link, half, False), direction, -1)
            half = link_times(link, half_spinor(get, direction, 1), True)
            acc = add_hop(acc, {k: move(h, -1) for k, h in half.items()}, direction, 1)
        acc = add_hop(acc, link_times(tile_link(tile_ref, 2), halves(mz_ref, rows, 0), False), 2, -1)
        acc = add_hop(acc, halves(mz_ref, rows, 288), 2, 1)
        for comp in range(24):
            acc_ref[rows(comp), :] = acc[comp]
        return carry

    lax.fori_loop(0, 3, group, 0)
    cor_ref[...] = own_ref[...]

    def add_surface(s, comps, first):
        for i, comp in enumerate(comps):
            at = slice(comp * ROWS + 2 * s, comp * ROWS + 2 * s + 2)
            cor_ref[at, :] = cor_ref[at, :] + corr_ref[first + i, 0:2, :]

    pl.when(core == 0)(lambda: add_surface(0, LOWER, 0))
    pl.when(core == 1)(lambda: add_surface(11, UPPER, 12))


def inner_kernel(own_ref, x2_ref, x1a_ref, x1b_ref, x3a_ref, x3b_ref, x4a_ref, x4b_ref, out_ref, gather_ref, link_ref, base_ref, r_ref, a_ref, z_ref, sem):
    core = lax.axis_index("sa")
    pick = lambda zero, one: jnp.where(core == 0, zero, one)
    placed = (
        (own_ref, 0, 0),
        (x2_ref, 0, 4),
        (x1a_ref, 0, pick(3, 1)),
        (x1b_ref, 0, pick(1, 3)),
        (x3a_ref, 0, pick(2, 5)),
        (x3b_ref, 0, pick(5, 2)),
        (x4a_ref, 0, pick(7, 6)),
        (x4b_ref, 0, pick(6, 7)),
    )
    copies = []
    for i, (ref, start, slot) in enumerate(placed):
        to = gather_ref.at[pl.ds(pl.multiple_of(slot * MESSAGE, 8), MESSAGE), :]
        copies.append(pltpu.make_async_copy(ref.at[pl.ds(start, MESSAGE), :], to, sem.at[i]))
        copies[-1].start()
    zero = jnp.zeros((8, 128), jnp.float32)
    for s in range(8):
        for comp in range(24):
            for dz in range(2):
                r_ref[s, comp, dz] = zero
    for copy in copies:
        copy.wait()

    time = lax.rem(lax.axis_index("ta") + sublane() // 2, 4)
    time_scale = jnp.where(time == 3, 0.5, -0.5).astype(jnp.float32)

    def gathered(comp, dz):
        return gather_ref[pl.ds(dz * 8 * BLOCK + comp, 8, stride=BLOCK), :]

    for dz in range(2):
        for direction in range(4):
            scale = time_scale if direction == 3 else -0.5
            for part in range(2):
                for i in range(6):
                    entry = gathered(direction * 12 + part * 6 + i, dz) * (scale if i < 3 else 1.0)
                    link_ref[direction * 18 + part * 9 + i, dz] = entry
            for b in range(3):
                p, q = ((b + 1) % 3, (b + 2) % 3)
                row = lambda part, a, at: link_ref[direction * 18 + part * 9 + a * 3 + at, dz]
                real = (
                    row(RE, 0, p) * row(RE, 1, q) - row(IM, 0, p) * row(IM, 1, q)
                    - row(RE, 0, q) * row(RE, 1, p) + row(IM, 0, q) * row(IM, 1, p)
                )
                imag = (
                    row(RE, 0, q) * row(IM, 1, p) + row(IM, 0, q) * row(RE, 1, p)
                    - row(RE, 0, p) * row(IM, 1, q) - row(IM, 0, p) * row(RE, 1, q)
                )
                link_ref[direction * 18 + 6 + b, dz] = real
                link_ref[direction * 18 + 15 + b, dz] = imag
            for part in range(2):
                for b in range(3):
                    at = direction * 18 + part * 9 + 3 + b
                    link_ref[at, dz] = link_ref[at, dz] * scale
        for comp in range(24):
            z_ref[0, comp, dz] = gathered(SENT + comp, dz)
            z_ref[1, comp, dz] = gathered(SENT + 24 + comp, dz)
        for i in range(24):
            base_ref[i, dz] = gathered(SENT + 48 + i, dz)

    def hops(slot, dz, acc):
        def link(direction, at):
            return lambda part, a, b: link_ref[direction * 18 + part * 9 + a * 3 + b, at]

        here = lambda comp: z_ref[slot, comp, dz]
        there = lambda comp: z_ref[slot, comp, 1 - dz]
        for direction, move in ((0, move_x), (1, move_y), (3, move_t)):
            half = {k: move(h, 1) for k, h in half_spinor(here, direction, -1).items()}
            acc = add_hop(acc, link_times(link(direction, dz), half, False), direction, -1)
            half = link_times(link(direction, dz), half_spinor(here, direction, 1), True)
            acc = add_hop(acc, {k: move(h, -1) for k, h in half.items()}, direction, 1)
        half = half_spinor(there, 2, -1)
        acc = add_hop(acc, link_times(link(2, dz), half, False), 2, -1)
        half = link_times(link(2, 1 - dz), half_spinor(there, 2, 1), True)
        return add_hop(acc, half, 2, 1)

    def surface(k, carry):
        for dz in range(2):
            acc = [2.2 * z_ref[k, comp, dz] for comp in range(24)]
            acc = hops(k, dz, acc)
            for comp in range(24):
                a_ref[k, comp, dz] = acc[comp]
        return carry

    lax.fori_loop(0, 2, surface, 0)
    for i, comp in enumerate(LOWER):
        for dz in range(2):
            r_ref[0, comp, dz] = base_ref[i, dz] - a_ref[0, comp, dz]
    for i, comp in enumerate(UPPER):
        for dz in range(2):
            r_ref[7, comp, dz] = base_ref[12 + i, dz] - a_ref[1, comp, dz]
    for i in range(24):
        out_ref[i] = zero

    def step(iteration, carry):
        def one(j, sums):
            s = jnp.where(j <= iteration, j, 8 + iteration - j)
            before = jnp.where(s == 0, 7, s - 1)
            after = jnp.where(s == 7, 0, s + 1)
            low = jnp.where(s == 0, -QUARK_MASS, 1.0).astype(jnp.float32)
            high = jnp.where(s == 7, -QUARK_MASS, 1.0).astype(jnp.float32)
            for dz in range(2):
                for comp in range(24):
                    chi = r_ref[before, comp, dz] * low if comp in UPPER else r_ref[after, comp, dz] * high
                    z_ref[0, comp, dz] = INNER_SCALE * r_ref[s, comp, dz] + INNER_SHIFT * chi
            real, imag, weight = sums
            for dz in range(2):
                acc = [6.0 * r_ref[s, comp, dz] - 1.8 * z_ref[0, comp, dz] for comp in range(24)]
                acc = hops(0, dz, acc)
                for i in range(12):
                    ar, ai = (acc[i], acc[i + 12])
                    rr, ri = (r_ref[s, i, dz], r_ref[s, i + 12, dz])
                    real = real + ar * rr + ai * ri
                    imag = imag + ar * ri - ai * rr
                    weight = weight + ar * ar + ai * ai
                for comp in range(24):
                    a_ref[s, comp, dz] = acc[comp]
            return (real, imag, weight)

        count = 2 * (iteration + 1)
        real, imag, weight = lax.fori_loop(0, count, one, (zero, zero, zero))
        total = lambda x: jnp.sum(x, axis=(0, 1), keepdims=True)
        scale = total(weight) + EPSILON
        alpha_real = jnp.broadcast_to(total(real) / scale, (8, 128))
        alpha_imag = jnp.broadcast_to(total(imag) / scale, (8, 128))
        for slot, (s, comps) in enumerate(((0, LOWER), (7, UPPER))):
            for i in range(6):
                rr, ri = (r_ref[s, comps[i], 0], r_ref[s, comps[i + 6], 0])
                at = slot * 12 + i
                out_ref[at] = out_ref[at] + alpha_real * rr - alpha_imag * ri
                out_ref[at + 6] = out_ref[at + 6] + alpha_real * ri + alpha_imag * rr

        def update(j, c):
            s = jnp.where(j <= iteration, j, 8 + iteration - j)
            for dz in range(2):
                for i in range(12):
                    ar, ai = (a_ref[s, i, dz], a_ref[s, i + 12, dz])
                    r_ref[s, i, dz] = r_ref[s, i, dz] - (alpha_real * ar - alpha_imag * ai)
                    r_ref[s, i + 12, dz] = r_ref[s, i + 12, dz] - (alpha_real * ai + alpha_imag * ar)
            return c

        lax.fori_loop(0, jnp.where(iteration == ITERS - 1, 0, count), update, 0)
        return carry

    lax.fori_loop(0, ITERS, step, 0)


def final_kernel(acc_ref, gauge_ref, ta_ref, tb_ref, res_ref, tile_ref):
    core = lax.axis_index("sa")
    last_time = lax.axis_index("ta") == lax.axis_size("ta") - 1
    scaled_links(gauge_ref, tile_ref, 0, 3, jnp.where(last_time, 0.5, -0.5).astype(jnp.float32))

    def finish(up_ref, down_ref, offset):
        def group(g, carry):
            rows = group_rows(g)
            acc = [acc_ref[rows(comp), :] for comp in range(24)]
            acc = add_hop(acc, link_times(tile_link(tile_ref, 0), halves(down_ref, rows, offset), False), 3, -1)
            acc = add_hop(acc, halves(up_ref, rows, offset), 3, 1)
            for comp in range(24):
                res_ref[rows(comp), :] = -acc[comp]
            return carry

        lax.fori_loop(0, 3, group, 0)

    pl.when(core == 0)(lambda: finish(ta_ref, tb_ref, 0))
    pl.when(core == 1)(lambda: finish(tb_ref, ta_ref, 288))


def cost(flops, moved):
    return pl.CostEstimate(flops=flops, bytes_accessed=moved, transcendentals=0)


def call(kernel, outs, scratch, in_specs, flops, moved, *args, limit=VMEM_LIMIT):
    shapes = [jax.ShapeDtypeStruct(s, jnp.float32) for s in outs]
    return pl.pallas_call(
        kernel,
        out_shape=shapes,
        in_specs=in_specs,
        out_specs=[pl.BlockSpec(memory_space=pltpu.VMEM)] * len(outs),
        scratch_shapes=scratch,
        cost_estimate=cost(flops, moved),
        compiler_params=pltpu.CompilerParams(vmem_limit_bytes=limit),
    )(*args)


def small_body(iterate, source, gauge_links):
    whole = iterate.shape
    own = iterate.reshape(FIELD, 128)
    src = source.reshape(FIELD, 128)
    gauge = gauge_links.reshape(2 * LINKS, 128)
    swap = [(0, 1), (1, 0)]
    oth = lax.ppermute(own, "sa", swap)
    src_oth = lax.ppermute(src, "sa", swap)
    vmem = pl.BlockSpec(memory_space=pltpu.VMEM)
    anywhere = pl.BlockSpec(memory_space=pl.ANY)
    f32 = jnp.float32
    own, src, gauge = call(
        stage_kernel,
        [(FIELD, 128), (FIELD, 128), (2 * LINKS, 128)],
        [pltpu.SemaphoreType.DMA((3,))],
        [pl.BlockSpec(memory_space=pltpu.HBM)] * 3,
        0,
        1_300_000,
        own, src, gauge,
    )
    mt, mz, blk, bl = call(
        send_kernel,
        [(FIELD, 128), (FIELD, 128), (MESSAGE, 128), (FIELD, 128)],
        [pltpu.VMEM((FIELD, 128), f32), pltpu.VMEM((36, 8, 128), f32)],
        [vmem] * 5,
        4_000_000,
        3_000_000,
        own, oth, src, src_oth, gauge,
    )

    def route(where):
        pairs_out = []
        for t in range(4):
            for z in range(2):
                for s in range(2):
                    dt, dz = where(s)
                    to = ((t + dt) % 4) * 4 + ((z + dz) % 2) * 2 + s
                    pairs_out.append((t * 4 + z * 2 + s, to))
        return pairs_out

    axes = ("ta", "gz", "sa")
    x4 = lax.ppermute(blk, axes, route(lambda s: (1, 1) if s == 0 else (2, 1)))
    x3 = lax.ppermute(blk, axes, route(lambda s: (2, 0) if s == 0 else (-1, 1)))
    x1 = lax.ppermute(blk, axes, route(lambda s: (1, 0) if s == 0 else (-1, 0)))
    x2 = lax.ppermute(blk, axes, route(lambda s: (0, 1)))
    x1, x2, x3, x4, mt, mz = lax.optimization_barrier((x1, x2, x3, x4, mt, mz))
    ta = lax.ppermute(mt, axes, route(lambda s: (1, 0) if s == 0 else (-1, 0)))
    tz = lax.ppermute(mz, axes, route(lambda s: (0, 1)))
    x1b = lax.ppermute(x1, "sa", swap)
    x3b = lax.ppermute(x3, "sa", swap)
    x4b = lax.ppermute(x4, "sa", swap)
    corr = call(
        inner_kernel,
        [(24, 8, 128)],
        [
            pltpu.VMEM((8 * MESSAGE, 128), f32),
            pltpu.VMEM((LINKS, 2, 8, 128), f32),
            pltpu.VMEM((24, 2, 8, 128), f32),
            pltpu.VMEM((8, 24, 2, 8, 128), f32),
            pltpu.VMEM((8, 24, 2, 8, 128), f32),
            pltpu.VMEM((2, 24, 2, 8, 128), f32),
            pltpu.SemaphoreType.DMA((8,)),
        ],
        [anywhere] * 8,
        40_000_000,
        2_000_000,
        blk, x2, x1, x1b, x3, x3b, x4, x4b,
    )[0]
    ta, tz, corr = lax.optimization_barrier((ta, tz, corr))
    tb = lax.ppermute(ta, "sa", swap)
    acc, corrected = call(
        local_kernel,
        [(FIELD, 128), (FIELD, 128)],
        [pltpu.VMEM((54, 8, 128), f32)],
        [vmem] * 6,
        6_000_000,
        3_000_000,
        own, bl, src, gauge, tz, corr,
    )
    residual = call(
        final_kernel,
        [(FIELD, 128)],
        [pltpu.VMEM((18, 8, 128), f32)],
        [vmem] * 4,
        2_000_000,
        2_000_000,
        acc, gauge, ta, tb,
    )[0]
    return (residual.reshape(whole), corrected.reshape(whole))


def solution(mesh):
    placed = (
        P("parts", None, None, "sa", "ta", "gz", None),
        P("parts", None, None, "sa", "ta", "gz", None),
        P("parts", None, "ta", "gz", None),
    )
    small = (mesh.shape["ta"], mesh.shape["gz"], mesh.shape["sa"]) == (4, 2, 2)

    def chosen(iterate, source, gauge_links):
        one_block = iterate.shape[3:] == (12, 1, 1, 256)
        return (small_body if small and one_block else body)(iterate, source, gauge_links)

    return jax.shard_map(
        chosen,
        mesh=mesh,
        in_specs=placed,
        out_specs=(
            P("parts", None, None, "sa", "ta", "gz", None),
            P("parts", None, None, "sa", "ta", "gz", None),
        ),
        check_vma=False,
    )
```

```python
import jax
import jax.numpy as jnp
import numpy as np
from jax import lax
from jax.experimental import pallas as pl
from jax.experimental.pallas import tpu as pltpu
from jax.sharding import PartitionSpec as P

NX = 32
LS = 24
LS8 = 8
ITERS = 3


WALL_HEIGHT = 1.8
OUTER_SCALE = 1.5
OUTER_SHIFT = 0.5
INNER_SCALE = 1.25
INNER_SHIFT = 0.25
QUARK_MASS = 0.05
EPSILON = 1e-06
HIGHEST = lax.Precision.HIGHEST


def padded_2(array, sides, width):
    for axis, dim in sides:
        count, length = (lax.axis_size(axis), array.shape[dim])
        up = [(i, (i + 1) % count) for i in range(count)]
        down = [(j, i) for i, j in up]
        last = lax.slice_in_dim(array, length - width, length, axis=dim)
        first = lax.slice_in_dim(array, 0, width, axis=dim)
        before = lax.ppermute(last, axis, up)
        after = lax.ppermute(first, axis, down)
        array = jnp.concatenate([before, array, after], axis=dim)
    return array


def shifted(block, axis, distance):
    devices = range(lax.axis_size(axis))
    route = [((i - distance) % len(devices), i) for i in devices]
    return lax.ppermute(block, axis, route)


def gamma_tables():
    pauli_list = [
        np.array([[0, 1], [1, 0]], complex),
        np.array([[0, -1j], [1j, 0]], complex),
        np.array([[1, 0], [0, -1]], complex),
    ]
    gammas = []
    for pauli_matrix in pauli_list:
        matrix = np.zeros((4, 4), complex)
        matrix[0:2, 2:4] = -1j * pauli_matrix
        matrix[2:4, 0:2] = 1j * pauli_matrix
        gammas.append(matrix)
    fourth = np.zeros((4, 4), complex)
    fourth[0:2, 2:4] = np.eye(2)
    fourth[2:4, 0:2] = np.eye(2)
    gammas.append(fourth)
    tables = np.zeros((4, 2, 8, 8), np.float32)
    for direction in range(4):
        for sign_slot, sign_value in enumerate((-1.0, 1.0)):
            matrix = np.eye(4) + sign_value * gammas[direction]
            tables[direction, sign_slot, :4, :4] = matrix.real
            tables[direction, sign_slot, :4, 4:] = -matrix.imag
            tables[direction, sign_slot, 4:, :4] = matrix.imag
            tables[direction, sign_slot, 4:, 4:] = matrix.real
    return tables


def spin_apply(matrix, spinor):
    flattened = spinor.reshape((8,) + spinor.shape[2:])
    product = jnp.einsum(
        "pq,q...->p...", jnp.asarray(matrix, spinor.dtype), flattened, precision=HIGHEST
    )
    return product.reshape(spinor.shape)


def color_apply(link_field, spinor, dagger):
    formula = "batzw,sbltzw->saltzw" if dagger else "abtzw,sbltzw->saltzw"

    def contract(matrix_part, spinor_part):
        return jnp.einsum(formula, matrix_part, spinor_part, precision=HIGHEST)

    if dagger:
        real_part = contract(link_field[0], spinor[0]) + contract(link_field[1], spinor[1])
        imag_part = contract(link_field[0], spinor[1]) - contract(link_field[1], spinor[0])
    else:
        real_part = contract(link_field[0], spinor[0]) - contract(link_field[1], spinor[1])
        imag_part = contract(link_field[0], spinor[1]) + contract(link_field[1], spinor[0])
    return jnp.stack([real_part, imag_part])


def along_x(spinor, offset):
    lattice = spinor.reshape(spinor.shape[:-1] + (spinor.shape[-1] // NX, NX))
    return jnp.roll(lattice, -offset, axis=-1).reshape(spinor.shape)


def along_y(spinor, offset):
    lattice = spinor.reshape(spinor.shape[:-1] + (spinor.shape[-1] // NX, NX))
    return jnp.roll(lattice, -offset, axis=-2).reshape(spinor.shape)


def project_plus(spinor):
    return jnp.concatenate([spinor[:, :2], jnp.zeros_like(spinor[:, 2:])], axis=1)


def project_minus(spinor):
    return jnp.concatenate([jnp.zeros_like(spinor[:, :2]), spinor[:, 2:]], axis=1)


def complex_scale(coef_real, coef_imag, spinor):
    return jnp.stack(
        [
            coef_real * spinor[0] - coef_imag * spinor[1],
            coef_real * spinor[1] + coef_imag * spinor[0],
        ]
    )


def padded_rims(padded):
    return (
        padded[:, :, :, :, :1, 1:-1],
        padded[:, :, :, :, -1:, 1:-1],
        padded[:, :, :, :, 1:-1, :1],
        padded[:, :, :, :, 1:-1, -1:],
    )


def time_signs():
    position = lax.axis_index("ta")
    sign_low = jnp.where(position == 0, -1.0, 1.0).astype(jnp.float32)
    sign_high = jnp.where(position == lax.axis_size("ta") - 1, -1.0, 1.0).astype(jnp.float32)
    return (sign_low, sign_high)


def slice_masses():
    position = lax.axis_index("sa")
    mass_low = jnp.where(position == 0, -QUARK_MASS, 1.0).astype(jnp.float32)
    mass_high = jnp.where(position == lax.axis_size("sa") - 1, -QUARK_MASS, 1.0).astype(jnp.float32)
    return (mass_low, mass_high)


def slice_mix(spinor, low_rim, high_rim, mass_low, mass_high):
    lower_part = jnp.concatenate([mass_low * low_rim, spinor[:, :2, :, :-1]], axis=3)
    upper_part = jnp.concatenate([spinor[:, 2:, :, 1:], mass_high * high_rim], axis=3)
    return jnp.concatenate([lower_part, upper_part], axis=1)


def hopping(centre, rims, here_links, down_links, y_forward, y_backward):
    tables = gamma_tables()
    sign_low, sign_high = time_signs()
    low_time, high_time, low_depth, high_depth = rims
    forward = [
        along_x(centre, 1),
        y_forward,
        jnp.concatenate([centre[:, :, :, :, :, 1:], high_depth], axis=5),
        jnp.concatenate([centre[:, :, :, :, 1:], sign_high * high_time], axis=4),
    ]
    backward = [
        along_x(centre, -1),
        y_backward,
        jnp.concatenate([low_depth, centre[:, :, :, :, :, :-1]], axis=5),
        jnp.concatenate([sign_low * low_time, centre[:, :, :, :, :-1]], axis=4),
    ]
    total = (4.0 - WALL_HEIGHT) * centre
    for direction in range(4):
        going = color_apply(here_links[direction], forward[direction], False)
        coming = color_apply(down_links[direction], backward[direction], True)
        total = total - 0.5 * (
            spin_apply(tables[direction, 0], going) + spin_apply(tables[direction, 1], coming)
        )
    return total


def outer_operator(iterate, here_links, down_links):
    mass_low, mass_high = slice_masses()
    with_rims = padded_2(iterate, (("sa", 3),), 1)
    low_rim = with_rims[:, :2, :, :1]
    high_rim = with_rims[:, 2:, :, -1:]
    chiral_mix = slice_mix(iterate, low_rim, high_rim, mass_low, mass_high)
    blended = OUTER_SCALE * iterate + OUTER_SHIFT * chiral_mix
    rims = padded_rims(padded_2(blended, (("ta", 4), ("gz", 5)), 1))
    hopped = hopping(
        blended, rims, here_links, down_links, along_y(blended, 1), along_y(blended, -1)
    )
    return hopped + iterate - chiral_mix


def inner_rows_operator(remainder, here_links, down_links):
    chiral_mix = slice_mix(
        remainder, remainder[:, :2, :, -1:], remainder[:, 2:, :, :1], -QUARK_MASS, -QUARK_MASS
    )
    blended = INNER_SCALE * remainder + INNER_SHIFT * chiral_mix
    rims = padded_rims(padded_2(blended, (("ta", 4), ("gz", 5)), 1))
    row_rims = padded_2(blended, (("sa", 6),), NX)
    y_forward = row_rims[..., 2 * NX :]
    y_backward = row_rims[..., : -2 * NX]
    hopped = hopping(blended, rims, here_links, down_links, y_forward, y_backward)
    return hopped + remainder - chiral_mix


def minimal_residual(inner_source, operator, here_links, down_links):
    correction = jnp.zeros_like(inner_source)
    remainder = inner_source
    for iteration in range(ITERS):
        applied = operator(remainder, here_links, down_links)
        inner_real, inner_imag, weight = lax.psum(
            (
                jnp.sum(applied[0] * remainder[0] + applied[1] * remainder[1]),
                jnp.sum(applied[0] * remainder[1] - applied[1] * remainder[0]),
                jnp.sum(applied * applied),
            ),
            ("ta", "gz", "sa"),
        )
        weight = weight + EPSILON
        alpha_real = inner_real / weight
        alpha_imag = inner_imag / weight
        correction = correction + complex_scale(alpha_real, alpha_imag, remainder)
        remainder = remainder - complex_scale(alpha_real, alpha_imag, applied)
    return correction


def body(iterate, source, gauge_links):
    span = gauge_links.shape[-1]
    link_set = gauge_links.reshape((4, 2, 3, 3) + gauge_links.shape[2:])
    rim_time = shifted(gauge_links[3, :, -1:], "ta", 1)
    rim_depth = shifted(gauge_links[2, :, :, -1:], "gz", 1)
    down_time = jnp.concatenate([rim_time, gauge_links[3, :, :-1]], axis=1).reshape(
        link_set.shape[1:]
    )
    down_depth = jnp.concatenate([rim_depth, gauge_links[2, :, :, :-1]], axis=2).reshape(
        link_set.shape[1:]
    )
    here_links = [link_set[0], link_set[1], link_set[2], link_set[3]]
    down_links = [along_x(link_set[0], -1), along_y(link_set[1], -1), down_depth, down_time]
    residual = source - outer_operator(iterate, here_links, down_links)
    core_index = lax.axis_index("sa")
    local_slices = iterate.shape[3]
    global_slice = core_index * local_slices + jnp.arange(local_slices)
    first_mask = (global_slice == 0).astype(jnp.float32).reshape(-1, 1, 1, 1)
    last_mask = (global_slice == LS - 1).astype(jnp.float32).reshape(-1, 1, 1, 1)
    surface_piece = jnp.where(
        core_index == 0, project_minus(residual[:, :, :, :1]), project_plus(residual[:, :, :, -1:])
    )
    surface_slots = lax.all_to_all(surface_piece, "sa", split_axis=6, concat_axis=3, tiled=True)
    blank = jnp.zeros(surface_slots.shape[:3] + (LS8 - 2,) + surface_slots.shape[4:], jnp.float32)
    inner_source = jnp.concatenate(
        [surface_slots[:, :, :, :1], blank, surface_slots[:, :, :, 1:]], axis=3
    )
    row_width = span // lax.axis_size("sa")
    row_start = core_index * row_width
    here_rows = [
        lax.dynamic_slice_in_dim(link_field, row_start, row_width, 5) for link_field in here_links
    ]
    down_rows = [
        lax.dynamic_slice_in_dim(link_field, row_start, row_width, 5) for link_field in down_links
    ]
    correction = minimal_residual(inner_source, inner_rows_operator, here_rows, down_rows)
    returned = jnp.concatenate(
        [project_minus(correction[:, :, :, :1]), project_plus(correction[:, :, :, -1:])], axis=3
    )
    received = lax.all_to_all(returned, "sa", split_axis=3, concat_axis=6, tiled=True)
    corrected = iterate + received * (first_mask + last_mask)
    return (residual, corrected)


UPPER = [ri * 12 + sp * 3 + c for ri in range(2) for sp in (0, 1) for c in range(3)]
LOWER = [ri * 12 + sp * 3 + c for ri in range(2) for sp in (2, 3) for c in range(3)]
RE, IM = 0, 1
SPIN = (
    (((1, 1, IM), (-1, 1, RE)), ((1, 0, IM), (-1, 0, RE))),
    (((-1, 1, RE), (-1, 1, IM)), ((1, 0, RE), (1, 0, IM))),
    (((1, 0, IM), (-1, 0, RE)), ((-1, 1, IM), (1, 1, RE))),
    (((1, 0, RE), (1, 0, IM)), ((1, 1, RE), (1, 1, IM))),
)
ROWS = 24
FIELD = 576
LINKS = 72
SENT = 48
BLOCK = SENT + 72
MESSAGE = 2 * BLOCK
WHOLE = 6.0
LINK_SCALE = -0.5 * INNER_SCALE / WHOLE
MIXED = -1.8 * INNER_SCALE / WHOLE
MIXED_FIRST = 2.2 * INNER_SCALE / WHOLE - 1.0
CHI = INNER_SHIFT / INNER_SCALE
VMEM_LIMIT = 48 * 1024 * 1024


def number(part, spin, color):
    return part * 12 + spin * 3 + color


def half_spinor(get, direction, side):
    out = {}
    for spin in range(2):
        for part in range(2):
            sign, from_spin, from_part = SPIN[direction][spin][part]
            for color in range(3):
                up = get(number(part, spin, color))
                low = get(number(from_part, 2 + from_spin, color))
                out[spin, part, color] = up + low if sign * side > 0 else up - low
    return out


def link_times(link, half, dagger):
    out = {}
    for row in range(3):
        for spin in range(2):
            real, imag = (None, None)
            for col in range(3):
                a, b = (col, row) if dagger else (row, col)
                ur, ui = (link(RE, a, b), link(IM, a, b))
                hr, hi = (half[spin, RE, col], half[spin, IM, col])
                if dagger:
                    re_new, im_new = (ur * hr + ui * hi, ur * hi - ui * hr)
                else:
                    re_new, im_new = (ur * hr - ui * hi, ur * hi + ui * hr)
                real = re_new if real is None else real + re_new
                imag = im_new if imag is None else imag + im_new
            out[spin, RE, row] = real
            out[spin, IM, row] = imag
    return out


def link_times_3(link, half, dagger):
    mixed = {}
    for spin in range(2):
        for col in range(3):
            real, imag = (half[spin, RE, col], half[spin, IM, col])
            lead, less = (imag, real - imag) if dagger else (real, imag - real)
            mixed[spin, col] = (lead, less, real + imag)
    out = {}
    for row in range(3):
        for spin in range(2):
            sums = None
            for col in range(3):
                a, b = (col, row) if dagger else (row, col)
                lead, less, both = mixed[spin, col]
                products = (lead * link(2, a, b), less * link(RE, a, b), both * link(IM, a, b))
                sums = products if sums is None else tuple(p + q for p, q in zip(sums, products))
            first, second, third = sums
            out[spin, RE, row] = first + second if dagger else first - third
            out[spin, IM, row] = first - third if dagger else first + second
    return out


def add_hop(acc, half, direction, side):
    flip = 1 if direction == 3 else -1
    for spin in range(2):
        for part in range(2):
            sign, from_spin, from_part = SPIN[direction][spin][part]
            for color in range(3):
                up = number(part, spin, color)
                acc[up] = acc[up] + half[spin, part, color]
                low = number(part, 2 + spin, color)
                g = half[from_spin, from_part, color]
                acc[low] = acc[low] + g if sign * side * flip > 0 else acc[low] - g
    return acc


def roll(x, shift, axis):
    return pltpu.roll(x, shift % x.shape[axis], axis)


def lane():
    return lax.broadcasted_iota(jnp.int32, (8, 128), 1)


def sublane():
    return lax.broadcasted_iota(jnp.int32, (8, 128), 0)


def move_x(x, offset):
    at = lane()
    return jnp.take_along_axis(x, at - at % NX + (at + offset + NX) % NX, axis=1)


def move_y(x, offset):
    near = roll(x, -offset * NX, 1)
    far = jnp.take_along_axis(near, sublane() + 1 - 2 * (sublane() % 2), axis=0)
    edge = lane() // NX == (3 if offset > 0 else 0)
    return jnp.where(edge, far, near)


def move_t(x, offset):
    return roll(x, -offset * 2, 0)


def pairs(x):
    return jnp.concatenate([x, x, x, x], axis=0)


def scaled_links(gauge_ref, tile_ref, slot, direction, scale):
    for entry in range(18):
        row = (direction * 18 + entry) * 2
        tile_ref[slot * 18 + entry] = pairs(gauge_ref[row : row + 2, :]) * scale


def tree_sum(terms):
    while len(terms) > 1:
        terms = [a + b for a, b in zip(terms[::2], terms[1::2])] + terms[len(terms) // 2 * 2 :]
    return terms[0]


def tile_link(tile_ref, slot):
    return lambda part, a, b: tile_ref[slot * 18 + part * 9 + a * 3 + b]


def blend_rows(out_ref, here_ref, there_ref, mass_low, mass_high):
    row = lax.broadcasted_iota(jnp.int32, (ROWS, 128), 0)
    for comp in range(24):
        rows = slice(comp * ROWS, (comp + 1) * ROWS)
        v, other = (here_ref[rows, :], there_ref[rows, :])
        if comp in UPPER:
            chi = jnp.where(row < 2, roll(other, 2, 0) * mass_low, roll(v, 2, 0))
        else:
            chi = jnp.where(row >= ROWS - 2, roll(other, -2, 0) * mass_high, roll(v, -2, 0))
        out_ref[rows, :] = OUTER_SCALE * v + OUTER_SHIFT * chi


def stage_kernel(own_ref, src_ref, gauge_ref, own_out, src_out, gauge_out, sem):
    copies = []
    for i, (ref, out) in enumerate(((own_ref, own_out), (src_ref, src_out), (gauge_ref, gauge_out))):
        copies.append(pltpu.make_async_copy(ref, out, sem.at[i]))
        copies[-1].start()
    for copy in copies:
        copy.wait()


def send_kernel(own_ref, oth_ref, src_own_ref, src_oth_ref, gauge_ref, mt_ref, mz_ref, blk_ref, bl_ref, blo_ref, tile_ref):
    core = lax.axis_index("sa")
    last_time = lax.axis_index("ta") == lax.axis_size("ta") - 1
    time_scale = jnp.where(last_time, 0.5, -0.5).astype(jnp.float32)
    first = jnp.where(core == 0, -QUARK_MASS, 1.0).astype(jnp.float32)
    last = jnp.where(core == 0, 1.0, -QUARK_MASS).astype(jnp.float32)
    blend_rows(bl_ref, own_ref, oth_ref, first, last)
    blend_rows(blo_ref, oth_ref, own_ref, last, first)

    for h in range(2):
        for i in range(8):
            base = h * BLOCK + i * 6
            blk_ref[base : base + 6, :] = gauge_ref[pl.ds(i * 18 + h, 6, stride=2), :]

    def surfaces(bl0_ref, it0_ref, src0_ref, bl1_ref, it1_ref, src1_ref):
        for h in range(2):
            base = h * BLOCK + SENT
            blk_ref[base : base + 24, :] = bl0_ref[pl.ds(h, 24, stride=ROWS), :]
            blk_ref[base + 24 : base + 48, :] = bl1_ref[pl.ds(22 + h, 24, stride=ROWS), :]
            for part in range(2):
                start = (part * 12 + 6) * ROWS + h
                value = (
                    src0_ref[pl.ds(start, 6, stride=ROWS), :]
                    - it0_ref[pl.ds(start, 6, stride=ROWS), :]
                    + it0_ref[pl.ds(start + 2, 6, stride=ROWS), :]
                )
                blk_ref[base + 48 + part * 6 : base + 54 + part * 6, :] = value
                start = part * 12 * ROWS + 22 + h
                value = (
                    src1_ref[pl.ds(start, 6, stride=ROWS), :]
                    - it1_ref[pl.ds(start, 6, stride=ROWS), :]
                    + it1_ref[pl.ds(start - 2, 6, stride=ROWS), :]
                )
                blk_ref[base + 60 + part * 6 : base + 66 + part * 6, :] = value

    pl.when(core == 0)(lambda: surfaces(bl_ref, own_ref, src_own_ref, blo_ref, oth_ref, src_oth_ref))
    pl.when(core == 1)(lambda: surfaces(blo_ref, oth_ref, src_oth_ref, bl_ref, own_ref, src_own_ref))

    scaled_links(gauge_ref, tile_ref, 0, 2, -0.5)
    scaled_links(gauge_ref, tile_ref, 1, 3, time_scale)

    def store(ref, half, offset, g):
        for (spin, part, color), value in half.items():
            ref[pl.ds(offset + (part * 6 + spin * 3 + color) * ROWS + g * 8, 8), :] = value

    def getter(ref, g):
        return lambda comp: ref[pl.ds(comp * ROWS + g * 8, 8), :]

    for g in range(3):
        get = getter(bl_ref, g)
        store(mz_ref, half_spinor(get, 2, -1), 0, g)
        store(mz_ref, link_times(tile_link(tile_ref, 0), half_spinor(get, 2, 1), True), 288, g)

    def time_up(first_ref, second_ref):
        for which, ref in enumerate((first_ref, second_ref)):
            for g in range(3):
                half = half_spinor(getter(ref, g), 3, 1)
                store(mt_ref, link_times(tile_link(tile_ref, 1), half, True), which * 288, g)

    def time_down(first_ref, second_ref):
        for which, ref in enumerate((first_ref, second_ref)):
            for g in range(3):
                store(mt_ref, half_spinor(getter(ref, g), 3, -1), which * 288, g)

    pl.when(core == 0)(lambda: time_up(bl_ref, blo_ref))
    pl.when(core == 1)(lambda: time_down(blo_ref, bl_ref))


def halves(ref, rows, start):
    return {
        (spin, part, color): ref[rows(part * 6 + spin * 3 + color, start), :]
        for spin in range(2)
        for part in range(2)
        for color in range(3)
    }


def group_rows(g):
    return lambda comp, start=0: pl.ds(pl.multiple_of(start + comp * ROWS + g * 8, 8), 8)


def local_kernel(own_ref, bl_ref, src_ref, gauge_ref, acc_ref, tile_ref):
    scaled_links(gauge_ref, tile_ref, 0, 0, -0.5)
    scaled_links(gauge_ref, tile_ref, 1, 1, -0.5)

    def group(g, carry):
        rows = group_rows(g)
        get = lambda comp: bl_ref[rows(comp), :]
        acc = [0.2 * get(comp) + 4.0 * own_ref[rows(comp), :] - src_ref[rows(comp), :] for comp in range(24)]
        for direction, move in ((0, move_x), (1, move_y)):
            link = tile_link(tile_ref, direction)
            half = {k: move(h, 1) for k, h in half_spinor(get, direction, -1).items()}
            acc = add_hop(acc, link_times(link, half, False), direction, -1)
            half = link_times(link, half_spinor(get, direction, 1), True)
            acc = add_hop(acc, {k: move(h, -1) for k, h in half.items()}, direction, 1)
        for comp in range(24):
            acc_ref[rows(comp), :] = acc[comp]
        return carry

    lax.fori_loop(0, 3, group, 0)


def surface_kernel(own_ref, acc_in, gauge_ref, mz_ref, corr_ref, acc_ref, cor_ref, tile_ref):
    core = lax.axis_index("sa")
    scaled_links(gauge_ref, tile_ref, 0, 2, -0.5)

    def group(g, carry):
        rows = group_rows(g)
        acc = [acc_in[rows(comp), :] for comp in range(24)]
        acc = add_hop(acc, link_times(tile_link(tile_ref, 0), halves(mz_ref, rows, 0), False), 2, -1)
        acc = add_hop(acc, halves(mz_ref, rows, 288), 2, 1)
        for comp in range(24):
            acc_ref[rows(comp), :] = acc[comp]
        return carry

    lax.fori_loop(0, 3, group, 0)
    cor_ref[...] = own_ref[...]

    def add_surface(s, comps, first):
        for i, comp in enumerate(comps):
            at = slice(comp * ROWS + 2 * s, comp * ROWS + 2 * s + 2)
            cor_ref[at, :] = cor_ref[at, :] + corr_ref[first + i, 0:2, :]

    pl.when(core == 0)(lambda: add_surface(0, LOWER, 0))
    pl.when(core == 1)(lambda: add_surface(11, UPPER, 12))


def inner_kernel(own_ref, xd_ref, xa_ref, xa2_ref, xb_ref, xb2_ref, xc_ref, xc2_ref, out_ref, gather_ref, link_ref, base_ref, r_ref, a_ref, z_ref, sem):
    core = lax.axis_index("sa")
    pick = lambda zero, one: jnp.where(core == 0, zero, one)
    placed = (
        (own_ref, 0),
        (xd_ref, 4),
        (xa_ref, pick(3, 7)),
        (xa2_ref, pick(7, 3)),
        (xb_ref, pick(1, 5)),
        (xb2_ref, pick(5, 1)),
        (xc_ref, pick(2, 6)),
        (xc2_ref, pick(6, 2)),
    )
    copies = []
    for i, (ref, slot) in enumerate(placed):
        to = gather_ref.at[pl.ds(pl.multiple_of(slot * MESSAGE, 8), MESSAGE), :]
        copies.append(pltpu.make_async_copy(ref, to, sem.at[i]))
        copies[-1].start()
    zero = jnp.zeros((8, 128), jnp.float32)
    for s in range(1, 7):
        for comp in range(24):
            for dz in range(2):
                r_ref[s, comp, dz] = zero
    for copy in copies:
        copy.wait()

    time = lax.rem(lax.axis_index("ta") + sublane() // 2, 4)
    time_scale = jnp.where(time == 3, -LINK_SCALE, LINK_SCALE).astype(jnp.float32)

    def gathered(comp, dz):
        return gather_ref[pl.ds(dz * 8 * BLOCK + comp, 8, stride=BLOCK), :]

    for dz in range(2):
        for direction in range(4):
            scale = time_scale if direction == 3 else LINK_SCALE
            entry = lambda part, a, b: gathered(direction * 12 + part * 6 + a * 3 + b, dz)
            rows = {(part, a, b): entry(part, a, b) for part in range(2) for a in range(2) for b in range(3)}
            for b in range(3):
                p, q = ((b + 1) % 3, (b + 2) % 3)
                rows[RE, 2, b] = (
                    rows[RE, 0, p] * rows[RE, 1, q] - rows[IM, 0, p] * rows[IM, 1, q]
                    - rows[RE, 0, q] * rows[RE, 1, p] + rows[IM, 0, q] * rows[IM, 1, p]
                )
                rows[IM, 2, b] = (
                    rows[RE, 0, q] * rows[IM, 1, p] + rows[IM, 0, q] * rows[RE, 1, p]
                    - rows[RE, 0, p] * rows[IM, 1, q] - rows[IM, 0, p] * rows[RE, 1, q]
                )
            for a in range(3):
                for b in range(3):
                    real, imag = (rows[RE, a, b] * scale, rows[IM, a, b] * scale)
                    at = direction * 27 + a * 3 + b
                    link_ref[at, dz] = real
                    link_ref[at + 9, dz] = imag
                    link_ref[at + 18, dz] = real + imag
        for comp in range(24):
            r_ref[0, comp, dz] = gathered(SENT + comp, dz) * (1.0 / INNER_SCALE)
            r_ref[7, comp, dz] = gathered(SENT + 24 + comp, dz) * (1.0 / INNER_SCALE)
        for i in range(24):
            base_ref[i, dz] = gathered(SENT + 48 + i, dz)

    def hops(slot, dz, acc):
        def link(direction, at):
            return lambda part, a, b: link_ref[direction * 27 + part * 9 + a * 3 + b, at]

        here = lambda comp: z_ref[slot, comp, dz]
        there = lambda comp: z_ref[slot, comp, 1 - dz]
        for direction, move in ((0, move_x), (1, move_y), (3, move_t)):
            half = {k: move(h, 1) for k, h in half_spinor(here, direction, -1).items()}
            acc = add_hop(acc, link_times_3(link(direction, dz), half, False), direction, -1)
            half = link_times_3(link(direction, dz), half_spinor(here, direction, 1), True)
            acc = add_hop(acc, {k: move(h, -1) for k, h in half.items()}, direction, 1)
        half = half_spinor(there, 2, -1)
        acc = add_hop(acc, link_times_3(link(2, dz), half, False), 2, -1)
        half = link_times_3(link(2, 1 - dz), half_spinor(there, 2, 1), True)
        return add_hop(acc, half, 2, 1)

    for i in range(24):
        out_ref[i] = zero

    def stage(at, carry):
        first = at == 0
        number_f32 = lambda zero, other: jnp.where(first, zero, other).astype(jnp.float32)
        mixed_share = number_f32(MIXED_FIRST, MIXED)
        wall, shift = (number_f32(0.0, -QUARK_MASS * CHI), number_f32(0.0, CHI))
        count = jnp.where(first, 1, at)

        def pair(j, sums):
            low_end = jnp.where(j == 0, wall, shift)
            sides = (
                (j, jnp.where(j == 0, 7, j - 1), j + 1, low_end, shift),
                (7 - j, 6 - j, jnp.where(j == 0, 0, 8 - j), shift, low_end),
            )
            for slot, (s, before, after, low, high) in enumerate(sides):
                for dz in range(2):
                    for comp in range(24):
                        chi = r_ref[before, comp, dz] * low if comp in UPPER else r_ref[after, comp, dz] * high
                        z_ref[slot, comp, dz] = r_ref[s, comp, dz] + chi
            for slot, (s, before, after, low, high) in enumerate(sides):
                for dz in range(2):
                    acc = [r_ref[s, comp, dz] + mixed_share * z_ref[slot, comp, dz] for comp in range(24)]
                    acc = hops(slot, dz, acc)
                    terms = ([], [], [])
                    for i in range(12):
                        ar, ai = (acc[i], acc[i + 12])
                        rr, ri = (r_ref[s, i, dz], r_ref[s, i + 12, dz])
                        terms[0].append(ar * rr + ai * ri)
                        terms[1].append(ar * ri - ai * rr)
                        terms[2].append(ar * ar + ai * ai)
                    sums = tuple(total + tree_sum(part) for total, part in zip(sums, terms))
                    for comp in range(24):
                        a_ref[s, comp, dz] = acc[comp]
            return sums

        real, imag, weight = lax.fori_loop(0, count, pair, (zero, zero, zero))

        @pl.when(first)
        def _():
            for dz in range(2):
                for i in range(12):
                    r_ref[0, LOWER[i], dz] = base_ref[i, dz] - WHOLE * a_ref[0, LOWER[i], dz]
                    r_ref[0, UPPER[i], dz] = zero
                    r_ref[7, UPPER[i], dz] = base_ref[12 + i, dz] - WHOLE * a_ref[7, UPPER[i], dz]
                    r_ref[7, LOWER[i], dz] = zero

        @pl.when(at > 0)
        def _():
            total = lambda x: jnp.sum(x, axis=(0, 1), keepdims=True)
            scale = total(weight) + EPSILON / WHOLE**2
            alpha_real = jnp.broadcast_to(total(real) / scale, (8, 128))
            alpha_imag = jnp.broadcast_to(total(imag) / scale, (8, 128))
            for slot, (s, comps) in enumerate(((0, LOWER), (7, UPPER))):
                for i in range(6):
                    rr, ri = (r_ref[s, comps[i], 0], r_ref[s, comps[i + 6], 0])
                    to = slot * 12 + i
                    out_ref[to] = out_ref[to] + (alpha_real * rr - alpha_imag * ri) * (1.0 / WHOLE)
                    out_ref[to + 6] = out_ref[to + 6] + (alpha_real * ri + alpha_imag * rr) * (1.0 / WHOLE)

            def update(j, c):
                for s in (j, 7 - j):
                    for dz in range(2):
                        for i in range(12):
                            ar, ai = (a_ref[s, i, dz], a_ref[s, i + 12, dz])
                            r_ref[s, i, dz] = r_ref[s, i, dz] - (alpha_real * ar - alpha_imag * ai)
                            r_ref[s, i + 12, dz] = r_ref[s, i + 12, dz] - (alpha_real * ai + alpha_imag * ar)
                return c

            lax.fori_loop(0, jnp.where(at == ITERS, 0, count), update, 0)

        return carry

    lax.fori_loop(0, ITERS + 1, stage, 0)


def final_kernel(acc_ref, gauge_ref, ta_ref, tb_ref, res_ref, tile_ref):
    core = lax.axis_index("sa")
    last_time = lax.axis_index("ta") == lax.axis_size("ta") - 1
    scaled_links(gauge_ref, tile_ref, 0, 3, jnp.where(last_time, 0.5, -0.5).astype(jnp.float32))

    def finish(up_ref, down_ref, offset):
        def group(g, carry):
            rows = group_rows(g)
            acc = [acc_ref[rows(comp), :] for comp in range(24)]
            acc = add_hop(acc, link_times(tile_link(tile_ref, 0), halves(down_ref, rows, offset), False), 3, -1)
            acc = add_hop(acc, halves(up_ref, rows, offset), 3, 1)
            for comp in range(24):
                res_ref[rows(comp), :] = -acc[comp]
            return carry

        lax.fori_loop(0, 3, group, 0)

    pl.when(core == 0)(lambda: finish(ta_ref, tb_ref, 0))
    pl.when(core == 1)(lambda: finish(tb_ref, ta_ref, 288))


def cost(flops, moved):
    return pl.CostEstimate(flops=flops, bytes_accessed=moved, transcendentals=0)


def call(kernel, outs, scratch, in_specs, flops, moved, *args, limit=VMEM_LIMIT):
    shapes = [jax.ShapeDtypeStruct(s, jnp.float32) for s in outs]
    return pl.pallas_call(
        kernel,
        out_shape=shapes,
        in_specs=in_specs,
        out_specs=[pl.BlockSpec(memory_space=pltpu.VMEM)] * len(outs),
        scratch_shapes=scratch,
        cost_estimate=cost(flops, moved),
        compiler_params=pltpu.CompilerParams(vmem_limit_bytes=limit),
    )(*args)


def small_body(iterate, source, gauge_links):
    whole = iterate.shape
    own = iterate.reshape(FIELD, 128)
    src = source.reshape(FIELD, 128)
    gauge = gauge_links.reshape(2 * LINKS, 128)
    swap = [(0, 1), (1, 0)]
    oth = lax.ppermute(own, "sa", swap)
    src_oth = lax.ppermute(src, "sa", swap)
    vmem = pl.BlockSpec(memory_space=pltpu.VMEM)
    anywhere = pl.BlockSpec(memory_space=pl.ANY)
    f32 = jnp.float32
    own, src, gauge = call(
        stage_kernel,
        [(FIELD, 128), (FIELD, 128), (2 * LINKS, 128)],
        [pltpu.SemaphoreType.DMA((3,))],
        [pl.BlockSpec(memory_space=pltpu.HBM)] * 3,
        0,
        1_300_000,
        *(pltpu.with_memory_space_constraint(a, pltpu.HBM) for a in (own, src, gauge)),
    )
    mt, mz, blk, bl = call(
        send_kernel,
        [(FIELD, 128), (FIELD, 128), (MESSAGE, 128), (FIELD, 128)],
        [pltpu.VMEM((FIELD, 128), f32), pltpu.VMEM((36, 8, 128), f32)],
        [vmem] * 5,
        4_000_000,
        3_000_000,
        own, oth, src, src_oth, gauge,
    )

    def route(where):
        pairs_out = []
        for t in range(4):
            for z in range(2):
                for s in range(2):
                    dt, dz = where(s)
                    to = ((t + dt) % 4) * 4 + ((z + dz) % 2) * 2 + s
                    pairs_out.append((t * 4 + z * 2 + s, to))
        return pairs_out

    axes = ("ta", "gz", "sa")
    xd = lax.ppermute(blk, axes, route(lambda s: (0, 1)))
    xc = lax.ppermute(blk, axes, route(lambda s: (2, s)))
    xb = lax.ppermute(blk, axes, route(lambda s: (-1, s)))
    xa = lax.ppermute(blk, axes, route(lambda s: (1, s)))
    xd, mz = lax.optimization_barrier((xd, mz))
    tz = lax.ppermute(mz, axes, route(lambda s: (0, 1)))
    xa, xb, xc, mt = lax.optimization_barrier((xa, xb, xc, mt))
    xa2 = lax.ppermute(xa, "sa", swap)
    xb2 = lax.ppermute(xb, "sa", swap)
    xc2 = lax.ppermute(xc, "sa", swap)
    ta = lax.ppermute(mt, axes, route(lambda s: (1, 0) if s == 0 else (-1, 0)))
    acc = call(
        local_kernel,
        [(FIELD, 128)],
        [pltpu.VMEM((36, 8, 128), f32)],
        [vmem] * 4,
        4_000_000,
        3_000_000,
        own, bl, src, gauge,
    )[0]
    corr = call(
        inner_kernel,
        [(24, 8, 128)],
        [
            pltpu.VMEM((8 * MESSAGE, 128), f32),
            pltpu.VMEM((108, 2, 8, 128), f32),
            pltpu.VMEM((24, 2, 8, 128), f32),
            pltpu.VMEM((8, 24, 2, 8, 128), f32),
            pltpu.VMEM((8, 24, 2, 8, 128), f32),
            pltpu.VMEM((2, 24, 2, 8, 128), f32),
            pltpu.SemaphoreType.DMA((8,)),
        ],
        [anywhere] * 8,
        10_000_000_000,
        1_000_000_000,
        blk, xd, xa, xa2, xb, xb2, xc, xc2,
    )[0]
    ta, tz, corr = lax.optimization_barrier((ta, tz, corr))
    tb = lax.ppermute(ta, "sa", swap)
    acc, corrected = call(
        surface_kernel,
        [(FIELD, 128), (FIELD, 128)],
        [pltpu.VMEM((18, 8, 128), f32)],
        [vmem] * 5,
        3_000_000,
        3_000_000,
        own, acc, gauge, tz, corr,
    )
    residual = call(
        final_kernel,
        [(FIELD, 128)],
        [pltpu.VMEM((18, 8, 128), f32)],
        [vmem] * 4,
        2_000_000,
        2_000_000,
        acc, gauge, ta, tb,
    )[0]
    return (residual.reshape(whole), corrected.reshape(whole))


def solution(mesh):
    placed = (
        P("parts", None, None, "sa", "ta", "gz", None),
        P("parts", None, None, "sa", "ta", "gz", None),
        P("parts", None, "ta", "gz", None),
    )
    small = (mesh.shape["ta"], mesh.shape["gz"], mesh.shape["sa"]) == (4, 2, 2)

    def chosen(iterate, source, gauge_links):
        one_block = iterate.shape[3:] == (12, 1, 1, 256)
        return (small_body if small and one_block else body)(iterate, source, gauge_links)

    return jax.shard_map(
        chosen,
        mesh=mesh,
        in_specs=placed,
        out_specs=(
            P("parts", None, None, "sa", "ta", "gz", None),
            P("parts", None, None, "sa", "ta", "gz", None),
        ),
        check_vma=False,
    )
```

```python
import jax
import jax.numpy as jnp
import numpy as np
from jax import lax
from jax.experimental import pallas as pl
from jax.experimental.pallas import tpu as pltpu
from jax.sharding import PartitionSpec as P

NX = 32
LS = 24
LS8 = 8
ITERS = 3


WALL_HEIGHT = 1.8
OUTER_SCALE = 1.5
OUTER_SHIFT = 0.5
INNER_SCALE = 1.25
INNER_SHIFT = 0.25
QUARK_MASS = 0.05
EPSILON = 1e-06
HIGHEST = lax.Precision.HIGHEST


def padded_2(array, sides, width):
    for axis, dim in sides:
        count, length = (lax.axis_size(axis), array.shape[dim])
        up = [(i, (i + 1) % count) for i in range(count)]
        down = [(j, i) for i, j in up]
        last = lax.slice_in_dim(array, length - width, length, axis=dim)
        first = lax.slice_in_dim(array, 0, width, axis=dim)
        before = lax.ppermute(last, axis, up)
        after = lax.ppermute(first, axis, down)
        array = jnp.concatenate([before, array, after], axis=dim)
    return array


def shifted(block, axis, distance):
    devices = range(lax.axis_size(axis))
    route = [((i - distance) % len(devices), i) for i in devices]
    return lax.ppermute(block, axis, route)


def gamma_tables():
    pauli_list = [
        np.array([[0, 1], [1, 0]], complex),
        np.array([[0, -1j], [1j, 0]], complex),
        np.array([[1, 0], [0, -1]], complex),
    ]
    gammas = []
    for pauli_matrix in pauli_list:
        matrix = np.zeros((4, 4), complex)
        matrix[0:2, 2:4] = -1j * pauli_matrix
        matrix[2:4, 0:2] = 1j * pauli_matrix
        gammas.append(matrix)
    fourth = np.zeros((4, 4), complex)
    fourth[0:2, 2:4] = np.eye(2)
    fourth[2:4, 0:2] = np.eye(2)
    gammas.append(fourth)
    tables = np.zeros((4, 2, 8, 8), np.float32)
    for direction in range(4):
        for sign_slot, sign_value in enumerate((-1.0, 1.0)):
            matrix = np.eye(4) + sign_value * gammas[direction]
            tables[direction, sign_slot, :4, :4] = matrix.real
            tables[direction, sign_slot, :4, 4:] = -matrix.imag
            tables[direction, sign_slot, 4:, :4] = matrix.imag
            tables[direction, sign_slot, 4:, 4:] = matrix.real
    return tables


def spin_apply(matrix, spinor):
    flattened = spinor.reshape((8,) + spinor.shape[2:])
    product = jnp.einsum(
        "pq,q...->p...", jnp.asarray(matrix, spinor.dtype), flattened, precision=HIGHEST
    )
    return product.reshape(spinor.shape)


def color_apply(link_field, spinor, dagger):
    formula = "batzw,sbltzw->saltzw" if dagger else "abtzw,sbltzw->saltzw"

    def contract(matrix_part, spinor_part):
        return jnp.einsum(formula, matrix_part, spinor_part, precision=HIGHEST)

    if dagger:
        real_part = contract(link_field[0], spinor[0]) + contract(link_field[1], spinor[1])
        imag_part = contract(link_field[0], spinor[1]) - contract(link_field[1], spinor[0])
    else:
        real_part = contract(link_field[0], spinor[0]) - contract(link_field[1], spinor[1])
        imag_part = contract(link_field[0], spinor[1]) + contract(link_field[1], spinor[0])
    return jnp.stack([real_part, imag_part])


def along_x(spinor, offset):
    lattice = spinor.reshape(spinor.shape[:-1] + (spinor.shape[-1] // NX, NX))
    return jnp.roll(lattice, -offset, axis=-1).reshape(spinor.shape)


def along_y(spinor, offset):
    lattice = spinor.reshape(spinor.shape[:-1] + (spinor.shape[-1] // NX, NX))
    return jnp.roll(lattice, -offset, axis=-2).reshape(spinor.shape)


def project_plus(spinor):
    return jnp.concatenate([spinor[:, :2], jnp.zeros_like(spinor[:, 2:])], axis=1)


def project_minus(spinor):
    return jnp.concatenate([jnp.zeros_like(spinor[:, :2]), spinor[:, 2:]], axis=1)


def complex_scale(coef_real, coef_imag, spinor):
    return jnp.stack(
        [
            coef_real * spinor[0] - coef_imag * spinor[1],
            coef_real * spinor[1] + coef_imag * spinor[0],
        ]
    )


def padded_rims(padded):
    return (
        padded[:, :, :, :, :1, 1:-1],
        padded[:, :, :, :, -1:, 1:-1],
        padded[:, :, :, :, 1:-1, :1],
        padded[:, :, :, :, 1:-1, -1:],
    )


def time_signs():
    position = lax.axis_index("ta")
    sign_low = jnp.where(position == 0, -1.0, 1.0).astype(jnp.float32)
    sign_high = jnp.where(position == lax.axis_size("ta") - 1, -1.0, 1.0).astype(jnp.float32)
    return (sign_low, sign_high)


def slice_masses():
    position = lax.axis_index("sa")
    mass_low = jnp.where(position == 0, -QUARK_MASS, 1.0).astype(jnp.float32)
    mass_high = jnp.where(position == lax.axis_size("sa") - 1, -QUARK_MASS, 1.0).astype(jnp.float32)
    return (mass_low, mass_high)


def slice_mix(spinor, low_rim, high_rim, mass_low, mass_high):
    lower_part = jnp.concatenate([mass_low * low_rim, spinor[:, :2, :, :-1]], axis=3)
    upper_part = jnp.concatenate([spinor[:, 2:, :, 1:], mass_high * high_rim], axis=3)
    return jnp.concatenate([lower_part, upper_part], axis=1)


def hopping(centre, rims, here_links, down_links, y_forward, y_backward):
    tables = gamma_tables()
    sign_low, sign_high = time_signs()
    low_time, high_time, low_depth, high_depth = rims
    forward = [
        along_x(centre, 1),
        y_forward,
        jnp.concatenate([centre[:, :, :, :, :, 1:], high_depth], axis=5),
        jnp.concatenate([centre[:, :, :, :, 1:], sign_high * high_time], axis=4),
    ]
    backward = [
        along_x(centre, -1),
        y_backward,
        jnp.concatenate([low_depth, centre[:, :, :, :, :, :-1]], axis=5),
        jnp.concatenate([sign_low * low_time, centre[:, :, :, :, :-1]], axis=4),
    ]
    total = (4.0 - WALL_HEIGHT) * centre
    for direction in range(4):
        going = color_apply(here_links[direction], forward[direction], False)
        coming = color_apply(down_links[direction], backward[direction], True)
        total = total - 0.5 * (
            spin_apply(tables[direction, 0], going) + spin_apply(tables[direction, 1], coming)
        )
    return total


def outer_operator(iterate, here_links, down_links):
    mass_low, mass_high = slice_masses()
    with_rims = padded_2(iterate, (("sa", 3),), 1)
    low_rim = with_rims[:, :2, :, :1]
    high_rim = with_rims[:, 2:, :, -1:]
    chiral_mix = slice_mix(iterate, low_rim, high_rim, mass_low, mass_high)
    blended = OUTER_SCALE * iterate + OUTER_SHIFT * chiral_mix
    rims = padded_rims(padded_2(blended, (("ta", 4), ("gz", 5)), 1))
    hopped = hopping(
        blended, rims, here_links, down_links, along_y(blended, 1), along_y(blended, -1)
    )
    return hopped + iterate - chiral_mix


def inner_rows_operator(remainder, here_links, down_links):
    chiral_mix = slice_mix(
        remainder, remainder[:, :2, :, -1:], remainder[:, 2:, :, :1], -QUARK_MASS, -QUARK_MASS
    )
    blended = INNER_SCALE * remainder + INNER_SHIFT * chiral_mix
    rims = padded_rims(padded_2(blended, (("ta", 4), ("gz", 5)), 1))
    row_rims = padded_2(blended, (("sa", 6),), NX)
    y_forward = row_rims[..., 2 * NX :]
    y_backward = row_rims[..., : -2 * NX]
    hopped = hopping(blended, rims, here_links, down_links, y_forward, y_backward)
    return hopped + remainder - chiral_mix


def minimal_residual(inner_source, operator, here_links, down_links):
    correction = jnp.zeros_like(inner_source)
    remainder = inner_source
    for iteration in range(ITERS):
        applied = operator(remainder, here_links, down_links)
        inner_real, inner_imag, weight = lax.psum(
            (
                jnp.sum(applied[0] * remainder[0] + applied[1] * remainder[1]),
                jnp.sum(applied[0] * remainder[1] - applied[1] * remainder[0]),
                jnp.sum(applied * applied),
            ),
            ("ta", "gz", "sa"),
        )
        weight = weight + EPSILON
        alpha_real = inner_real / weight
        alpha_imag = inner_imag / weight
        correction = correction + complex_scale(alpha_real, alpha_imag, remainder)
        remainder = remainder - complex_scale(alpha_real, alpha_imag, applied)
    return correction


def body(iterate, source, gauge_links):
    span = gauge_links.shape[-1]
    link_set = gauge_links.reshape((4, 2, 3, 3) + gauge_links.shape[2:])
    rim_time = shifted(gauge_links[3, :, -1:], "ta", 1)
    rim_depth = shifted(gauge_links[2, :, :, -1:], "gz", 1)
    down_time = jnp.concatenate([rim_time, gauge_links[3, :, :-1]], axis=1).reshape(
        link_set.shape[1:]
    )
    down_depth = jnp.concatenate([rim_depth, gauge_links[2, :, :, :-1]], axis=2).reshape(
        link_set.shape[1:]
    )
    here_links = [link_set[0], link_set[1], link_set[2], link_set[3]]
    down_links = [along_x(link_set[0], -1), along_y(link_set[1], -1), down_depth, down_time]
    residual = source - outer_operator(iterate, here_links, down_links)
    core_index = lax.axis_index("sa")
    local_slices = iterate.shape[3]
    global_slice = core_index * local_slices + jnp.arange(local_slices)
    first_mask = (global_slice == 0).astype(jnp.float32).reshape(-1, 1, 1, 1)
    last_mask = (global_slice == LS - 1).astype(jnp.float32).reshape(-1, 1, 1, 1)
    surface_piece = jnp.where(
        core_index == 0, project_minus(residual[:, :, :, :1]), project_plus(residual[:, :, :, -1:])
    )
    surface_slots = lax.all_to_all(surface_piece, "sa", split_axis=6, concat_axis=3, tiled=True)
    blank = jnp.zeros(surface_slots.shape[:3] + (LS8 - 2,) + surface_slots.shape[4:], jnp.float32)
    inner_source = jnp.concatenate(
        [surface_slots[:, :, :, :1], blank, surface_slots[:, :, :, 1:]], axis=3
    )
    row_width = span // lax.axis_size("sa")
    row_start = core_index * row_width
    here_rows = [
        lax.dynamic_slice_in_dim(link_field, row_start, row_width, 5) for link_field in here_links
    ]
    down_rows = [
        lax.dynamic_slice_in_dim(link_field, row_start, row_width, 5) for link_field in down_links
    ]
    correction = minimal_residual(inner_source, inner_rows_operator, here_rows, down_rows)
    returned = jnp.concatenate(
        [project_minus(correction[:, :, :, :1]), project_plus(correction[:, :, :, -1:])], axis=3
    )
    received = lax.all_to_all(returned, "sa", split_axis=3, concat_axis=6, tiled=True)
    corrected = iterate + received * (first_mask + last_mask)
    return (residual, corrected)


UPPER = [ri * 12 + sp * 3 + c for ri in range(2) for sp in (0, 1) for c in range(3)]
LOWER = [ri * 12 + sp * 3 + c for ri in range(2) for sp in (2, 3) for c in range(3)]
RE, IM = 0, 1
SPIN = (
    (((1, 1, IM), (-1, 1, RE)), ((1, 0, IM), (-1, 0, RE))),
    (((-1, 1, RE), (-1, 1, IM)), ((1, 0, RE), (1, 0, IM))),
    (((1, 0, IM), (-1, 0, RE)), ((-1, 1, IM), (1, 1, RE))),
    (((1, 0, RE), (1, 0, IM)), ((1, 1, RE), (1, 1, IM))),
)
ROWS = 24
FIELD = 576
LINKS = 72
SENT = 48
BLOCK = SENT + 72
MESSAGE = 2 * BLOCK
WHOLE = 6.0
LINK_SCALE = -0.5 * INNER_SCALE / WHOLE
MIXED = -1.8 * INNER_SCALE / WHOLE
MIXED_FIRST = 2.2 * INNER_SCALE / WHOLE - 1.0
CHI = INNER_SHIFT / INNER_SCALE
VMEM_LIMIT = 48 * 1024 * 1024


def number(part, spin, color):
    return part * 12 + spin * 3 + color


def half_spinor(get, direction, side):
    out = {}
    for spin in range(2):
        for part in range(2):
            sign, from_spin, from_part = SPIN[direction][spin][part]
            for color in range(3):
                up = get(number(part, spin, color))
                low = get(number(from_part, 2 + from_spin, color))
                out[spin, part, color] = up + low if sign * side > 0 else up - low
    return out


def link_times(link, half, dagger):
    out = {}
    for row in range(3):
        for spin in range(2):
            real, imag = (None, None)
            for col in range(3):
                a, b = (col, row) if dagger else (row, col)
                ur, ui = (link(RE, a, b), link(IM, a, b))
                hr, hi = (half[spin, RE, col], half[spin, IM, col])
                if dagger:
                    re_new, im_new = (ur * hr + ui * hi, ur * hi - ui * hr)
                else:
                    re_new, im_new = (ur * hr - ui * hi, ur * hi + ui * hr)
                real = re_new if real is None else real + re_new
                imag = im_new if imag is None else imag + im_new
            out[spin, RE, row] = real
            out[spin, IM, row] = imag
    return out


def link_times_3(link, half, dagger):
    mixed = {}
    for spin in range(2):
        for col in range(3):
            real, imag = (half[spin, RE, col], half[spin, IM, col])
            lead, less = (imag, real - imag) if dagger else (real, imag - real)
            mixed[spin, col] = (lead, less, real + imag)
    out = {}
    for row in range(3):
        for spin in range(2):
            sums = None
            for col in range(3):
                a, b = (col, row) if dagger else (row, col)
                lead, less, both = mixed[spin, col]
                products = (lead * link(2, a, b), less * link(RE, a, b), both * link(IM, a, b))
                sums = products if sums is None else tuple(p + q for p, q in zip(sums, products))
            first, second, third = sums
            out[spin, RE, row] = first + second if dagger else first - third
            out[spin, IM, row] = first - third if dagger else first + second
    return out


def add_hop(acc, half, direction, side):
    flip = 1 if direction == 3 else -1
    for spin in range(2):
        for part in range(2):
            sign, from_spin, from_part = SPIN[direction][spin][part]
            for color in range(3):
                up = number(part, spin, color)
                acc[up] = acc[up] + half[spin, part, color]
                low = number(part, 2 + spin, color)
                g = half[from_spin, from_part, color]
                acc[low] = acc[low] + g if sign * side * flip > 0 else acc[low] - g
    return acc


def roll(x, shift, axis):
    return pltpu.roll(x, shift % x.shape[axis], axis)


def lane():
    return lax.broadcasted_iota(jnp.int32, (8, 128), 1)


def sublane():
    return lax.broadcasted_iota(jnp.int32, (8, 128), 0)


def move_x(x, offset):
    at = lane()
    return jnp.take_along_axis(x, at - at % NX + (at + offset + NX) % NX, axis=1)


def move_y(x, offset):
    near = roll(x, -offset * NX, 1)
    far = jnp.take_along_axis(near, sublane() + 1 - 2 * (sublane() % 2), axis=0)
    edge = lane() // NX == (3 if offset > 0 else 0)
    return jnp.where(edge, far, near)


def move_t(x, offset):
    return roll(x, -offset * 2, 0)


def pairs(x):
    return jnp.concatenate([x, x, x, x], axis=0)


def scaled_links(gauge_ref, tile_ref, slot, direction, scale):
    for entry in range(18):
        row = (direction * 18 + entry) * 2
        tile_ref[slot * 18 + entry] = pairs(gauge_ref[row : row + 2, :]) * scale


def tree_sum(terms):
    while len(terms) > 1:
        terms = [a + b for a, b in zip(terms[::2], terms[1::2])] + terms[len(terms) // 2 * 2 :]
    return terms[0]


def tile_link(tile_ref, slot):
    return lambda part, a, b: tile_ref[slot * 18 + part * 9 + a * 3 + b]


def blend_rows(out_ref, here_ref, there_ref, mass_low, mass_high):
    row = lax.broadcasted_iota(jnp.int32, (ROWS, 128), 0)
    for comp in range(24):
        rows = slice(comp * ROWS, (comp + 1) * ROWS)
        v, other = (here_ref[rows, :], there_ref[rows, :])
        if comp in UPPER:
            chi = jnp.where(row < 2, roll(other, 2, 0) * mass_low, roll(v, 2, 0))
        else:
            chi = jnp.where(row >= ROWS - 2, roll(other, -2, 0) * mass_high, roll(v, -2, 0))
        out_ref[rows, :] = OUTER_SCALE * v + OUTER_SHIFT * chi


def stage_kernel(own_ref, src_ref, gauge_ref, own_out, src_out, gauge_out, sem):
    copies = []
    for i, (ref, out) in enumerate(((own_ref, own_out), (src_ref, src_out), (gauge_ref, gauge_out))):
        copies.append(pltpu.make_async_copy(ref, out, sem.at[i]))
        copies[-1].start()
    for copy in copies:
        copy.wait()


def send_kernel(own_ref, oth_ref, src_own_ref, src_oth_ref, gauge_ref, up_ref, down_ref, mz_ref, blk_ref, bl_ref, blo_ref, tile_ref):
    core = lax.axis_index("sa")
    last_time = lax.axis_index("ta") == lax.axis_size("ta") - 1
    time_scale = jnp.where(last_time, 0.5, -0.5).astype(jnp.float32)
    first = jnp.where(core == 0, -QUARK_MASS, 1.0).astype(jnp.float32)
    last = jnp.where(core == 0, 1.0, -QUARK_MASS).astype(jnp.float32)
    blend_rows(bl_ref, own_ref, oth_ref, first, last)
    blend_rows(blo_ref, oth_ref, own_ref, last, first)

    for h in range(2):
        for i in range(8):
            base = h * BLOCK + i * 6
            blk_ref[base : base + 6, :] = gauge_ref[pl.ds(i * 18 + h, 6, stride=2), :]

    def surfaces(bl0_ref, it0_ref, src0_ref, bl1_ref, it1_ref, src1_ref):
        for h in range(2):
            base = h * BLOCK + SENT
            blk_ref[base : base + 24, :] = bl0_ref[pl.ds(h, 24, stride=ROWS), :]
            blk_ref[base + 24 : base + 48, :] = bl1_ref[pl.ds(22 + h, 24, stride=ROWS), :]
            for part in range(2):
                start = (part * 12 + 6) * ROWS + h
                value = (
                    src0_ref[pl.ds(start, 6, stride=ROWS), :]
                    - it0_ref[pl.ds(start, 6, stride=ROWS), :]
                    + it0_ref[pl.ds(start + 2, 6, stride=ROWS), :]
                )
                blk_ref[base + 48 + part * 6 : base + 54 + part * 6, :] = value
                start = part * 12 * ROWS + 22 + h
                value = (
                    src1_ref[pl.ds(start, 6, stride=ROWS), :]
                    - it1_ref[pl.ds(start, 6, stride=ROWS), :]
                    + it1_ref[pl.ds(start - 2, 6, stride=ROWS), :]
                )
                blk_ref[base + 60 + part * 6 : base + 66 + part * 6, :] = value

    pl.when(core == 0)(lambda: surfaces(bl_ref, own_ref, src_own_ref, blo_ref, oth_ref, src_oth_ref))
    pl.when(core == 1)(lambda: surfaces(blo_ref, oth_ref, src_oth_ref, bl_ref, own_ref, src_own_ref))

    scaled_links(gauge_ref, tile_ref, 0, 2, -0.5)
    scaled_links(gauge_ref, tile_ref, 1, 3, time_scale)

    def store(ref, half, offset, g):
        for (spin, part, color), value in half.items():
            ref[pl.ds(offset + (part * 6 + spin * 3 + color) * ROWS + g * 8, 8), :] = value

    def getter(ref, g):
        return lambda comp: ref[pl.ds(comp * ROWS + g * 8, 8), :]

    for g in range(3):
        get = getter(bl_ref, g)
        store(mz_ref, half_spinor(get, 2, -1), 0, g)
        store(mz_ref, link_times(tile_link(tile_ref, 0), half_spinor(get, 2, 1), True), 288, g)
        store(up_ref, link_times(tile_link(tile_ref, 1), half_spinor(get, 3, 1), True), 0, g)
        store(down_ref, half_spinor(get, 3, -1), 0, g)


def halves(ref, rows, start):
    return {
        (spin, part, color): ref[rows(part * 6 + spin * 3 + color, start), :]
        for spin in range(2)
        for part in range(2)
        for color in range(3)
    }


def group_rows(g):
    return lambda comp, start=0: pl.ds(pl.multiple_of(start + comp * ROWS + g * 8, 8), 8)


def local_kernel(own_ref, bl_ref, src_ref, gauge_ref, acc_ref, tile_ref):
    scaled_links(gauge_ref, tile_ref, 0, 0, -0.5)
    scaled_links(gauge_ref, tile_ref, 1, 1, -0.5)

    def group(g, carry):
        rows = group_rows(g)
        get = lambda comp: bl_ref[rows(comp), :]
        acc = [0.2 * get(comp) + 4.0 * own_ref[rows(comp), :] - src_ref[rows(comp), :] for comp in range(24)]
        for direction, move in ((0, move_x), (1, move_y)):
            link = tile_link(tile_ref, direction)
            half = {k: move(h, 1) for k, h in half_spinor(get, direction, -1).items()}
            acc = add_hop(acc, link_times(link, half, False), direction, -1)
            half = link_times(link, half_spinor(get, direction, 1), True)
            acc = add_hop(acc, {k: move(h, -1) for k, h in half.items()}, direction, 1)
        for comp in range(24):
            acc_ref[rows(comp), :] = acc[comp]
        return carry

    lax.fori_loop(0, 3, group, 0)


def inner_kernel(own_ref, xd_ref, xa_ref, xa2_ref, xb_ref, xb2_ref, xc_ref, xc2_ref, out_ref, gather_ref, link_ref, base_ref, r_ref, a_ref, z_ref, sem):
    core = lax.axis_index("sa")
    pick = lambda zero, one: jnp.where(core == 0, zero, one)
    placed = (
        (own_ref, 0),
        (xd_ref, 4),
        (xa_ref, pick(3, 7)),
        (xa2_ref, pick(7, 3)),
        (xb_ref, pick(1, 5)),
        (xb2_ref, pick(5, 1)),
        (xc_ref, pick(2, 6)),
        (xc2_ref, pick(6, 2)),
    )
    copies = []
    for i, (ref, slot) in enumerate(placed):
        to = gather_ref.at[pl.ds(pl.multiple_of(slot * MESSAGE, 8), MESSAGE), :]
        copies.append(pltpu.make_async_copy(ref, to, sem.at[i]))
        copies[-1].start()
    zero = jnp.zeros((8, 128), jnp.float32)
    for s in range(1, 7):
        for comp in range(24):
            for dz in range(2):
                r_ref[s, comp, dz] = zero
    for copy in copies:
        copy.wait()

    time = lax.rem(lax.axis_index("ta") + sublane() // 2, 4)
    time_scale = jnp.where(time == 3, -LINK_SCALE, LINK_SCALE).astype(jnp.float32)

    def gathered(comp, dz):
        return gather_ref[pl.ds(dz * 8 * BLOCK + comp, 8, stride=BLOCK), :]

    for dz in range(2):
        for direction in range(4):
            scale = time_scale if direction == 3 else LINK_SCALE
            entry = lambda part, a, b: gathered(direction * 12 + part * 6 + a * 3 + b, dz)
            rows = {(part, a, b): entry(part, a, b) for part in range(2) for a in range(2) for b in range(3)}
            for b in range(3):
                p, q = ((b + 1) % 3, (b + 2) % 3)
                rows[RE, 2, b] = (
                    rows[RE, 0, p] * rows[RE, 1, q] - rows[IM, 0, p] * rows[IM, 1, q]
                    - rows[RE, 0, q] * rows[RE, 1, p] + rows[IM, 0, q] * rows[IM, 1, p]
                )
                rows[IM, 2, b] = (
                    rows[RE, 0, q] * rows[IM, 1, p] + rows[IM, 0, q] * rows[RE, 1, p]
                    - rows[RE, 0, p] * rows[IM, 1, q] - rows[IM, 0, p] * rows[RE, 1, q]
                )
            for a in range(3):
                for b in range(3):
                    real, imag = (rows[RE, a, b] * scale, rows[IM, a, b] * scale)
                    at = direction * 27 + a * 3 + b
                    link_ref[at, dz] = real
                    link_ref[at + 9, dz] = imag
                    link_ref[at + 18, dz] = real + imag
        for comp in range(24):
            r_ref[0, comp, dz] = gathered(SENT + comp, dz) * (1.0 / INNER_SCALE)
            r_ref[7, comp, dz] = gathered(SENT + 24 + comp, dz) * (1.0 / INNER_SCALE)
        for i in range(24):
            base_ref[i, dz] = gathered(SENT + 48 + i, dz)

    def hops(slot, dz, acc):
        def link(direction, at):
            return lambda part, a, b: link_ref[direction * 27 + part * 9 + a * 3 + b, at]

        here = lambda comp: z_ref[slot, comp, dz]
        there = lambda comp: z_ref[slot, comp, 1 - dz]
        for direction, move in ((0, move_x), (1, move_y), (3, move_t)):
            half = {k: move(h, 1) for k, h in half_spinor(here, direction, -1).items()}
            acc = add_hop(acc, link_times_3(link(direction, dz), half, False), direction, -1)
            half = link_times_3(link(direction, dz), half_spinor(here, direction, 1), True)
            acc = add_hop(acc, {k: move(h, -1) for k, h in half.items()}, direction, 1)
        half = half_spinor(there, 2, -1)
        acc = add_hop(acc, link_times_3(link(2, dz), half, False), 2, -1)
        half = link_times_3(link(2, 1 - dz), half_spinor(there, 2, 1), True)
        return add_hop(acc, half, 2, 1)

    for i in range(24):
        out_ref[i] = zero

    def stage(at, carry):
        first = at == 0
        number_f32 = lambda zero, other: jnp.where(first, zero, other).astype(jnp.float32)
        mixed_share = number_f32(MIXED_FIRST, MIXED)
        wall, shift = (number_f32(0.0, -QUARK_MASS * CHI), number_f32(0.0, CHI))
        count = jnp.where(first, 1, at)

        def pair(j, sums):
            low_end = jnp.where(j == 0, wall, shift)
            sides = (
                (j, jnp.where(j == 0, 7, j - 1), j + 1, low_end, shift),
                (7 - j, 6 - j, jnp.where(j == 0, 0, 8 - j), shift, low_end),
            )
            for slot, (s, before, after, low, high) in enumerate(sides):
                for dz in range(2):
                    for comp in range(24):
                        chi = r_ref[before, comp, dz] * low if comp in UPPER else r_ref[after, comp, dz] * high
                        z_ref[slot, comp, dz] = r_ref[s, comp, dz] + chi
            for slot, (s, before, after, low, high) in enumerate(sides):
                for dz in range(2):
                    acc = [r_ref[s, comp, dz] + mixed_share * z_ref[slot, comp, dz] for comp in range(24)]
                    acc = hops(slot, dz, acc)
                    terms = ([], [], [])
                    for i in range(12):
                        ar, ai = (acc[i], acc[i + 12])
                        rr, ri = (r_ref[s, i, dz], r_ref[s, i + 12, dz])
                        terms[0].append(ar * rr + ai * ri)
                        terms[1].append(ar * ri - ai * rr)
                        terms[2].append(ar * ar + ai * ai)
                    sums = tuple(total + tree_sum(part) for total, part in zip(sums, terms))
                    for comp in range(24):
                        a_ref[s, comp, dz] = acc[comp]
            return sums

        real, imag, weight = lax.fori_loop(0, count, pair, (zero, zero, zero))

        @pl.when(first)
        def _():
            for dz in range(2):
                for i in range(12):
                    r_ref[0, LOWER[i], dz] = base_ref[i, dz] - WHOLE * a_ref[0, LOWER[i], dz]
                    r_ref[0, UPPER[i], dz] = zero
                    r_ref[7, UPPER[i], dz] = base_ref[12 + i, dz] - WHOLE * a_ref[7, UPPER[i], dz]
                    r_ref[7, LOWER[i], dz] = zero

        @pl.when(at > 0)
        def _():
            total = lambda x: jnp.sum(x, axis=(0, 1), keepdims=True)
            scale = total(weight) + EPSILON / WHOLE**2
            alpha_real = jnp.broadcast_to(total(real) / scale, (8, 128))
            alpha_imag = jnp.broadcast_to(total(imag) / scale, (8, 128))
            for slot, (s, comps) in enumerate(((0, LOWER), (7, UPPER))):
                for i in range(6):
                    rr, ri = (r_ref[s, comps[i], 0], r_ref[s, comps[i + 6], 0])
                    to = slot * 12 + i
                    out_ref[to] = out_ref[to] + (alpha_real * rr - alpha_imag * ri) * (1.0 / WHOLE)
                    out_ref[to + 6] = out_ref[to + 6] + (alpha_real * ri + alpha_imag * rr) * (1.0 / WHOLE)

            def update(j, c):
                for s in (j, 7 - j):
                    for dz in range(2):
                        for i in range(12):
                            ar, ai = (a_ref[s, i, dz], a_ref[s, i + 12, dz])
                            r_ref[s, i, dz] = r_ref[s, i, dz] - (alpha_real * ar - alpha_imag * ai)
                            r_ref[s, i + 12, dz] = r_ref[s, i + 12, dz] - (alpha_real * ai + alpha_imag * ar)
                return c

            lax.fori_loop(0, jnp.where(at == ITERS, 0, count), update, 0)

        return carry

    lax.fori_loop(0, ITERS + 1, stage, 0)


def final_kernel(own_ref, acc_ref, gauge_ref, up_ref, down_ref, mz_ref, corr_ref, res_ref, cor_ref, tile_ref):
    core = lax.axis_index("sa")
    last_time = lax.axis_index("ta") == lax.axis_size("ta") - 1
    scaled_links(gauge_ref, tile_ref, 0, 2, -0.5)
    scaled_links(gauge_ref, tile_ref, 1, 3, jnp.where(last_time, 0.5, -0.5).astype(jnp.float32))

    def group(g, carry):
        rows = group_rows(g)
        acc = [acc_ref[rows(comp), :] for comp in range(24)]
        acc = add_hop(acc, link_times(tile_link(tile_ref, 0), halves(mz_ref, rows, 0), False), 2, -1)
        acc = add_hop(acc, halves(mz_ref, rows, 288), 2, 1)
        acc = add_hop(acc, link_times(tile_link(tile_ref, 1), halves(down_ref, rows, 0), False), 3, -1)
        acc = add_hop(acc, halves(up_ref, rows, 0), 3, 1)
        for comp in range(24):
            res_ref[rows(comp), :] = -acc[comp]
        return carry

    lax.fori_loop(0, 3, group, 0)
    cor_ref[...] = own_ref[...]

    def add_surface(s, comps, first):
        for i, comp in enumerate(comps):
            at = slice(comp * ROWS + 2 * s, comp * ROWS + 2 * s + 2)
            cor_ref[at, :] = cor_ref[at, :] + corr_ref[first + i, 0:2, :]

    pl.when(core == 0)(lambda: add_surface(0, LOWER, 0))
    pl.when(core == 1)(lambda: add_surface(11, UPPER, 12))


def cost(flops, moved):
    return pl.CostEstimate(flops=flops, bytes_accessed=moved, transcendentals=0)


def call(kernel, outs, scratch, in_specs, flops, moved, *args, limit=VMEM_LIMIT):
    shapes = [jax.ShapeDtypeStruct(s, jnp.float32) for s in outs]
    return pl.pallas_call(
        kernel,
        out_shape=shapes,
        in_specs=in_specs,
        out_specs=[pl.BlockSpec(memory_space=pltpu.VMEM)] * len(outs),
        scratch_shapes=scratch,
        cost_estimate=cost(flops, moved),
        compiler_params=pltpu.CompilerParams(vmem_limit_bytes=limit),
    )(*args)


def small_body(iterate, source, gauge_links):
    whole = iterate.shape
    own = iterate.reshape(FIELD, 128)
    src = source.reshape(FIELD, 128)
    gauge = gauge_links.reshape(2 * LINKS, 128)
    swap = [(0, 1), (1, 0)]
    oth = lax.ppermute(own, "sa", swap)
    src_oth = lax.ppermute(src, "sa", swap)
    vmem = pl.BlockSpec(memory_space=pltpu.VMEM)
    anywhere = pl.BlockSpec(memory_space=pl.ANY)
    f32 = jnp.float32
    own, src, gauge = call(
        stage_kernel,
        [(FIELD, 128), (FIELD, 128), (2 * LINKS, 128)],
        [pltpu.SemaphoreType.DMA((3,))],
        [pl.BlockSpec(memory_space=pltpu.HBM)] * 3,
        0,
        1_300_000,
        *(pltpu.with_memory_space_constraint(a, pltpu.HBM) for a in (own, src, gauge)),
    )
    up, down, mz, blk, bl = call(
        send_kernel,
        [(FIELD // 2, 128), (FIELD // 2, 128), (FIELD, 128), (MESSAGE, 128), (FIELD, 128)],
        [pltpu.VMEM((FIELD, 128), f32), pltpu.VMEM((36, 8, 128), f32)],
        [vmem] * 5,
        4_000_000,
        3_000_000,
        own, oth, src, src_oth, gauge,
    )

    def route(where):
        pairs_out = []
        for t in range(4):
            for z in range(2):
                for s in range(2):
                    dt, dz = where(s)
                    to = ((t + dt) % 4) * 4 + ((z + dz) % 2) * 2 + s
                    pairs_out.append((t * 4 + z * 2 + s, to))
        return pairs_out

    axes = ("ta", "gz", "sa")
    xd = lax.ppermute(blk, axes, route(lambda s: (0, 1)))
    xc = lax.ppermute(blk, axes, route(lambda s: (2, s)))
    xb = lax.ppermute(blk, axes, route(lambda s: (-1, s)))
    xa = lax.ppermute(blk, axes, route(lambda s: (1, s)))
    tz = lax.ppermute(mz, axes, route(lambda s: (0, 1)))
    ta = lax.ppermute(up, axes, route(lambda s: (1, 0)))
    tb = lax.ppermute(down, axes, route(lambda s: (-1, 0)))
    acc = call(
        local_kernel,
        [(FIELD, 128)],
        [pltpu.VMEM((36, 8, 128), f32)],
        [vmem] * 4,
        4_000_000,
        3_000_000,
        own, bl, src, gauge,
    )[0]
    xa, xb, xc, xd, acc = lax.optimization_barrier((xa, xb, xc, xd, acc))
    xa2 = lax.ppermute(xa, "sa", swap)
    xb2 = lax.ppermute(xb, "sa", swap)
    xc2 = lax.ppermute(xc, "sa", swap)
    corr = call(
        inner_kernel,
        [(24, 8, 128)],
        [
            pltpu.VMEM((8 * MESSAGE, 128), f32),
            pltpu.VMEM((108, 2, 8, 128), f32),
            pltpu.VMEM((24, 2, 8, 128), f32),
            pltpu.VMEM((8, 24, 2, 8, 128), f32),
            pltpu.VMEM((8, 24, 2, 8, 128), f32),
            pltpu.VMEM((2, 24, 2, 8, 128), f32),
            pltpu.SemaphoreType.DMA((8,)),
        ],
        [anywhere] * 8,
        1_000_000_000,
        1_000_000_000,
        blk, xd, xa, xa2, xb, xb2, xc, xc2,
    )[0]
    residual, corrected = call(
        final_kernel,
        [(FIELD, 128), (FIELD, 128)],
        [pltpu.VMEM((36, 8, 128), f32)],
        [vmem] * 7,
        4_000_000,
        3_000_000,
        own, acc, gauge, ta, tb, tz, corr,
    )
    return (residual.reshape(whole), corrected.reshape(whole))


def solution(mesh):
    placed = (
        P("parts", None, None, "sa", "ta", "gz", None),
        P("parts", None, None, "sa", "ta", "gz", None),
        P("parts", None, "ta", "gz", None),
    )
    small = (mesh.shape["ta"], mesh.shape["gz"], mesh.shape["sa"]) == (4, 2, 2)

    def chosen(iterate, source, gauge_links):
        one_block = iterate.shape[3:] == (12, 1, 1, 256)
        return (small_body if small and one_block else body)(iterate, source, gauge_links)

    return jax.shard_map(
        chosen,
        mesh=mesh,
        in_specs=placed,
        out_specs=(
            P("parts", None, None, "sa", "ta", "gz", None),
            P("parts", None, None, "sa", "ta", "gz", None),
        ),
        check_vma=False,
    )
```

```python
import jax
import jax.numpy as jnp
import numpy as np
from jax import lax
from jax.experimental import pallas as pl
from jax.experimental.pallas import tpu as pltpu
from jax.sharding import PartitionSpec as P

NX = 32
LS = 24
LS8 = 8
ITERS = 3


WALL_HEIGHT = 1.8
OUTER_SCALE = 1.5
OUTER_SHIFT = 0.5
INNER_SCALE = 1.25
INNER_SHIFT = 0.25
QUARK_MASS = 0.05
EPSILON = 1e-06
HIGHEST = lax.Precision.HIGHEST


def padded_2(array, sides, width):
    for axis, dim in sides:
        count, length = (lax.axis_size(axis), array.shape[dim])
        up = [(i, (i + 1) % count) for i in range(count)]
        down = [(j, i) for i, j in up]
        last = lax.slice_in_dim(array, length - width, length, axis=dim)
        first = lax.slice_in_dim(array, 0, width, axis=dim)
        before = lax.ppermute(last, axis, up)
        after = lax.ppermute(first, axis, down)
        array = jnp.concatenate([before, array, after], axis=dim)
    return array


def shifted(block, axis, distance):
    devices = range(lax.axis_size(axis))
    route = [((i - distance) % len(devices), i) for i in devices]
    return lax.ppermute(block, axis, route)


def gamma_tables():
    pauli_list = [
        np.array([[0, 1], [1, 0]], complex),
        np.array([[0, -1j], [1j, 0]], complex),
        np.array([[1, 0], [0, -1]], complex),
    ]
    gammas = []
    for pauli_matrix in pauli_list:
        matrix = np.zeros((4, 4), complex)
        matrix[0:2, 2:4] = -1j * pauli_matrix
        matrix[2:4, 0:2] = 1j * pauli_matrix
        gammas.append(matrix)
    fourth = np.zeros((4, 4), complex)
    fourth[0:2, 2:4] = np.eye(2)
    fourth[2:4, 0:2] = np.eye(2)
    gammas.append(fourth)
    tables = np.zeros((4, 2, 8, 8), np.float32)
    for direction in range(4):
        for sign_slot, sign_value in enumerate((-1.0, 1.0)):
            matrix = np.eye(4) + sign_value * gammas[direction]
            tables[direction, sign_slot, :4, :4] = matrix.real
            tables[direction, sign_slot, :4, 4:] = -matrix.imag
            tables[direction, sign_slot, 4:, :4] = matrix.imag
            tables[direction, sign_slot, 4:, 4:] = matrix.real
    return tables


def spin_apply(matrix, spinor):
    flattened = spinor.reshape((8,) + spinor.shape[2:])
    product = jnp.einsum(
        "pq,q...->p...", jnp.asarray(matrix, spinor.dtype), flattened, precision=HIGHEST
    )
    return product.reshape(spinor.shape)


def color_apply(link_field, spinor, dagger):
    formula = "batzw,sbltzw->saltzw" if dagger else "abtzw,sbltzw->saltzw"

    def contract(matrix_part, spinor_part):
        return jnp.einsum(formula, matrix_part, spinor_part, precision=HIGHEST)

    if dagger:
        real_part = contract(link_field[0], spinor[0]) + contract(link_field[1], spinor[1])
        imag_part = contract(link_field[0], spinor[1]) - contract(link_field[1], spinor[0])
    else:
        real_part = contract(link_field[0], spinor[0]) - contract(link_field[1], spinor[1])
        imag_part = contract(link_field[0], spinor[1]) + contract(link_field[1], spinor[0])
    return jnp.stack([real_part, imag_part])


def along_x(spinor, offset):
    lattice = spinor.reshape(spinor.shape[:-1] + (spinor.shape[-1] // NX, NX))
    return jnp.roll(lattice, -offset, axis=-1).reshape(spinor.shape)


def along_y(spinor, offset):
    lattice = spinor.reshape(spinor.shape[:-1] + (spinor.shape[-1] // NX, NX))
    return jnp.roll(lattice, -offset, axis=-2).reshape(spinor.shape)


def project_plus(spinor):
    return jnp.concatenate([spinor[:, :2], jnp.zeros_like(spinor[:, 2:])], axis=1)


def project_minus(spinor):
    return jnp.concatenate([jnp.zeros_like(spinor[:, :2]), spinor[:, 2:]], axis=1)


def complex_scale(coef_real, coef_imag, spinor):
    return jnp.stack(
        [
            coef_real * spinor[0] - coef_imag * spinor[1],
            coef_real * spinor[1] + coef_imag * spinor[0],
        ]
    )


def padded_rims(padded):
    return (
        padded[:, :, :, :, :1, 1:-1],
        padded[:, :, :, :, -1:, 1:-1],
        padded[:, :, :, :, 1:-1, :1],
        padded[:, :, :, :, 1:-1, -1:],
    )


def time_signs():
    position = lax.axis_index("ta")
    sign_low = jnp.where(position == 0, -1.0, 1.0).astype(jnp.float32)
    sign_high = jnp.where(position == lax.axis_size("ta") - 1, -1.0, 1.0).astype(jnp.float32)
    return (sign_low, sign_high)


def slice_masses():
    position = lax.axis_index("sa")
    mass_low = jnp.where(position == 0, -QUARK_MASS, 1.0).astype(jnp.float32)
    mass_high = jnp.where(position == lax.axis_size("sa") - 1, -QUARK_MASS, 1.0).astype(jnp.float32)
    return (mass_low, mass_high)


def slice_mix(spinor, low_rim, high_rim, mass_low, mass_high):
    lower_part = jnp.concatenate([mass_low * low_rim, spinor[:, :2, :, :-1]], axis=3)
    upper_part = jnp.concatenate([spinor[:, 2:, :, 1:], mass_high * high_rim], axis=3)
    return jnp.concatenate([lower_part, upper_part], axis=1)


def hopping(centre, rims, here_links, down_links, y_forward, y_backward):
    tables = gamma_tables()
    sign_low, sign_high = time_signs()
    low_time, high_time, low_depth, high_depth = rims
    forward = [
        along_x(centre, 1),
        y_forward,
        jnp.concatenate([centre[:, :, :, :, :, 1:], high_depth], axis=5),
        jnp.concatenate([centre[:, :, :, :, 1:], sign_high * high_time], axis=4),
    ]
    backward = [
        along_x(centre, -1),
        y_backward,
        jnp.concatenate([low_depth, centre[:, :, :, :, :, :-1]], axis=5),
        jnp.concatenate([sign_low * low_time, centre[:, :, :, :, :-1]], axis=4),
    ]
    total = (4.0 - WALL_HEIGHT) * centre
    for direction in range(4):
        going = color_apply(here_links[direction], forward[direction], False)
        coming = color_apply(down_links[direction], backward[direction], True)
        total = total - 0.5 * (
            spin_apply(tables[direction, 0], going) + spin_apply(tables[direction, 1], coming)
        )
    return total


def outer_operator(iterate, here_links, down_links):
    mass_low, mass_high = slice_masses()
    with_rims = padded_2(iterate, (("sa", 3),), 1)
    low_rim = with_rims[:, :2, :, :1]
    high_rim = with_rims[:, 2:, :, -1:]
    chiral_mix = slice_mix(iterate, low_rim, high_rim, mass_low, mass_high)
    blended = OUTER_SCALE * iterate + OUTER_SHIFT * chiral_mix
    rims = padded_rims(padded_2(blended, (("ta", 4), ("gz", 5)), 1))
    hopped = hopping(
        blended, rims, here_links, down_links, along_y(blended, 1), along_y(blended, -1)
    )
    return hopped + iterate - chiral_mix


def inner_rows_operator(remainder, here_links, down_links):
    chiral_mix = slice_mix(
        remainder, remainder[:, :2, :, -1:], remainder[:, 2:, :, :1], -QUARK_MASS, -QUARK_MASS
    )
    blended = INNER_SCALE * remainder + INNER_SHIFT * chiral_mix
    rims = padded_rims(padded_2(blended, (("ta", 4), ("gz", 5)), 1))
    row_rims = padded_2(blended, (("sa", 6),), NX)
    y_forward = row_rims[..., 2 * NX :]
    y_backward = row_rims[..., : -2 * NX]
    hopped = hopping(blended, rims, here_links, down_links, y_forward, y_backward)
    return hopped + remainder - chiral_mix


def minimal_residual(inner_source, operator, here_links, down_links):
    correction = jnp.zeros_like(inner_source)
    remainder = inner_source
    for iteration in range(ITERS):
        applied = operator(remainder, here_links, down_links)
        inner_real, inner_imag, weight = lax.psum(
            (
                jnp.sum(applied[0] * remainder[0] + applied[1] * remainder[1]),
                jnp.sum(applied[0] * remainder[1] - applied[1] * remainder[0]),
                jnp.sum(applied * applied),
            ),
            ("ta", "gz", "sa"),
        )
        weight = weight + EPSILON
        alpha_real = inner_real / weight
        alpha_imag = inner_imag / weight
        correction = correction + complex_scale(alpha_real, alpha_imag, remainder)
        remainder = remainder - complex_scale(alpha_real, alpha_imag, applied)
    return correction


def body(iterate, source, gauge_links):
    span = gauge_links.shape[-1]
    link_set = gauge_links.reshape((4, 2, 3, 3) + gauge_links.shape[2:])
    rim_time = shifted(gauge_links[3, :, -1:], "ta", 1)
    rim_depth = shifted(gauge_links[2, :, :, -1:], "gz", 1)
    down_time = jnp.concatenate([rim_time, gauge_links[3, :, :-1]], axis=1).reshape(
        link_set.shape[1:]
    )
    down_depth = jnp.concatenate([rim_depth, gauge_links[2, :, :, :-1]], axis=2).reshape(
        link_set.shape[1:]
    )
    here_links = [link_set[0], link_set[1], link_set[2], link_set[3]]
    down_links = [along_x(link_set[0], -1), along_y(link_set[1], -1), down_depth, down_time]
    residual = source - outer_operator(iterate, here_links, down_links)
    core_index = lax.axis_index("sa")
    local_slices = iterate.shape[3]
    global_slice = core_index * local_slices + jnp.arange(local_slices)
    first_mask = (global_slice == 0).astype(jnp.float32).reshape(-1, 1, 1, 1)
    last_mask = (global_slice == LS - 1).astype(jnp.float32).reshape(-1, 1, 1, 1)
    surface_piece = jnp.where(
        core_index == 0, project_minus(residual[:, :, :, :1]), project_plus(residual[:, :, :, -1:])
    )
    surface_slots = lax.all_to_all(surface_piece, "sa", split_axis=6, concat_axis=3, tiled=True)
    blank = jnp.zeros(surface_slots.shape[:3] + (LS8 - 2,) + surface_slots.shape[4:], jnp.float32)
    inner_source = jnp.concatenate(
        [surface_slots[:, :, :, :1], blank, surface_slots[:, :, :, 1:]], axis=3
    )
    row_width = span // lax.axis_size("sa")
    row_start = core_index * row_width
    here_rows = [
        lax.dynamic_slice_in_dim(link_field, row_start, row_width, 5) for link_field in here_links
    ]
    down_rows = [
        lax.dynamic_slice_in_dim(link_field, row_start, row_width, 5) for link_field in down_links
    ]
    correction = minimal_residual(inner_source, inner_rows_operator, here_rows, down_rows)
    returned = jnp.concatenate(
        [project_minus(correction[:, :, :, :1]), project_plus(correction[:, :, :, -1:])], axis=3
    )
    received = lax.all_to_all(returned, "sa", split_axis=3, concat_axis=6, tiled=True)
    corrected = iterate + received * (first_mask + last_mask)
    return (residual, corrected)


UPPER = [ri * 12 + sp * 3 + c for ri in range(2) for sp in (0, 1) for c in range(3)]
LOWER = [ri * 12 + sp * 3 + c for ri in range(2) for sp in (2, 3) for c in range(3)]
RE, IM = 0, 1
SPIN = (
    (((1, 1, IM), (-1, 1, RE)), ((1, 0, IM), (-1, 0, RE))),
    (((-1, 1, RE), (-1, 1, IM)), ((1, 0, RE), (1, 0, IM))),
    (((1, 0, IM), (-1, 0, RE)), ((-1, 1, IM), (1, 1, RE))),
    (((1, 0, RE), (1, 0, IM)), ((1, 1, RE), (1, 1, IM))),
)
ROWS = 24
FIELD = 576
LINKS = 72
SENT = 48
BLOCK = SENT + 72
MESSAGE = 2 * BLOCK
WHOLE = 6.0
LINK_SCALE = -0.5 * INNER_SCALE / WHOLE
MIXED = -1.8 * INNER_SCALE / WHOLE
MIXED_FIRST = 2.2 * INNER_SCALE / WHOLE - 1.0
CHI = INNER_SHIFT / INNER_SCALE
VMEM_LIMIT = 48 * 1024 * 1024


def number(part, spin, color):
    return part * 12 + spin * 3 + color


def half_spinor(get, direction, side):
    out = {}
    for spin in range(2):
        for part in range(2):
            sign, from_spin, from_part = SPIN[direction][spin][part]
            for color in range(3):
                up = get(number(part, spin, color))
                low = get(number(from_part, 2 + from_spin, color))
                out[spin, part, color] = up + low if sign * side > 0 else up - low
    return out


def link_times(link, half, dagger):
    out = {}
    for row in range(3):
        for spin in range(2):
            real, imag = (None, None)
            for col in range(3):
                a, b = (col, row) if dagger else (row, col)
                ur, ui = (link(RE, a, b), link(IM, a, b))
                hr, hi = (half[spin, RE, col], half[spin, IM, col])
                if dagger:
                    re_new, im_new = (ur * hr + ui * hi, ur * hi - ui * hr)
                else:
                    re_new, im_new = (ur * hr - ui * hi, ur * hi + ui * hr)
                real = re_new if real is None else real + re_new
                imag = im_new if imag is None else imag + im_new
            out[spin, RE, row] = real
            out[spin, IM, row] = imag
    return out


def link_times_3(link, half, dagger):
    mixed = {}
    for spin in range(2):
        for col in range(3):
            real, imag = (half[spin, RE, col], half[spin, IM, col])
            lead, less = (imag, real - imag) if dagger else (real, imag - real)
            mixed[spin, col] = (lead, less, real + imag)
    out = {}
    for row in range(3):
        for spin in range(2):
            sums = None
            for col in range(3):
                a, b = (col, row) if dagger else (row, col)
                lead, less, both = mixed[spin, col]
                products = (lead * link(2, a, b), less * link(RE, a, b), both * link(IM, a, b))
                sums = products if sums is None else tuple(p + q for p, q in zip(sums, products))
            first, second, third = sums
            out[spin, RE, row] = first + second if dagger else first - third
            out[spin, IM, row] = first - third if dagger else first + second
    return out


def add_hop(acc, half, direction, side):
    flip = 1 if direction == 3 else -1
    for spin in range(2):
        for part in range(2):
            sign, from_spin, from_part = SPIN[direction][spin][part]
            for color in range(3):
                up = number(part, spin, color)
                acc[up] = acc[up] + half[spin, part, color]
                low = number(part, 2 + spin, color)
                g = half[from_spin, from_part, color]
                acc[low] = acc[low] + g if sign * side * flip > 0 else acc[low] - g
    return acc


def roll(x, shift, axis):
    return pltpu.roll(x, shift % x.shape[axis], axis)


def lane():
    return lax.broadcasted_iota(jnp.int32, (8, 128), 1)


def sublane():
    return lax.broadcasted_iota(jnp.int32, (8, 128), 0)


def move_x(x, offset):
    at = lane()
    return jnp.take_along_axis(x, at - at % NX + (at + offset + NX) % NX, axis=1)


def move_y(x, offset):
    near = roll(x, -offset * NX, 1)
    far = jnp.take_along_axis(near, sublane() + 1 - 2 * (sublane() % 2), axis=0)
    edge = lane() // NX == (3 if offset > 0 else 0)
    return jnp.where(edge, far, near)


def move_t(x, offset):
    return roll(x, -offset * 2, 0)


def pairs(x):
    return jnp.concatenate([x, x, x, x], axis=0)


def scaled_links(gauge_ref, tile_ref, slot, direction, scale):
    for entry in range(18):
        row = (direction * 18 + entry) * 2
        tile_ref[slot * 18 + entry] = pairs(gauge_ref[row : row + 2, :]) * scale


def tree_sum(terms):
    while len(terms) > 1:
        terms = [a + b for a, b in zip(terms[::2], terms[1::2])] + terms[len(terms) // 2 * 2 :]
    return terms[0]


def tile_link(tile_ref, slot):
    return lambda part, a, b: tile_ref[slot * 18 + part * 9 + a * 3 + b]


def blend_rows(out_ref, here_ref, there_ref, mass_low, mass_high):
    row = lax.broadcasted_iota(jnp.int32, (ROWS, 128), 0)
    for comp in range(24):
        rows = slice(comp * ROWS, (comp + 1) * ROWS)
        v, other = (here_ref[rows, :], there_ref[rows, :])
        if comp in UPPER:
            chi = jnp.where(row < 2, roll(other, 2, 0) * mass_low, roll(v, 2, 0))
        else:
            chi = jnp.where(row >= ROWS - 2, roll(other, -2, 0) * mass_high, roll(v, -2, 0))
        out_ref[rows, :] = OUTER_SCALE * v + OUTER_SHIFT * chi


def stage_kernel(own_ref, src_ref, gauge_ref, own_out, src_out, gauge_out, sem):
    copies = []
    for i, (ref, out) in enumerate(((own_ref, own_out), (src_ref, src_out), (gauge_ref, gauge_out))):
        copies.append(pltpu.make_async_copy(ref, out, sem.at[i]))
        copies[-1].start()
    for copy in copies:
        copy.wait()


def send_kernel(own_ref, oth_ref, src_own_ref, src_oth_ref, gauge_ref, up_ref, down_ref, mz_ref, blk_ref, bl_ref, blo_ref, tile_ref):
    core = lax.axis_index("sa")
    last_time = lax.axis_index("ta") == lax.axis_size("ta") - 1
    time_scale = jnp.where(last_time, 0.5, -0.5).astype(jnp.float32)
    first = jnp.where(core == 0, -QUARK_MASS, 1.0).astype(jnp.float32)
    last = jnp.where(core == 0, 1.0, -QUARK_MASS).astype(jnp.float32)
    blend_rows(bl_ref, own_ref, oth_ref, first, last)
    blend_rows(blo_ref, oth_ref, own_ref, last, first)

    for h in range(2):
        for i in range(8):
            base = h * BLOCK + i * 6
            blk_ref[base : base + 6, :] = gauge_ref[pl.ds(i * 18 + h, 6, stride=2), :]

    def surfaces(bl0_ref, it0_ref, src0_ref, bl1_ref, it1_ref, src1_ref):
        for h in range(2):
            base = h * BLOCK + SENT
            blk_ref[base : base + 24, :] = bl0_ref[pl.ds(h, 24, stride=ROWS), :]
            blk_ref[base + 24 : base + 48, :] = bl1_ref[pl.ds(22 + h, 24, stride=ROWS), :]
            for part in range(2):
                start = (part * 12 + 6) * ROWS + h
                value = (
                    src0_ref[pl.ds(start, 6, stride=ROWS), :]
                    - it0_ref[pl.ds(start, 6, stride=ROWS), :]
                    + it0_ref[pl.ds(start + 2, 6, stride=ROWS), :]
                )
                blk_ref[base + 48 + part * 6 : base + 54 + part * 6, :] = value
                start = part * 12 * ROWS + 22 + h
                value = (
                    src1_ref[pl.ds(start, 6, stride=ROWS), :]
                    - it1_ref[pl.ds(start, 6, stride=ROWS), :]
                    + it1_ref[pl.ds(start - 2, 6, stride=ROWS), :]
                )
                blk_ref[base + 60 + part * 6 : base + 66 + part * 6, :] = value

    pl.when(core == 0)(lambda: surfaces(bl_ref, own_ref, src_own_ref, blo_ref, oth_ref, src_oth_ref))
    pl.when(core == 1)(lambda: surfaces(blo_ref, oth_ref, src_oth_ref, bl_ref, own_ref, src_own_ref))

    scaled_links(gauge_ref, tile_ref, 0, 2, -0.5)
    scaled_links(gauge_ref, tile_ref, 1, 3, time_scale)

    def store(ref, half, offset, g):
        for (spin, part, color), value in half.items():
            ref[pl.ds(offset + (part * 6 + spin * 3 + color) * ROWS + g * 8, 8), :] = value

    def getter(ref, g):
        return lambda comp: ref[pl.ds(comp * ROWS + g * 8, 8), :]

    for g in range(3):
        get = getter(bl_ref, g)
        store(mz_ref, half_spinor(get, 2, -1), 0, g)
        store(mz_ref, link_times(tile_link(tile_ref, 0), half_spinor(get, 2, 1), True), 288, g)
        store(up_ref, link_times(tile_link(tile_ref, 1), half_spinor(get, 3, 1), True), 0, g)
        store(down_ref, half_spinor(get, 3, -1), 0, g)


def halves(ref, rows, start):
    return {
        (spin, part, color): ref[rows(part * 6 + spin * 3 + color, start), :]
        for spin in range(2)
        for part in range(2)
        for color in range(3)
    }


def group_rows(g):
    at = lambda row: row if isinstance(g, int) else pl.multiple_of(row, 8)
    return lambda comp, start=0: pl.ds(at(start + comp * ROWS + g * 8), 8)


def local_kernel(own_ref, bl_ref, src_ref, gauge_ref, acc_ref, tile_ref):
    scaled_links(gauge_ref, tile_ref, 0, 0, -0.5)
    scaled_links(gauge_ref, tile_ref, 1, 1, -0.5)

    def group(g, carry):
        rows = group_rows(g)
        get = lambda comp: bl_ref[rows(comp), :]
        acc = [0.2 * get(comp) + 4.0 * own_ref[rows(comp), :] - src_ref[rows(comp), :] for comp in range(24)]
        for direction, move in ((0, move_x), (1, move_y)):
            link = tile_link(tile_ref, direction)
            half = {k: move(h, 1) for k, h in half_spinor(get, direction, -1).items()}
            acc = add_hop(acc, link_times(link, half, False), direction, -1)
            half = link_times(link, half_spinor(get, direction, 1), True)
            acc = add_hop(acc, {k: move(h, -1) for k, h in half.items()}, direction, 1)
        for comp in range(24):
            acc_ref[rows(comp), :] = acc[comp]
        return carry

    lax.fori_loop(0, 3, group, 0)


def inner_kernel(own_ref, xd_ref, xa_ref, xa2_ref, xb_ref, xb2_ref, xc_ref, xc2_ref, out_ref, gather_ref, link_ref, base_ref, r_ref, a_ref, z_ref, sem):
    core = lax.axis_index("sa")
    pick = lambda zero, one: jnp.where(core == 0, zero, one)
    placed = (
        (own_ref, 0),
        (xd_ref, 4),
        (xa_ref, pick(3, 7)),
        (xa2_ref, pick(7, 3)),
        (xb_ref, pick(1, 5)),
        (xb2_ref, pick(5, 1)),
        (xc_ref, pick(2, 6)),
        (xc2_ref, pick(6, 2)),
    )
    copies = []
    for i, (ref, slot) in enumerate(placed):
        to = gather_ref.at[pl.ds(pl.multiple_of(slot * MESSAGE, 8), MESSAGE), :]
        copies.append(pltpu.make_async_copy(ref, to, sem.at[i]))
        copies[-1].start()
    zero = jnp.zeros((8, 128), jnp.float32)
    for s in range(1, 7):
        for comp in range(24):
            for dz in range(2):
                r_ref[s, comp, dz] = zero
    for copy in copies:
        copy.wait()

    time = lax.rem(lax.axis_index("ta") + sublane() // 2, 4)
    time_scale = jnp.where(time == 3, -LINK_SCALE, LINK_SCALE).astype(jnp.float32)

    def gathered(comp, dz):
        return gather_ref[pl.ds(dz * 8 * BLOCK + comp, 8, stride=BLOCK), :]

    for dz in range(2):
        for direction in range(4):
            scale = time_scale if direction == 3 else LINK_SCALE
            entry = lambda part, a, b: gathered(direction * 12 + part * 6 + a * 3 + b, dz)
            rows = {(part, a, b): entry(part, a, b) for part in range(2) for a in range(2) for b in range(3)}
            for b in range(3):
                p, q = ((b + 1) % 3, (b + 2) % 3)
                rows[RE, 2, b] = (
                    rows[RE, 0, p] * rows[RE, 1, q] - rows[IM, 0, p] * rows[IM, 1, q]
                    - rows[RE, 0, q] * rows[RE, 1, p] + rows[IM, 0, q] * rows[IM, 1, p]
                )
                rows[IM, 2, b] = (
                    rows[RE, 0, q] * rows[IM, 1, p] + rows[IM, 0, q] * rows[RE, 1, p]
                    - rows[RE, 0, p] * rows[IM, 1, q] - rows[IM, 0, p] * rows[RE, 1, q]
                )
            for a in range(3):
                for b in range(3):
                    real, imag = (rows[RE, a, b] * scale, rows[IM, a, b] * scale)
                    at = direction * 27 + a * 3 + b
                    link_ref[at, dz] = real
                    link_ref[at + 9, dz] = imag
                    link_ref[at + 18, dz] = real + imag
        for comp in range(24):
            r_ref[0, comp, dz] = gathered(SENT + comp, dz) * (1.0 / INNER_SCALE)
            r_ref[7, comp, dz] = gathered(SENT + 24 + comp, dz) * (1.0 / INNER_SCALE)
        for i in range(24):
            base_ref[i, dz] = gathered(SENT + 48 + i, dz)

    def hops(slot, dz, acc):
        def link(direction, at):
            return lambda part, a, b: link_ref[direction * 27 + part * 9 + a * 3 + b, at]

        here = lambda comp: z_ref[slot, comp, dz]
        there = lambda comp: z_ref[slot, comp, 1 - dz]
        for direction, move in ((0, move_x), (1, move_y), (3, move_t)):
            half = {k: move(h, 1) for k, h in half_spinor(here, direction, -1).items()}
            acc = add_hop(acc, link_times_3(link(direction, dz), half, False), direction, -1)
            half = link_times_3(link(direction, dz), half_spinor(here, direction, 1), True)
            acc = add_hop(acc, {k: move(h, -1) for k, h in half.items()}, direction, 1)
        half = half_spinor(there, 2, -1)
        acc = add_hop(acc, link_times_3(link(2, dz), half, False), 2, -1)
        half = link_times_3(link(2, 1 - dz), half_spinor(there, 2, 1), True)
        return add_hop(acc, half, 2, 1)

    for i in range(24):
        out_ref[i] = zero

    def stage(at, carry):
        first = at == 0
        number_f32 = lambda zero, other: jnp.where(first, zero, other).astype(jnp.float32)
        mixed_share = number_f32(MIXED_FIRST, MIXED)
        wall, shift = (number_f32(0.0, -QUARK_MASS * CHI), number_f32(0.0, CHI))
        count = jnp.where(first, 1, at)

        def pair(j, sums):
            low_end = jnp.where(j == 0, wall, shift)
            sides = (
                (j, jnp.where(j == 0, 7, j - 1), j + 1, low_end, shift),
                (7 - j, 6 - j, jnp.where(j == 0, 0, 8 - j), shift, low_end),
            )
            for slot, (s, before, after, low, high) in enumerate(sides):
                for dz in range(2):
                    for comp in range(24):
                        chi = r_ref[before, comp, dz] * low if comp in UPPER else r_ref[after, comp, dz] * high
                        z_ref[slot, comp, dz] = r_ref[s, comp, dz] + chi
            for slot, (s, before, after, low, high) in enumerate(sides):
                for dz in range(2):
                    acc = [r_ref[s, comp, dz] + mixed_share * z_ref[slot, comp, dz] for comp in range(24)]
                    acc = hops(slot, dz, acc)
                    terms = ([], [], [])
                    for i in range(12):
                        ar, ai = (acc[i], acc[i + 12])
                        rr, ri = (r_ref[s, i, dz], r_ref[s, i + 12, dz])
                        terms[0].append(ar * rr + ai * ri)
                        terms[1].append(ar * ri - ai * rr)
                        terms[2].append(ar * ar + ai * ai)
                    sums = tuple(total + tree_sum(part) for total, part in zip(sums, terms))
                    for comp in range(24):
                        a_ref[s, comp, dz] = acc[comp]
            return sums

        real, imag, weight = lax.fori_loop(0, count, pair, (zero, zero, zero))

        @pl.when(first)
        def _():
            for dz in range(2):
                for i in range(12):
                    r_ref[0, LOWER[i], dz] = base_ref[i, dz] - WHOLE * a_ref[0, LOWER[i], dz]
                    r_ref[0, UPPER[i], dz] = zero
                    r_ref[7, UPPER[i], dz] = base_ref[12 + i, dz] - WHOLE * a_ref[7, UPPER[i], dz]
                    r_ref[7, LOWER[i], dz] = zero

        @pl.when(at > 0)
        def _():
            total = lambda x: jnp.sum(x, axis=(0, 1), keepdims=True)
            scale = total(weight) + EPSILON / WHOLE**2
            alpha_real = jnp.broadcast_to(total(real) / scale, (8, 128))
            alpha_imag = jnp.broadcast_to(total(imag) / scale, (8, 128))
            for slot, (s, comps) in enumerate(((0, LOWER), (7, UPPER))):
                for i in range(6):
                    rr, ri = (r_ref[s, comps[i], 0], r_ref[s, comps[i + 6], 0])
                    to = slot * 12 + i
                    out_ref[to] = out_ref[to] + (alpha_real * rr - alpha_imag * ri) * (1.0 / WHOLE)
                    out_ref[to + 6] = out_ref[to + 6] + (alpha_real * ri + alpha_imag * rr) * (1.0 / WHOLE)

            def update(j, c):
                for s in (j, 7 - j):
                    for dz in range(2):
                        for i in range(12):
                            ar, ai = (a_ref[s, i, dz], a_ref[s, i + 12, dz])
                            r_ref[s, i, dz] = r_ref[s, i, dz] - (alpha_real * ar - alpha_imag * ai)
                            r_ref[s, i + 12, dz] = r_ref[s, i + 12, dz] - (alpha_real * ai + alpha_imag * ar)
                return c

            lax.fori_loop(0, jnp.where(at == ITERS, 0, count), update, 0)

        return carry

    lax.fori_loop(0, ITERS + 1, stage, 0)


def final_kernel(own_ref, acc_ref, gauge_ref, up_ref, down_ref, mz_ref, corr_ref, res_out, cor_out, tile_ref, res_ref, cor_ref, sem):
    core = lax.axis_index("sa")
    last_time = lax.axis_index("ta") == lax.axis_size("ta") - 1
    cor_ref[...] = own_ref[...]

    def add_surface(s, comps, first):
        for i, comp in enumerate(comps):
            at = slice(comp * ROWS + 2 * s, comp * ROWS + 2 * s + 2)
            cor_ref[at, :] = cor_ref[at, :] + corr_ref[first + i, 0:2, :]

    pl.when(core == 0)(lambda: add_surface(0, LOWER, 0))
    pl.when(core == 1)(lambda: add_surface(11, UPPER, 12))
    copies = [pltpu.make_async_copy(cor_ref, cor_out, sem.at[3])]
    copies[0].start()
    scaled_links(gauge_ref, tile_ref, 0, 2, -0.5)
    scaled_links(gauge_ref, tile_ref, 1, 3, jnp.where(last_time, 0.5, -0.5).astype(jnp.float32))
    for g in range(3):
        rows = group_rows(g)
        acc = [acc_ref[rows(comp), :] for comp in range(24)]
        acc = add_hop(acc, link_times(tile_link(tile_ref, 0), halves(mz_ref, rows, 0), False), 2, -1)
        acc = add_hop(acc, halves(mz_ref, rows, 288), 2, 1)
        acc = add_hop(acc, link_times(tile_link(tile_ref, 1), halves(down_ref, rows, 0), False), 3, -1)
        acc = add_hop(acc, halves(up_ref, rows, 0), 3, 1)
        for comp in range(24):
            res_ref[g, comp] = -acc[comp]
        copies.append(pltpu.make_async_copy(res_ref.at[g], res_out.at[:, g], sem.at[g]))
        copies[-1].start()
    for copy in copies:
        copy.wait()


def cost(flops, moved):
    return pl.CostEstimate(flops=flops, bytes_accessed=moved, transcendentals=0)


def call(kernel, outs, scratch, in_specs, flops, moved, *args, limit=VMEM_LIMIT, out_space=pltpu.VMEM):
    shapes = [jax.ShapeDtypeStruct(s, jnp.float32) for s in outs]
    return pl.pallas_call(
        kernel,
        out_shape=shapes,
        in_specs=in_specs,
        out_specs=[pl.BlockSpec(memory_space=out_space)] * len(outs),
        scratch_shapes=scratch,
        cost_estimate=cost(flops, moved),
        compiler_params=pltpu.CompilerParams(vmem_limit_bytes=limit),
    )(*args)


def small_body(iterate, source, gauge_links):
    whole = iterate.shape
    own = iterate.reshape(FIELD, 128)
    src = source.reshape(FIELD, 128)
    gauge = gauge_links.reshape(2 * LINKS, 128)
    swap = [(0, 1), (1, 0)]
    oth = lax.ppermute(own, "sa", swap)
    src_oth = lax.ppermute(src, "sa", swap)
    vmem = pl.BlockSpec(memory_space=pltpu.VMEM)
    anywhere = pl.BlockSpec(memory_space=pl.ANY)
    f32 = jnp.float32
    own, src, gauge = call(
        stage_kernel,
        [(FIELD, 128), (FIELD, 128), (2 * LINKS, 128)],
        [pltpu.SemaphoreType.DMA((3,))],
        [pl.BlockSpec(memory_space=pltpu.HBM)] * 3,
        0,
        1_300_000,
        *(pltpu.with_memory_space_constraint(a, pltpu.HBM) for a in (own, src, gauge)),
    )
    up, down, mz, blk, bl = call(
        send_kernel,
        [(FIELD // 2, 128), (FIELD // 2, 128), (FIELD, 128), (MESSAGE, 128), (FIELD, 128)],
        [pltpu.VMEM((FIELD, 128), f32), pltpu.VMEM((36, 8, 128), f32)],
        [vmem] * 5,
        4_000_000,
        3_000_000,
        own, oth, src, src_oth, gauge,
    )

    def route(where):
        pairs_out = []
        for t in range(4):
            for z in range(2):
                for s in range(2):
                    dt, dz = where(s)
                    to = ((t + dt) % 4) * 4 + ((z + dz) % 2) * 2 + s
                    pairs_out.append((t * 4 + z * 2 + s, to))
        return pairs_out

    axes = ("ta", "gz", "sa")
    xd = lax.ppermute(blk, axes, route(lambda s: (0, 1)))
    xc = lax.ppermute(blk, axes, route(lambda s: (2, s)))
    xb = lax.ppermute(blk, axes, route(lambda s: (-1, s)))
    xa = lax.ppermute(blk, axes, route(lambda s: (1, s)))
    tz = lax.ppermute(mz, axes, route(lambda s: (0, 1)))
    ta = lax.ppermute(up, axes, route(lambda s: (1, 0)))
    tb = lax.ppermute(down, axes, route(lambda s: (-1, 0)))
    acc = call(
        local_kernel,
        [(FIELD, 128)],
        [pltpu.VMEM((36, 8, 128), f32)],
        [vmem] * 4,
        4_000_000,
        3_000_000,
        own, bl, src, gauge,
    )[0]
    xa, xb, xc, xd, acc = lax.optimization_barrier((xa, xb, xc, xd, acc))
    xa2 = lax.ppermute(xa, "sa", swap)
    xb2 = lax.ppermute(xb, "sa", swap)
    xc2 = lax.ppermute(xc, "sa", swap)
    corr = call(
        inner_kernel,
        [(24, 8, 128)],
        [
            pltpu.VMEM((8 * MESSAGE, 128), f32),
            pltpu.VMEM((108, 2, 8, 128), f32),
            pltpu.VMEM((24, 2, 8, 128), f32),
            pltpu.VMEM((8, 24, 2, 8, 128), f32),
            pltpu.VMEM((8, 24, 2, 8, 128), f32),
            pltpu.VMEM((2, 24, 2, 8, 128), f32),
            pltpu.SemaphoreType.DMA((8,)),
        ],
        [anywhere] * 8,
        1_000_000_000,
        1_000_000_000,
        blk, xd, xa, xa2, xb, xb2, xc, xc2,
    )[0]
    residual, corrected = call(
        final_kernel,
        [(24, 3, 8, 128), (FIELD, 128)],
        [
            pltpu.VMEM((36, 8, 128), f32),
            pltpu.VMEM((3, 24, 8, 128), f32),
            pltpu.VMEM((FIELD, 128), f32),
            pltpu.SemaphoreType.DMA((4,)),
        ],
        [vmem] * 7,
        4_000_000,
        3_000_000,
        own, acc, gauge, ta, tb, tz, corr,
        out_space=pltpu.HBM,
    )
    return (residual.reshape(whole), corrected.reshape(whole))


def solution(mesh):
    placed = (
        P("parts", None, None, "sa", "ta", "gz", None),
        P("parts", None, None, "sa", "ta", "gz", None),
        P("parts", None, "ta", "gz", None),
    )
    small = (mesh.shape["ta"], mesh.shape["gz"], mesh.shape["sa"]) == (4, 2, 2)

    def chosen(iterate, source, gauge_links):
        one_block = iterate.shape[3:] == (12, 1, 1, 256)
        return (small_body if small and one_block else body)(iterate, source, gauge_links)

    return jax.shard_map(
        chosen,
        mesh=mesh,
        in_specs=placed,
        out_specs=(
            P("parts", None, None, "sa", "ta", "gz", None),
            P("parts", None, None, "sa", "ta", "gz", None),
        ),
        check_vma=False,
    )
```

```python
import jax
import jax.numpy as jnp
import numpy as np
from jax import lax
from jax.experimental import pallas as pl
from jax.experimental.pallas import tpu as pltpu
from jax.sharding import PartitionSpec as P

NX = 32
LS = 24
LS8 = 8
ITERS = 3


WALL_HEIGHT = 1.8
OUTER_SCALE = 1.5
OUTER_SHIFT = 0.5
INNER_SCALE = 1.25
INNER_SHIFT = 0.25
QUARK_MASS = 0.05
EPSILON = 1e-06
HIGHEST = lax.Precision.HIGHEST


def padded_2(array, sides, width):
    for axis, dim in sides:
        count, length = (lax.axis_size(axis), array.shape[dim])
        up = [(i, (i + 1) % count) for i in range(count)]
        down = [(j, i) for i, j in up]
        last = lax.slice_in_dim(array, length - width, length, axis=dim)
        first = lax.slice_in_dim(array, 0, width, axis=dim)
        before = lax.ppermute(last, axis, up)
        after = lax.ppermute(first, axis, down)
        array = jnp.concatenate([before, array, after], axis=dim)
    return array


def shifted(block, axis, distance):
    devices = range(lax.axis_size(axis))
    route = [((i - distance) % len(devices), i) for i in devices]
    return lax.ppermute(block, axis, route)


def gamma_tables():
    pauli_list = [
        np.array([[0, 1], [1, 0]], complex),
        np.array([[0, -1j], [1j, 0]], complex),
        np.array([[1, 0], [0, -1]], complex),
    ]
    gammas = []
    for pauli_matrix in pauli_list:
        matrix = np.zeros((4, 4), complex)
        matrix[0:2, 2:4] = -1j * pauli_matrix
        matrix[2:4, 0:2] = 1j * pauli_matrix
        gammas.append(matrix)
    fourth = np.zeros((4, 4), complex)
    fourth[0:2, 2:4] = np.eye(2)
    fourth[2:4, 0:2] = np.eye(2)
    gammas.append(fourth)
    tables = np.zeros((4, 2, 8, 8), np.float32)
    for direction in range(4):
        for sign_slot, sign_value in enumerate((-1.0, 1.0)):
            matrix = np.eye(4) + sign_value * gammas[direction]
            tables[direction, sign_slot, :4, :4] = matrix.real
            tables[direction, sign_slot, :4, 4:] = -matrix.imag
            tables[direction, sign_slot, 4:, :4] = matrix.imag
            tables[direction, sign_slot, 4:, 4:] = matrix.real
    return tables


def spin_apply(matrix, spinor):
    flattened = spinor.reshape((8,) + spinor.shape[2:])
    product = jnp.einsum(
        "pq,q...->p...", jnp.asarray(matrix, spinor.dtype), flattened, precision=HIGHEST
    )
    return product.reshape(spinor.shape)


def color_apply(link_field, spinor, dagger):
    formula = "batzw,sbltzw->saltzw" if dagger else "abtzw,sbltzw->saltzw"

    def contract(matrix_part, spinor_part):
        return jnp.einsum(formula, matrix_part, spinor_part, precision=HIGHEST)

    if dagger:
        real_part = contract(link_field[0], spinor[0]) + contract(link_field[1], spinor[1])
        imag_part = contract(link_field[0], spinor[1]) - contract(link_field[1], spinor[0])
    else:
        real_part = contract(link_field[0], spinor[0]) - contract(link_field[1], spinor[1])
        imag_part = contract(link_field[0], spinor[1]) + contract(link_field[1], spinor[0])
    return jnp.stack([real_part, imag_part])


def along_x(spinor, offset):
    lattice = spinor.reshape(spinor.shape[:-1] + (spinor.shape[-1] // NX, NX))
    return jnp.roll(lattice, -offset, axis=-1).reshape(spinor.shape)


def along_y(spinor, offset):
    lattice = spinor.reshape(spinor.shape[:-1] + (spinor.shape[-1] // NX, NX))
    return jnp.roll(lattice, -offset, axis=-2).reshape(spinor.shape)


def project_plus(spinor):
    return jnp.concatenate([spinor[:, :2], jnp.zeros_like(spinor[:, 2:])], axis=1)


def project_minus(spinor):
    return jnp.concatenate([jnp.zeros_like(spinor[:, :2]), spinor[:, 2:]], axis=1)


def complex_scale(coef_real, coef_imag, spinor):
    return jnp.stack(
        [
            coef_real * spinor[0] - coef_imag * spinor[1],
            coef_real * spinor[1] + coef_imag * spinor[0],
        ]
    )


def padded_rims(padded):
    return (
        padded[:, :, :, :, :1, 1:-1],
        padded[:, :, :, :, -1:, 1:-1],
        padded[:, :, :, :, 1:-1, :1],
        padded[:, :, :, :, 1:-1, -1:],
    )


def time_signs():
    position = lax.axis_index("ta")
    sign_low = jnp.where(position == 0, -1.0, 1.0).astype(jnp.float32)
    sign_high = jnp.where(position == lax.axis_size("ta") - 1, -1.0, 1.0).astype(jnp.float32)
    return (sign_low, sign_high)


def slice_masses():
    position = lax.axis_index("sa")
    mass_low = jnp.where(position == 0, -QUARK_MASS, 1.0).astype(jnp.float32)
    mass_high = jnp.where(position == lax.axis_size("sa") - 1, -QUARK_MASS, 1.0).astype(jnp.float32)
    return (mass_low, mass_high)


def slice_mix(spinor, low_rim, high_rim, mass_low, mass_high):
    lower_part = jnp.concatenate([mass_low * low_rim, spinor[:, :2, :, :-1]], axis=3)
    upper_part = jnp.concatenate([spinor[:, 2:, :, 1:], mass_high * high_rim], axis=3)
    return jnp.concatenate([lower_part, upper_part], axis=1)


def hopping(centre, rims, here_links, down_links, y_forward, y_backward):
    tables = gamma_tables()
    sign_low, sign_high = time_signs()
    low_time, high_time, low_depth, high_depth = rims
    forward = [
        along_x(centre, 1),
        y_forward,
        jnp.concatenate([centre[:, :, :, :, :, 1:], high_depth], axis=5),
        jnp.concatenate([centre[:, :, :, :, 1:], sign_high * high_time], axis=4),
    ]
    backward = [
        along_x(centre, -1),
        y_backward,
        jnp.concatenate([low_depth, centre[:, :, :, :, :, :-1]], axis=5),
        jnp.concatenate([sign_low * low_time, centre[:, :, :, :, :-1]], axis=4),
    ]
    total = (4.0 - WALL_HEIGHT) * centre
    for direction in range(4):
        going = color_apply(here_links[direction], forward[direction], False)
        coming = color_apply(down_links[direction], backward[direction], True)
        total = total - 0.5 * (
            spin_apply(tables[direction, 0], going) + spin_apply(tables[direction, 1], coming)
        )
    return total


def outer_operator(iterate, here_links, down_links):
    mass_low, mass_high = slice_masses()
    with_rims = padded_2(iterate, (("sa", 3),), 1)
    low_rim = with_rims[:, :2, :, :1]
    high_rim = with_rims[:, 2:, :, -1:]
    chiral_mix = slice_mix(iterate, low_rim, high_rim, mass_low, mass_high)
    blended = OUTER_SCALE * iterate + OUTER_SHIFT * chiral_mix
    rims = padded_rims(padded_2(blended, (("ta", 4), ("gz", 5)), 1))
    hopped = hopping(
        blended, rims, here_links, down_links, along_y(blended, 1), along_y(blended, -1)
    )
    return hopped + iterate - chiral_mix


def inner_rows_operator(remainder, here_links, down_links):
    chiral_mix = slice_mix(
        remainder, remainder[:, :2, :, -1:], remainder[:, 2:, :, :1], -QUARK_MASS, -QUARK_MASS
    )
    blended = INNER_SCALE * remainder + INNER_SHIFT * chiral_mix
    rims = padded_rims(padded_2(blended, (("ta", 4), ("gz", 5)), 1))
    row_rims = padded_2(blended, (("sa", 6),), NX)
    y_forward = row_rims[..., 2 * NX :]
    y_backward = row_rims[..., : -2 * NX]
    hopped = hopping(blended, rims, here_links, down_links, y_forward, y_backward)
    return hopped + remainder - chiral_mix


def minimal_residual(inner_source, operator, here_links, down_links):
    correction = jnp.zeros_like(inner_source)
    remainder = inner_source
    for iteration in range(ITERS):
        applied = operator(remainder, here_links, down_links)
        inner_real, inner_imag, weight = lax.psum(
            (
                jnp.sum(applied[0] * remainder[0] + applied[1] * remainder[1]),
                jnp.sum(applied[0] * remainder[1] - applied[1] * remainder[0]),
                jnp.sum(applied * applied),
            ),
            ("ta", "gz", "sa"),
        )
        weight = weight + EPSILON
        alpha_real = inner_real / weight
        alpha_imag = inner_imag / weight
        correction = correction + complex_scale(alpha_real, alpha_imag, remainder)
        remainder = remainder - complex_scale(alpha_real, alpha_imag, applied)
    return correction


def body(iterate, source, gauge_links):
    span = gauge_links.shape[-1]
    link_set = gauge_links.reshape((4, 2, 3, 3) + gauge_links.shape[2:])
    rim_time = shifted(gauge_links[3, :, -1:], "ta", 1)
    rim_depth = shifted(gauge_links[2, :, :, -1:], "gz", 1)
    down_time = jnp.concatenate([rim_time, gauge_links[3, :, :-1]], axis=1).reshape(
        link_set.shape[1:]
    )
    down_depth = jnp.concatenate([rim_depth, gauge_links[2, :, :, :-1]], axis=2).reshape(
        link_set.shape[1:]
    )
    here_links = [link_set[0], link_set[1], link_set[2], link_set[3]]
    down_links = [along_x(link_set[0], -1), along_y(link_set[1], -1), down_depth, down_time]
    residual = source - outer_operator(iterate, here_links, down_links)
    core_index = lax.axis_index("sa")
    local_slices = iterate.shape[3]
    global_slice = core_index * local_slices + jnp.arange(local_slices)
    first_mask = (global_slice == 0).astype(jnp.float32).reshape(-1, 1, 1, 1)
    last_mask = (global_slice == LS - 1).astype(jnp.float32).reshape(-1, 1, 1, 1)
    surface_piece = jnp.where(
        core_index == 0, project_minus(residual[:, :, :, :1]), project_plus(residual[:, :, :, -1:])
    )
    surface_slots = lax.all_to_all(surface_piece, "sa", split_axis=6, concat_axis=3, tiled=True)
    blank = jnp.zeros(surface_slots.shape[:3] + (LS8 - 2,) + surface_slots.shape[4:], jnp.float32)
    inner_source = jnp.concatenate(
        [surface_slots[:, :, :, :1], blank, surface_slots[:, :, :, 1:]], axis=3
    )
    row_width = span // lax.axis_size("sa")
    row_start = core_index * row_width
    here_rows = [
        lax.dynamic_slice_in_dim(link_field, row_start, row_width, 5) for link_field in here_links
    ]
    down_rows = [
        lax.dynamic_slice_in_dim(link_field, row_start, row_width, 5) for link_field in down_links
    ]
    correction = minimal_residual(inner_source, inner_rows_operator, here_rows, down_rows)
    returned = jnp.concatenate(
        [project_minus(correction[:, :, :, :1]), project_plus(correction[:, :, :, -1:])], axis=3
    )
    received = lax.all_to_all(returned, "sa", split_axis=3, concat_axis=6, tiled=True)
    corrected = iterate + received * (first_mask + last_mask)
    return (residual, corrected)


UPPER = [ri * 12 + sp * 3 + c for ri in range(2) for sp in (0, 1) for c in range(3)]
LOWER = [ri * 12 + sp * 3 + c for ri in range(2) for sp in (2, 3) for c in range(3)]
RE, IM = 0, 1
SPIN = (
    (((1, 1, IM), (-1, 1, RE)), ((1, 0, IM), (-1, 0, RE))),
    (((-1, 1, RE), (-1, 1, IM)), ((1, 0, RE), (1, 0, IM))),
    (((1, 0, IM), (-1, 0, RE)), ((-1, 1, IM), (1, 1, RE))),
    (((1, 0, RE), (1, 0, IM)), ((1, 1, RE), (1, 1, IM))),
)
ROWS = 24
FIELD = 576
LINKS = 72
SENT = 48
BLOCK = SENT + 72
MESSAGE = 2 * BLOCK
WHOLE = 6.0
LINK_SCALE = -0.5 * INNER_SCALE / WHOLE
MIXED = -1.8 * INNER_SCALE / WHOLE
MIXED_FIRST = 2.2 * INNER_SCALE / WHOLE - 1.0
CHI = INNER_SHIFT / INNER_SCALE
VMEM_LIMIT = 48 * 1024 * 1024


def number(part, spin, color):
    return part * 12 + spin * 3 + color


def half_spinor(get, direction, side):
    out = {}
    for spin in range(2):
        for part in range(2):
            sign, from_spin, from_part = SPIN[direction][spin][part]
            for color in range(3):
                up = get(number(part, spin, color))
                low = get(number(from_part, 2 + from_spin, color))
                out[spin, part, color] = up + low if sign * side > 0 else up - low
    return out


def link_times(link, half, dagger):
    out = {}
    for row in range(3):
        for spin in range(2):
            real, imag = (None, None)
            for col in range(3):
                a, b = (col, row) if dagger else (row, col)
                ur, ui = (link(RE, a, b), link(IM, a, b))
                hr, hi = (half[spin, RE, col], half[spin, IM, col])
                if dagger:
                    re_new, im_new = (ur * hr + ui * hi, ur * hi - ui * hr)
                else:
                    re_new, im_new = (ur * hr - ui * hi, ur * hi + ui * hr)
                real = re_new if real is None else real + re_new
                imag = im_new if imag is None else imag + im_new
            out[spin, RE, row] = real
            out[spin, IM, row] = imag
    return out


def link_times_3(link, half, dagger):
    mixed = {}
    for spin in range(2):
        for col in range(3):
            real, imag = (half[spin, RE, col], half[spin, IM, col])
            lead, less = (imag, real - imag) if dagger else (real, imag - real)
            mixed[spin, col] = (lead, less, real + imag)
    out = {}
    for row in range(3):
        for spin in range(2):
            sums = None
            for col in range(3):
                a, b = (col, row) if dagger else (row, col)
                lead, less, both = mixed[spin, col]
                products = (lead * link(2, a, b), less * link(RE, a, b), both * link(IM, a, b))
                sums = products if sums is None else tuple(p + q for p, q in zip(sums, products))
            first, second, third = sums
            out[spin, RE, row] = first + second if dagger else first - third
            out[spin, IM, row] = first - third if dagger else first + second
    return out


def add_hop(acc, half, direction, side):
    flip = 1 if direction == 3 else -1
    for spin in range(2):
        for part in range(2):
            sign, from_spin, from_part = SPIN[direction][spin][part]
            for color in range(3):
                up = number(part, spin, color)
                acc[up] = acc[up] + half[spin, part, color]
                low = number(part, 2 + spin, color)
                g = half[from_spin, from_part, color]
                acc[low] = acc[low] + g if sign * side * flip > 0 else acc[low] - g
    return acc


def roll(x, shift, axis):
    return pltpu.roll(x, shift % x.shape[axis], axis)


def lane():
    return lax.broadcasted_iota(jnp.int32, (8, 128), 1)


def sublane():
    return lax.broadcasted_iota(jnp.int32, (8, 128), 0)


def move_x(x, offset):
    at = lane()
    return jnp.take_along_axis(x, at - at % NX + (at + offset + NX) % NX, axis=1)


def move_y(x, offset):
    near = roll(x, -offset * NX, 1)
    far = jnp.take_along_axis(near, sublane() + 1 - 2 * (sublane() % 2), axis=0)
    edge = lane() // NX == (3 if offset > 0 else 0)
    return jnp.where(edge, far, near)


def move_t(x, offset):
    return roll(x, -offset * 2, 0)


def pairs(x):
    return jnp.concatenate([x, x, x, x], axis=0)


def scaled_links(gauge_ref, tile_ref, slot, direction, scale):
    for entry in range(18):
        row = (direction * 18 + entry) * 2
        tile_ref[slot * 18 + entry] = pairs(gauge_ref[row : row + 2, :]) * scale


def tree_sum(terms):
    while len(terms) > 1:
        terms = [a + b for a, b in zip(terms[::2], terms[1::2])] + terms[len(terms) // 2 * 2 :]
    return terms[0]


def tile_link(tile_ref, slot):
    return lambda part, a, b: tile_ref[slot * 18 + part * 9 + a * 3 + b]


def blend_rows(out_ref, here_ref, there_ref, mass_low, mass_high):
    row = lax.broadcasted_iota(jnp.int32, (ROWS, 128), 0)
    for comp in range(24):
        rows = slice(comp * ROWS, (comp + 1) * ROWS)
        v, other = (here_ref[rows, :], there_ref[rows, :])
        if comp in UPPER:
            chi = jnp.where(row < 2, roll(other, 2, 0) * mass_low, roll(v, 2, 0))
        else:
            chi = jnp.where(row >= ROWS - 2, roll(other, -2, 0) * mass_high, roll(v, -2, 0))
        out_ref[rows, :] = OUTER_SCALE * v + OUTER_SHIFT * chi


def stage_kernel(own_ref, src_ref, gauge_ref, own_out, src_out, gauge_out, sem):
    copies = []
    for i, (ref, out) in enumerate(((own_ref, own_out), (src_ref, src_out), (gauge_ref, gauge_out))):
        copies.append(pltpu.make_async_copy(ref, out, sem.at[i]))
        copies[-1].start()
    for copy in copies:
        copy.wait()


def halo_kernel(own_ref, oth_ref, gauge_ref, up_ref, down_ref, mz_ref, bl_ref, blo_ref, tile_ref):
    core = lax.axis_index("sa")
    last_time = lax.axis_index("ta") == lax.axis_size("ta") - 1
    time_scale = jnp.where(last_time, 0.5, -0.5).astype(jnp.float32)
    first = jnp.where(core == 0, -QUARK_MASS, 1.0).astype(jnp.float32)
    last = jnp.where(core == 0, 1.0, -QUARK_MASS).astype(jnp.float32)
    blend_rows(bl_ref, own_ref, oth_ref, first, last)
    blend_rows(blo_ref, oth_ref, own_ref, last, first)

    scaled_links(gauge_ref, tile_ref, 0, 2, -0.5)
    scaled_links(gauge_ref, tile_ref, 1, 3, time_scale)

    def store(ref, half, offset, g):
        for (spin, part, color), value in half.items():
            ref[pl.ds(offset + (part * 6 + spin * 3 + color) * ROWS + g * 8, 8), :] = value

    def getter(ref, g):
        return lambda comp: ref[pl.ds(comp * ROWS + g * 8, 8), :]

    for g in range(3):
        get = getter(bl_ref, g)
        store(mz_ref, half_spinor(get, 2, -1), 0, g)
        store(mz_ref, link_times(tile_link(tile_ref, 0), half_spinor(get, 2, 1), True), 288, g)
        store(up_ref, link_times(tile_link(tile_ref, 1), half_spinor(get, 3, 1), True), 0, g)
        store(down_ref, half_spinor(get, 3, -1), 0, g)


def block_kernel(own_ref, oth_ref, src_own_ref, src_oth_ref, gauge_ref, bl_ref, blo_ref, blk_ref):
    core = lax.axis_index("sa")
    for h in range(2):
        for i in range(8):
            base = h * BLOCK + i * 6
            blk_ref[base : base + 6, :] = gauge_ref[pl.ds(i * 18 + h, 6, stride=2), :]

    def surfaces(bl0_ref, it0_ref, src0_ref, bl1_ref, it1_ref, src1_ref):
        for h in range(2):
            base = h * BLOCK + SENT
            blk_ref[base : base + 24, :] = bl0_ref[pl.ds(h, 24, stride=ROWS), :]
            blk_ref[base + 24 : base + 48, :] = bl1_ref[pl.ds(22 + h, 24, stride=ROWS), :]
            for part in range(2):
                start = (part * 12 + 6) * ROWS + h
                value = (
                    src0_ref[pl.ds(start, 6, stride=ROWS), :]
                    - it0_ref[pl.ds(start, 6, stride=ROWS), :]
                    + it0_ref[pl.ds(start + 2, 6, stride=ROWS), :]
                )
                blk_ref[base + 48 + part * 6 : base + 54 + part * 6, :] = value
                start = part * 12 * ROWS + 22 + h
                value = (
                    src1_ref[pl.ds(start, 6, stride=ROWS), :]
                    - it1_ref[pl.ds(start, 6, stride=ROWS), :]
                    + it1_ref[pl.ds(start - 2, 6, stride=ROWS), :]
                )
                blk_ref[base + 60 + part * 6 : base + 66 + part * 6, :] = value

    pl.when(core == 0)(lambda: surfaces(bl_ref, own_ref, src_own_ref, blo_ref, oth_ref, src_oth_ref))
    pl.when(core == 1)(lambda: surfaces(blo_ref, oth_ref, src_oth_ref, bl_ref, own_ref, src_own_ref))


def halves(ref, rows, start):
    return {
        (spin, part, color): ref[rows(part * 6 + spin * 3 + color, start), :]
        for spin in range(2)
        for part in range(2)
        for color in range(3)
    }


def group_rows(g):
    at = lambda row: row if isinstance(g, int) else pl.multiple_of(row, 8)
    return lambda comp, start=0: pl.ds(at(start + comp * ROWS + g * 8), 8)


def local_kernel(own_ref, bl_ref, src_ref, gauge_ref, acc_ref, tile_ref):
    scaled_links(gauge_ref, tile_ref, 0, 0, -0.5)
    scaled_links(gauge_ref, tile_ref, 1, 1, -0.5)

    def group(g, carry):
        rows = group_rows(g)
        get = lambda comp: bl_ref[rows(comp), :]
        acc = [0.2 * get(comp) + 4.0 * own_ref[rows(comp), :] - src_ref[rows(comp), :] for comp in range(24)]
        for direction, move in ((0, move_x), (1, move_y)):
            link = tile_link(tile_ref, direction)
            half = {k: move(h, 1) for k, h in half_spinor(get, direction, -1).items()}
            acc = add_hop(acc, link_times(link, half, False), direction, -1)
            half = link_times(link, half_spinor(get, direction, 1), True)
            acc = add_hop(acc, {k: move(h, -1) for k, h in half.items()}, direction, 1)
        for comp in range(24):
            acc_ref[rows(comp), :] = acc[comp]
        return carry

    lax.fori_loop(0, 3, group, 0)


def inner_kernel(own_ref, xd_ref, xa_ref, xa2_ref, xb_ref, xb2_ref, xc_ref, xc2_ref, out_ref, gather_ref, link_ref, base_ref, r_ref, a_ref, z_ref, sem):
    core = lax.axis_index("sa")
    pick = lambda zero, one: jnp.where(core == 0, zero, one)
    placed = (
        (own_ref, 0),
        (xd_ref, 4),
        (xa_ref, pick(3, 7)),
        (xa2_ref, pick(7, 3)),
        (xb_ref, pick(1, 5)),
        (xb2_ref, pick(5, 1)),
        (xc_ref, pick(2, 6)),
        (xc2_ref, pick(6, 2)),
    )
    copies = []
    for i, (ref, slot) in enumerate(placed):
        to = gather_ref.at[pl.ds(pl.multiple_of(slot * MESSAGE, 8), MESSAGE), :]
        copies.append(pltpu.make_async_copy(ref, to, sem.at[i]))
        copies[-1].start()
    zero = jnp.zeros((8, 128), jnp.float32)
    for s in range(1, 7):
        for comp in range(24):
            for dz in range(2):
                r_ref[s, comp, dz] = zero
    for copy in copies:
        copy.wait()

    time = lax.rem(lax.axis_index("ta") + sublane() // 2, 4)
    time_scale = jnp.where(time == 3, -LINK_SCALE, LINK_SCALE).astype(jnp.float32)

    def gathered(comp, dz):
        return gather_ref[pl.ds(dz * 8 * BLOCK + comp, 8, stride=BLOCK), :]

    for dz in range(2):
        for direction in range(4):
            scale = time_scale if direction == 3 else LINK_SCALE
            entry = lambda part, a, b: gathered(direction * 12 + part * 6 + a * 3 + b, dz)
            rows = {(part, a, b): entry(part, a, b) for part in range(2) for a in range(2) for b in range(3)}
            for b in range(3):
                p, q = ((b + 1) % 3, (b + 2) % 3)
                rows[RE, 2, b] = (
                    rows[RE, 0, p] * rows[RE, 1, q] - rows[IM, 0, p] * rows[IM, 1, q]
                    - rows[RE, 0, q] * rows[RE, 1, p] + rows[IM, 0, q] * rows[IM, 1, p]
                )
                rows[IM, 2, b] = (
                    rows[RE, 0, q] * rows[IM, 1, p] + rows[IM, 0, q] * rows[RE, 1, p]
                    - rows[RE, 0, p] * rows[IM, 1, q] - rows[IM, 0, p] * rows[RE, 1, q]
                )
            for a in range(3):
                for b in range(3):
                    real, imag = (rows[RE, a, b] * scale, rows[IM, a, b] * scale)
                    at = direction * 27 + a * 3 + b
                    link_ref[at, dz] = real
                    link_ref[at + 9, dz] = imag
                    link_ref[at + 18, dz] = real + imag
        for comp in range(24):
            r_ref[0, comp, dz] = gathered(SENT + comp, dz) * (1.0 / INNER_SCALE)
            r_ref[7, comp, dz] = gathered(SENT + 24 + comp, dz) * (1.0 / INNER_SCALE)
        for i in range(24):
            base_ref[i, dz] = gathered(SENT + 48 + i, dz)

    def hops(slot, dz, acc):
        def link(direction, at):
            return lambda part, a, b: link_ref[direction * 27 + part * 9 + a * 3 + b, at]

        here = lambda comp: z_ref[slot, comp, dz]
        there = lambda comp: z_ref[slot, comp, 1 - dz]
        for direction, move in ((0, move_x), (1, move_y), (3, move_t)):
            half = {k: move(h, 1) for k, h in half_spinor(here, direction, -1).items()}
            acc = add_hop(acc, link_times_3(link(direction, dz), half, False), direction, -1)
            half = link_times_3(link(direction, dz), half_spinor(here, direction, 1), True)
            acc = add_hop(acc, {k: move(h, -1) for k, h in half.items()}, direction, 1)
        half = half_spinor(there, 2, -1)
        acc = add_hop(acc, link_times_3(link(2, dz), half, False), 2, -1)
        half = link_times_3(link(2, 1 - dz), half_spinor(there, 2, 1), True)
        return add_hop(acc, half, 2, 1)

    for i in range(24):
        out_ref[i] = zero

    def stage(at, carry):
        first = at == 0
        number_f32 = lambda zero, other: jnp.where(first, zero, other).astype(jnp.float32)
        mixed_share = number_f32(MIXED_FIRST, MIXED)
        wall, shift = (number_f32(0.0, -QUARK_MASS * CHI), number_f32(0.0, CHI))
        count = jnp.where(first, 1, at)

        def pair(j, sums):
            low_end = jnp.where(j == 0, wall, shift)
            sides = (
                (j, jnp.where(j == 0, 7, j - 1), j + 1, low_end, shift),
                (7 - j, 6 - j, jnp.where(j == 0, 0, 8 - j), shift, low_end),
            )
            for slot, (s, before, after, low, high) in enumerate(sides):
                for dz in range(2):
                    for comp in range(24):
                        chi = r_ref[before, comp, dz] * low if comp in UPPER else r_ref[after, comp, dz] * high
                        z_ref[slot, comp, dz] = r_ref[s, comp, dz] + chi
            for slot, (s, before, after, low, high) in enumerate(sides):
                for dz in range(2):
                    acc = [r_ref[s, comp, dz] + mixed_share * z_ref[slot, comp, dz] for comp in range(24)]
                    acc = hops(slot, dz, acc)
                    terms = ([], [], [])
                    for i in range(12):
                        ar, ai = (acc[i], acc[i + 12])
                        rr, ri = (r_ref[s, i, dz], r_ref[s, i + 12, dz])
                        terms[0].append(ar * rr + ai * ri)
                        terms[1].append(ar * ri - ai * rr)
                        terms[2].append(ar * ar + ai * ai)
                    sums = tuple(total + tree_sum(part) for total, part in zip(sums, terms))
                    for comp in range(24):
                        a_ref[s, comp, dz] = acc[comp]
            return sums

        real, imag, weight = lax.fori_loop(0, count, pair, (zero, zero, zero))

        @pl.when(first)
        def _():
            for dz in range(2):
                for i in range(12):
                    r_ref[0, LOWER[i], dz] = base_ref[i, dz] - WHOLE * a_ref[0, LOWER[i], dz]
                    r_ref[0, UPPER[i], dz] = zero
                    r_ref[7, UPPER[i], dz] = base_ref[12 + i, dz] - WHOLE * a_ref[7, UPPER[i], dz]
                    r_ref[7, LOWER[i], dz] = zero

        @pl.when(at > 0)
        def _():
            total = lambda x: jnp.sum(x, axis=(0, 1), keepdims=True)
            scale = total(weight) + EPSILON / WHOLE**2
            alpha_real = jnp.broadcast_to(total(real) / scale, (8, 128))
            alpha_imag = jnp.broadcast_to(total(imag) / scale, (8, 128))
            for slot, (s, comps) in enumerate(((0, LOWER), (7, UPPER))):
                for i in range(6):
                    rr, ri = (r_ref[s, comps[i], 0], r_ref[s, comps[i + 6], 0])
                    to = slot * 12 + i
                    out_ref[to] = out_ref[to] + (alpha_real * rr - alpha_imag * ri) * (1.0 / WHOLE)
                    out_ref[to + 6] = out_ref[to + 6] + (alpha_real * ri + alpha_imag * rr) * (1.0 / WHOLE)

            def update(j, c):
                for s in (j, 7 - j):
                    for dz in range(2):
                        for i in range(12):
                            ar, ai = (a_ref[s, i, dz], a_ref[s, i + 12, dz])
                            r_ref[s, i, dz] = r_ref[s, i, dz] - (alpha_real * ar - alpha_imag * ai)
                            r_ref[s, i + 12, dz] = r_ref[s, i + 12, dz] - (alpha_real * ai + alpha_imag * ar)
                return c

            lax.fori_loop(0, jnp.where(at == ITERS, 0, count), update, 0)

        return carry

    lax.fori_loop(0, ITERS + 1, stage, 0)


def final_kernel(own_ref, acc_ref, gauge_ref, up_ref, down_ref, mz_ref, corr_ref, res_out, cor_out, tile_ref, res_ref, cor_ref, sem):
    core = lax.axis_index("sa")
    last_time = lax.axis_index("ta") == lax.axis_size("ta") - 1
    cor_ref[...] = own_ref[...]

    def add_surface(s, comps, first):
        for i, comp in enumerate(comps):
            at = slice(comp * ROWS + 2 * s, comp * ROWS + 2 * s + 2)
            cor_ref[at, :] = cor_ref[at, :] + corr_ref[first + i, 0:2, :]

    pl.when(core == 0)(lambda: add_surface(0, LOWER, 0))
    pl.when(core == 1)(lambda: add_surface(11, UPPER, 12))
    copies = [pltpu.make_async_copy(cor_ref, cor_out, sem.at[3])]
    copies[0].start()
    scaled_links(gauge_ref, tile_ref, 0, 2, -0.5)
    scaled_links(gauge_ref, tile_ref, 1, 3, jnp.where(last_time, 0.5, -0.5).astype(jnp.float32))
    for g in range(3):
        rows = group_rows(g)
        acc = [acc_ref[rows(comp), :] for comp in range(24)]
        acc = add_hop(acc, link_times(tile_link(tile_ref, 0), halves(mz_ref, rows, 0), False), 2, -1)
        acc = add_hop(acc, halves(mz_ref, rows, 288), 2, 1)
        acc = add_hop(acc, link_times(tile_link(tile_ref, 1), halves(down_ref, rows, 0), False), 3, -1)
        acc = add_hop(acc, halves(up_ref, rows, 0), 3, 1)
        for comp in range(24):
            res_ref[g, comp] = -acc[comp]
        copies.append(pltpu.make_async_copy(res_ref.at[g], res_out.at[:, g], sem.at[g]))
        copies[-1].start()
    for copy in copies:
        copy.wait()


def cost(flops, moved):
    return pl.CostEstimate(flops=flops, bytes_accessed=moved, transcendentals=0)


def call(kernel, outs, scratch, in_specs, flops, moved, *args, limit=VMEM_LIMIT, out_space=pltpu.VMEM):
    shapes = [jax.ShapeDtypeStruct(s, jnp.float32) for s in outs]
    return pl.pallas_call(
        kernel,
        out_shape=shapes,
        in_specs=in_specs,
        out_specs=[pl.BlockSpec(memory_space=out_space)] * len(outs),
        scratch_shapes=scratch,
        cost_estimate=cost(flops, moved),
        compiler_params=pltpu.CompilerParams(vmem_limit_bytes=limit),
    )(*args)


def small_body(iterate, source, gauge_links):
    whole = iterate.shape
    own = iterate.reshape(FIELD, 128)
    src = source.reshape(FIELD, 128)
    gauge = gauge_links.reshape(2 * LINKS, 128)
    swap = [(0, 1), (1, 0)]
    oth = lax.ppermute(own, "sa", swap)
    src_oth = lax.ppermute(src, "sa", swap)
    vmem = pl.BlockSpec(memory_space=pltpu.VMEM)
    anywhere = pl.BlockSpec(memory_space=pl.ANY)
    f32 = jnp.float32
    own, src, gauge = call(
        stage_kernel,
        [(FIELD, 128), (FIELD, 128), (2 * LINKS, 128)],
        [pltpu.SemaphoreType.DMA((3,))],
        [pl.BlockSpec(memory_space=pltpu.HBM)] * 3,
        0,
        1_300_000,
        *(pltpu.with_memory_space_constraint(a, pltpu.HBM) for a in (own, src, gauge)),
    )
    up, down, mz, bl, blo = call(
        halo_kernel,
        [(FIELD // 2, 128), (FIELD // 2, 128), (FIELD, 128), (FIELD, 128), (FIELD, 128)],
        [pltpu.VMEM((36, 8, 128), f32)],
        [vmem] * 3,
        4_000_000,
        2_000_000,
        own, oth, gauge,
    )
    blk = call(
        block_kernel,
        [(MESSAGE, 128)],
        [],
        [vmem] * 7,
        100_000,
        300_000,
        own, oth, src, src_oth, gauge, bl, blo,
    )[0]

    def route(where):
        pairs_out = []
        for t in range(4):
            for z in range(2):
                for s in range(2):
                    dt, dz = where(s)
                    to = ((t + dt) % 4) * 4 + ((z + dz) % 2) * 2 + s
                    pairs_out.append((t * 4 + z * 2 + s, to))
        return pairs_out

    axes = ("ta", "gz", "sa")
    xd = lax.ppermute(blk, axes, route(lambda s: (0, 1)))
    xc = lax.ppermute(blk, axes, route(lambda s: (2, s)))
    xb = lax.ppermute(blk, axes, route(lambda s: (-1, s)))
    xa = lax.ppermute(blk, axes, route(lambda s: (1, s)))
    tz = lax.ppermute(mz, axes, route(lambda s: (0, 1)))
    ta = lax.ppermute(up, axes, route(lambda s: (1, 0)))
    tb = lax.ppermute(down, axes, route(lambda s: (-1, 0)))
    acc = call(
        local_kernel,
        [(FIELD, 128)],
        [pltpu.VMEM((36, 8, 128), f32)],
        [vmem] * 4,
        4_000_000,
        3_000_000,
        own, bl, src, gauge,
    )[0]
    xa, xb, xc, xd, acc = lax.optimization_barrier((xa, xb, xc, xd, acc))
    xa2 = lax.ppermute(xa, "sa", swap)
    xb2 = lax.ppermute(xb, "sa", swap)
    xc2 = lax.ppermute(xc, "sa", swap)
    corr = call(
        inner_kernel,
        [(24, 8, 128)],
        [
            pltpu.VMEM((8 * MESSAGE, 128), f32),
            pltpu.VMEM((108, 2, 8, 128), f32),
            pltpu.VMEM((24, 2, 8, 128), f32),
            pltpu.VMEM((8, 24, 2, 8, 128), f32),
            pltpu.VMEM((8, 24, 2, 8, 128), f32),
            pltpu.VMEM((2, 24, 2, 8, 128), f32),
            pltpu.SemaphoreType.DMA((8,)),
        ],
        [anywhere] * 8,
        1_000_000_000,
        1_000_000_000,
        blk, xd, xa, xa2, xb, xb2, xc, xc2,
    )[0]
    residual, corrected = call(
        final_kernel,
        [(24, 3, 8, 128), (FIELD, 128)],
        [
            pltpu.VMEM((36, 8, 128), f32),
            pltpu.VMEM((3, 24, 8, 128), f32),
            pltpu.VMEM((FIELD, 128), f32),
            pltpu.SemaphoreType.DMA((4,)),
        ],
        [vmem] * 7,
        4_000_000,
        3_000_000,
        own, acc, gauge, ta, tb, tz, corr,
        out_space=pltpu.HBM,
    )
    return (residual.reshape(whole), corrected.reshape(whole))


def solution(mesh):
    placed = (
        P("parts", None, None, "sa", "ta", "gz", None),
        P("parts", None, None, "sa", "ta", "gz", None),
        P("parts", None, "ta", "gz", None),
    )
    small = (mesh.shape["ta"], mesh.shape["gz"], mesh.shape["sa"]) == (4, 2, 2)

    def chosen(iterate, source, gauge_links):
        one_block = iterate.shape[3:] == (12, 1, 1, 256)
        return (small_body if small and one_block else body)(iterate, source, gauge_links)

    return jax.shard_map(
        chosen,
        mesh=mesh,
        in_specs=placed,
        out_specs=(
            P("parts", None, None, "sa", "ta", "gz", None),
            P("parts", None, None, "sa", "ta", "gz", None),
        ),
        check_vma=False,
    )
```

```python
import jax
import jax.numpy as jnp
import numpy as np
from jax import lax
from jax.experimental import pallas as pl
from jax.experimental.pallas import tpu as pltpu
from jax.sharding import PartitionSpec as P

NX = 32
LS = 24
LS8 = 8
ITERS = 3


WALL_HEIGHT = 1.8
OUTER_SCALE = 1.5
OUTER_SHIFT = 0.5
INNER_SCALE = 1.25
INNER_SHIFT = 0.25
QUARK_MASS = 0.05
EPSILON = 1e-06
HIGHEST = lax.Precision.HIGHEST


def padded_2(array, sides, width):
    for axis, dim in sides:
        count, length = (lax.axis_size(axis), array.shape[dim])
        up = [(i, (i + 1) % count) for i in range(count)]
        down = [(j, i) for i, j in up]
        last = lax.slice_in_dim(array, length - width, length, axis=dim)
        first = lax.slice_in_dim(array, 0, width, axis=dim)
        before = lax.ppermute(last, axis, up)
        after = lax.ppermute(first, axis, down)
        array = jnp.concatenate([before, array, after], axis=dim)
    return array


def shifted(block, axis, distance):
    devices = range(lax.axis_size(axis))
    route = [((i - distance) % len(devices), i) for i in devices]
    return lax.ppermute(block, axis, route)


def gamma_tables():
    pauli_list = [
        np.array([[0, 1], [1, 0]], complex),
        np.array([[0, -1j], [1j, 0]], complex),
        np.array([[1, 0], [0, -1]], complex),
    ]
    gammas = []
    for pauli_matrix in pauli_list:
        matrix = np.zeros((4, 4), complex)
        matrix[0:2, 2:4] = -1j * pauli_matrix
        matrix[2:4, 0:2] = 1j * pauli_matrix
        gammas.append(matrix)
    fourth = np.zeros((4, 4), complex)
    fourth[0:2, 2:4] = np.eye(2)
    fourth[2:4, 0:2] = np.eye(2)
    gammas.append(fourth)
    tables = np.zeros((4, 2, 8, 8), np.float32)
    for direction in range(4):
        for sign_slot, sign_value in enumerate((-1.0, 1.0)):
            matrix = np.eye(4) + sign_value * gammas[direction]
            tables[direction, sign_slot, :4, :4] = matrix.real
            tables[direction, sign_slot, :4, 4:] = -matrix.imag
            tables[direction, sign_slot, 4:, :4] = matrix.imag
            tables[direction, sign_slot, 4:, 4:] = matrix.real
    return tables


def spin_apply(matrix, spinor):
    flattened = spinor.reshape((8,) + spinor.shape[2:])
    product = jnp.einsum(
        "pq,q...->p...", jnp.asarray(matrix, spinor.dtype), flattened, precision=HIGHEST
    )
    return product.reshape(spinor.shape)


def color_apply(link_field, spinor, dagger):
    formula = "batzw,sbltzw->saltzw" if dagger else "abtzw,sbltzw->saltzw"

    def contract(matrix_part, spinor_part):
        return jnp.einsum(formula, matrix_part, spinor_part, precision=HIGHEST)

    if dagger:
        real_part = contract(link_field[0], spinor[0]) + contract(link_field[1], spinor[1])
        imag_part = contract(link_field[0], spinor[1]) - contract(link_field[1], spinor[0])
    else:
        real_part = contract(link_field[0], spinor[0]) - contract(link_field[1], spinor[1])
        imag_part = contract(link_field[0], spinor[1]) + contract(link_field[1], spinor[0])
    return jnp.stack([real_part, imag_part])


def along_x(spinor, offset):
    lattice = spinor.reshape(spinor.shape[:-1] + (spinor.shape[-1] // NX, NX))
    return jnp.roll(lattice, -offset, axis=-1).reshape(spinor.shape)


def along_y(spinor, offset):
    lattice = spinor.reshape(spinor.shape[:-1] + (spinor.shape[-1] // NX, NX))
    return jnp.roll(lattice, -offset, axis=-2).reshape(spinor.shape)


def project_plus(spinor):
    return jnp.concatenate([spinor[:, :2], jnp.zeros_like(spinor[:, 2:])], axis=1)


def project_minus(spinor):
    return jnp.concatenate([jnp.zeros_like(spinor[:, :2]), spinor[:, 2:]], axis=1)


def complex_scale(coef_real, coef_imag, spinor):
    return jnp.stack(
        [
            coef_real * spinor[0] - coef_imag * spinor[1],
            coef_real * spinor[1] + coef_imag * spinor[0],
        ]
    )


def padded_rims(padded):
    return (
        padded[:, :, :, :, :1, 1:-1],
        padded[:, :, :, :, -1:, 1:-1],
        padded[:, :, :, :, 1:-1, :1],
        padded[:, :, :, :, 1:-1, -1:],
    )


def time_signs():
    position = lax.axis_index("ta")
    sign_low = jnp.where(position == 0, -1.0, 1.0).astype(jnp.float32)
    sign_high = jnp.where(position == lax.axis_size("ta") - 1, -1.0, 1.0).astype(jnp.float32)
    return (sign_low, sign_high)


def slice_masses():
    position = lax.axis_index("sa")
    mass_low = jnp.where(position == 0, -QUARK_MASS, 1.0).astype(jnp.float32)
    mass_high = jnp.where(position == lax.axis_size("sa") - 1, -QUARK_MASS, 1.0).astype(jnp.float32)
    return (mass_low, mass_high)


def slice_mix(spinor, low_rim, high_rim, mass_low, mass_high):
    lower_part = jnp.concatenate([mass_low * low_rim, spinor[:, :2, :, :-1]], axis=3)
    upper_part = jnp.concatenate([spinor[:, 2:, :, 1:], mass_high * high_rim], axis=3)
    return jnp.concatenate([lower_part, upper_part], axis=1)


def hopping(centre, rims, here_links, down_links, y_forward, y_backward):
    tables = gamma_tables()
    sign_low, sign_high = time_signs()
    low_time, high_time, low_depth, high_depth = rims
    forward = [
        along_x(centre, 1),
        y_forward,
        jnp.concatenate([centre[:, :, :, :, :, 1:], high_depth], axis=5),
        jnp.concatenate([centre[:, :, :, :, 1:], sign_high * high_time], axis=4),
    ]
    backward = [
        along_x(centre, -1),
        y_backward,
        jnp.concatenate([low_depth, centre[:, :, :, :, :, :-1]], axis=5),
        jnp.concatenate([sign_low * low_time, centre[:, :, :, :, :-1]], axis=4),
    ]
    total = (4.0 - WALL_HEIGHT) * centre
    for direction in range(4):
        going = color_apply(here_links[direction], forward[direction], False)
        coming = color_apply(down_links[direction], backward[direction], True)
        total = total - 0.5 * (
            spin_apply(tables[direction, 0], going) + spin_apply(tables[direction, 1], coming)
        )
    return total


def outer_operator(iterate, here_links, down_links):
    mass_low, mass_high = slice_masses()
    with_rims = padded_2(iterate, (("sa", 3),), 1)
    low_rim = with_rims[:, :2, :, :1]
    high_rim = with_rims[:, 2:, :, -1:]
    chiral_mix = slice_mix(iterate, low_rim, high_rim, mass_low, mass_high)
    blended = OUTER_SCALE * iterate + OUTER_SHIFT * chiral_mix
    rims = padded_rims(padded_2(blended, (("ta", 4), ("gz", 5)), 1))
    hopped = hopping(
        blended, rims, here_links, down_links, along_y(blended, 1), along_y(blended, -1)
    )
    return hopped + iterate - chiral_mix


def inner_rows_operator(remainder, here_links, down_links):
    chiral_mix = slice_mix(
        remainder, remainder[:, :2, :, -1:], remainder[:, 2:, :, :1], -QUARK_MASS, -QUARK_MASS
    )
    blended = INNER_SCALE * remainder + INNER_SHIFT * chiral_mix
    rims = padded_rims(padded_2(blended, (("ta", 4), ("gz", 5)), 1))
    row_rims = padded_2(blended, (("sa", 6),), NX)
    y_forward = row_rims[..., 2 * NX :]
    y_backward = row_rims[..., : -2 * NX]
    hopped = hopping(blended, rims, here_links, down_links, y_forward, y_backward)
    return hopped + remainder - chiral_mix


def minimal_residual(inner_source, operator, here_links, down_links):
    correction = jnp.zeros_like(inner_source)
    remainder = inner_source
    for iteration in range(ITERS):
        applied = operator(remainder, here_links, down_links)
        inner_real, inner_imag, weight = lax.psum(
            (
                jnp.sum(applied[0] * remainder[0] + applied[1] * remainder[1]),
                jnp.sum(applied[0] * remainder[1] - applied[1] * remainder[0]),
                jnp.sum(applied * applied),
            ),
            ("ta", "gz", "sa"),
        )
        weight = weight + EPSILON
        alpha_real = inner_real / weight
        alpha_imag = inner_imag / weight
        correction = correction + complex_scale(alpha_real, alpha_imag, remainder)
        remainder = remainder - complex_scale(alpha_real, alpha_imag, applied)
    return correction


def body(iterate, source, gauge_links):
    span = gauge_links.shape[-1]
    link_set = gauge_links.reshape((4, 2, 3, 3) + gauge_links.shape[2:])
    rim_time = shifted(gauge_links[3, :, -1:], "ta", 1)
    rim_depth = shifted(gauge_links[2, :, :, -1:], "gz", 1)
    down_time = jnp.concatenate([rim_time, gauge_links[3, :, :-1]], axis=1).reshape(
        link_set.shape[1:]
    )
    down_depth = jnp.concatenate([rim_depth, gauge_links[2, :, :, :-1]], axis=2).reshape(
        link_set.shape[1:]
    )
    here_links = [link_set[0], link_set[1], link_set[2], link_set[3]]
    down_links = [along_x(link_set[0], -1), along_y(link_set[1], -1), down_depth, down_time]
    residual = source - outer_operator(iterate, here_links, down_links)
    core_index = lax.axis_index("sa")
    local_slices = iterate.shape[3]
    global_slice = core_index * local_slices + jnp.arange(local_slices)
    first_mask = (global_slice == 0).astype(jnp.float32).reshape(-1, 1, 1, 1)
    last_mask = (global_slice == LS - 1).astype(jnp.float32).reshape(-1, 1, 1, 1)
    surface_piece = jnp.where(
        core_index == 0, project_minus(residual[:, :, :, :1]), project_plus(residual[:, :, :, -1:])
    )
    surface_slots = lax.all_to_all(surface_piece, "sa", split_axis=6, concat_axis=3, tiled=True)
    blank = jnp.zeros(surface_slots.shape[:3] + (LS8 - 2,) + surface_slots.shape[4:], jnp.float32)
    inner_source = jnp.concatenate(
        [surface_slots[:, :, :, :1], blank, surface_slots[:, :, :, 1:]], axis=3
    )
    row_width = span // lax.axis_size("sa")
    row_start = core_index * row_width
    here_rows = [
        lax.dynamic_slice_in_dim(link_field, row_start, row_width, 5) for link_field in here_links
    ]
    down_rows = [
        lax.dynamic_slice_in_dim(link_field, row_start, row_width, 5) for link_field in down_links
    ]
    correction = minimal_residual(inner_source, inner_rows_operator, here_rows, down_rows)
    returned = jnp.concatenate(
        [project_minus(correction[:, :, :, :1]), project_plus(correction[:, :, :, -1:])], axis=3
    )
    received = lax.all_to_all(returned, "sa", split_axis=3, concat_axis=6, tiled=True)
    corrected = iterate + received * (first_mask + last_mask)
    return (residual, corrected)


UPPER = [ri * 12 + sp * 3 + c for ri in range(2) for sp in (0, 1) for c in range(3)]
LOWER = [ri * 12 + sp * 3 + c for ri in range(2) for sp in (2, 3) for c in range(3)]
RE, IM = 0, 1
SPIN = (
    (((1, 1, IM), (-1, 1, RE)), ((1, 0, IM), (-1, 0, RE))),
    (((-1, 1, RE), (-1, 1, IM)), ((1, 0, RE), (1, 0, IM))),
    (((1, 0, IM), (-1, 0, RE)), ((-1, 1, IM), (1, 1, RE))),
    (((1, 0, RE), (1, 0, IM)), ((1, 1, RE), (1, 1, IM))),
)
ROWS = 24
FIELD = 576
LINKS = 72
SENT = 48
BLOCK = SENT + 72
MESSAGE = 2 * BLOCK
WHOLE = 6.0
LINK_SCALE = -0.5 * INNER_SCALE / WHOLE
MIXED = -1.8 * INNER_SCALE / WHOLE
MIXED_FIRST = 2.2 * INNER_SCALE / WHOLE - 1.0
CHI = INNER_SHIFT / INNER_SCALE
VMEM_LIMIT = 48 * 1024 * 1024


def number(part, spin, color):
    return part * 12 + spin * 3 + color


def half_spinor(get, direction, side):
    out = {}
    for spin in range(2):
        for part in range(2):
            sign, from_spin, from_part = SPIN[direction][spin][part]
            for color in range(3):
                up = get(number(part, spin, color))
                low = get(number(from_part, 2 + from_spin, color))
                out[spin, part, color] = up + low if sign * side > 0 else up - low
    return out


def link_times(link, half, dagger):
    out = {}
    for row in range(3):
        for spin in range(2):
            real, imag = (None, None)
            for col in range(3):
                a, b = (col, row) if dagger else (row, col)
                ur, ui = (link(RE, a, b), link(IM, a, b))
                hr, hi = (half[spin, RE, col], half[spin, IM, col])
                if dagger:
                    re_new, im_new = (ur * hr + ui * hi, ur * hi - ui * hr)
                else:
                    re_new, im_new = (ur * hr - ui * hi, ur * hi + ui * hr)
                real = re_new if real is None else real + re_new
                imag = im_new if imag is None else imag + im_new
            out[spin, RE, row] = real
            out[spin, IM, row] = imag
    return out


def link_times_3(link, half, dagger):
    mixed = {}
    for spin in range(2):
        for col in range(3):
            real, imag = (half[spin, RE, col], half[spin, IM, col])
            lead, less = (imag, real - imag) if dagger else (real, imag - real)
            mixed[spin, col] = (lead, less, real + imag)
    out = {}
    for row in range(3):
        for spin in range(2):
            sums = None
            for col in range(3):
                a, b = (col, row) if dagger else (row, col)
                lead, less, both = mixed[spin, col]
                products = (lead * link(2, a, b), less * link(RE, a, b), both * link(IM, a, b))
                sums = products if sums is None else tuple(p + q for p, q in zip(sums, products))
            first, second, third = sums
            out[spin, RE, row] = first + second if dagger else first - third
            out[spin, IM, row] = first - third if dagger else first + second
    return out


def add_hop(acc, half, direction, side):
    flip = 1 if direction == 3 else -1
    for spin in range(2):
        for part in range(2):
            sign, from_spin, from_part = SPIN[direction][spin][part]
            for color in range(3):
                up = number(part, spin, color)
                acc[up] = acc[up] + half[spin, part, color]
                low = number(part, 2 + spin, color)
                g = half[from_spin, from_part, color]
                acc[low] = acc[low] + g if sign * side * flip > 0 else acc[low] - g
    return acc


def roll(x, shift, axis):
    return pltpu.roll(x, shift % x.shape[axis], axis)


def lane():
    return lax.broadcasted_iota(jnp.int32, (8, 128), 1)


def sublane():
    return lax.broadcasted_iota(jnp.int32, (8, 128), 0)


def move_x(x, offset):
    at = lane()
    return jnp.take_along_axis(x, at - at % NX + (at + offset + NX) % NX, axis=1)


def move_y(x, offset):
    near = roll(x, -offset * NX, 1)
    far = jnp.take_along_axis(near, sublane() + 1 - 2 * (sublane() % 2), axis=0)
    edge = lane() // NX == (3 if offset > 0 else 0)
    return jnp.where(edge, far, near)


def move_t(x, offset):
    return roll(x, -offset * 2, 0)


def pairs(x):
    return jnp.concatenate([x, x, x, x], axis=0)


def scaled_links(gauge_ref, tile_ref, slot, direction, scale):
    for entry in range(18):
        row = (direction * 18 + entry) * 2
        tile_ref[slot * 18 + entry] = pairs(gauge_ref[row : row + 2, :]) * scale


def tree_sum(terms):
    while len(terms) > 1:
        terms = [a + b for a, b in zip(terms[::2], terms[1::2])] + terms[len(terms) // 2 * 2 :]
    return terms[0]


def tile_link(tile_ref, slot):
    return lambda part, a, b: tile_ref[slot * 18 + part * 9 + a * 3 + b]


def blend_rows(out_ref, here_ref, there_ref, mass_low, mass_high):
    row = lax.broadcasted_iota(jnp.int32, (ROWS, 128), 0)
    for comp in range(24):
        rows = slice(comp * ROWS, (comp + 1) * ROWS)
        v, other = (here_ref[rows, :], there_ref[rows, :])
        if comp in UPPER:
            chi = jnp.where(row < 2, roll(other, 2, 0) * mass_low, roll(v, 2, 0))
        else:
            chi = jnp.where(row >= ROWS - 2, roll(other, -2, 0) * mass_high, roll(v, -2, 0))
        out_ref[rows, :] = OUTER_SCALE * v + OUTER_SHIFT * chi


def stage_kernel(own_ref, src_ref, gauge_ref, own_out, src_out, gauge_out, sem):
    copies = []
    for i, (ref, out) in enumerate(((own_ref, own_out), (src_ref, src_out), (gauge_ref, gauge_out))):
        copies.append(pltpu.make_async_copy(ref, out, sem.at[i]))
        copies[-1].start()
    for copy in copies:
        copy.wait()


def halo_kernel(own_ref, oth_ref, gauge_ref, up_ref, down_ref, mz_ref, bl_ref, blo_ref, tile_ref):
    core = lax.axis_index("sa")
    last_time = lax.axis_index("ta") == lax.axis_size("ta") - 1
    time_scale = jnp.where(last_time, 0.5, -0.5).astype(jnp.float32)
    first = jnp.where(core == 0, -QUARK_MASS, 1.0).astype(jnp.float32)
    last = jnp.where(core == 0, 1.0, -QUARK_MASS).astype(jnp.float32)
    blend_rows(bl_ref, own_ref, oth_ref, first, last)
    blend_rows(blo_ref, oth_ref, own_ref, last, first)

    scaled_links(gauge_ref, tile_ref, 0, 2, -0.5)
    scaled_links(gauge_ref, tile_ref, 1, 3, time_scale)

    def store(ref, half, offset, g):
        for (spin, part, color), value in half.items():
            ref[pl.ds(offset + (part * 6 + spin * 3 + color) * ROWS + g * 8, 8), :] = value

    def getter(ref, g):
        return lambda comp: ref[pl.ds(comp * ROWS + g * 8, 8), :]

    for g in range(3):
        get = getter(bl_ref, g)
        store(mz_ref, half_spinor(get, 2, -1), 0, g)
        store(mz_ref, link_times(tile_link(tile_ref, 0), half_spinor(get, 2, 1), True), 288, g)
        store(up_ref, link_times(tile_link(tile_ref, 1), half_spinor(get, 3, 1), True), 0, g)
        store(down_ref, half_spinor(get, 3, -1), 0, g)


def block_kernel(own_ref, oth_ref, src_own_ref, src_oth_ref, gauge_ref, bl_ref, blo_ref, blk_ref):
    core = lax.axis_index("sa")
    for h in range(2):
        for i in range(8):
            base = h * BLOCK + i * 6
            blk_ref[base : base + 6, :] = gauge_ref[pl.ds(i * 18 + h, 6, stride=2), :]

    def surfaces(bl0_ref, it0_ref, src0_ref, bl1_ref, it1_ref, src1_ref):
        for h in range(2):
            base = h * BLOCK + SENT
            blk_ref[base : base + 24, :] = bl0_ref[pl.ds(h, 24, stride=ROWS), :]
            blk_ref[base + 24 : base + 48, :] = bl1_ref[pl.ds(22 + h, 24, stride=ROWS), :]
            for part in range(2):
                start = (part * 12 + 6) * ROWS + h
                value = (
                    src0_ref[pl.ds(start, 6, stride=ROWS), :]
                    - it0_ref[pl.ds(start, 6, stride=ROWS), :]
                    + it0_ref[pl.ds(start + 2, 6, stride=ROWS), :]
                )
                blk_ref[base + 48 + part * 6 : base + 54 + part * 6, :] = value
                start = part * 12 * ROWS + 22 + h
                value = (
                    src1_ref[pl.ds(start, 6, stride=ROWS), :]
                    - it1_ref[pl.ds(start, 6, stride=ROWS), :]
                    + it1_ref[pl.ds(start - 2, 6, stride=ROWS), :]
                )
                blk_ref[base + 60 + part * 6 : base + 66 + part * 6, :] = value

    pl.when(core == 0)(lambda: surfaces(bl_ref, own_ref, src_own_ref, blo_ref, oth_ref, src_oth_ref))
    pl.when(core == 1)(lambda: surfaces(blo_ref, oth_ref, src_oth_ref, bl_ref, own_ref, src_own_ref))


def halves(ref, rows, start):
    return {
        (spin, part, color): ref[rows(part * 6 + spin * 3 + color, start), :]
        for spin in range(2)
        for part in range(2)
        for color in range(3)
    }


def group_rows(g):
    at = lambda row: row if isinstance(g, int) else pl.multiple_of(row, 8)
    return lambda comp, start=0: pl.ds(at(start + comp * ROWS + g * 8), 8)


def local_kernel(own_ref, bl_ref, src_ref, gauge_ref, acc_ref, tile_ref):
    scaled_links(gauge_ref, tile_ref, 0, 0, -0.5)
    scaled_links(gauge_ref, tile_ref, 1, 1, -0.5)

    def group(g, carry):
        rows = group_rows(g)
        get = lambda comp: bl_ref[rows(comp), :]
        acc = [0.2 * get(comp) + 4.0 * own_ref[rows(comp), :] - src_ref[rows(comp), :] for comp in range(24)]
        for direction, move in ((0, move_x), (1, move_y)):
            link = tile_link(tile_ref, direction)
            half = {k: move(h, 1) for k, h in half_spinor(get, direction, -1).items()}
            acc = add_hop(acc, link_times(link, half, False), direction, -1)
            half = link_times(link, half_spinor(get, direction, 1), True)
            acc = add_hop(acc, {k: move(h, -1) for k, h in half.items()}, direction, 1)
        for comp in range(24):
            acc_ref[rows(comp), :] = acc[comp]
        return carry

    lax.fori_loop(0, 3, group, 0)


def inner_kernel(own_ref, xd_ref, xa_ref, xa2_ref, xb_ref, xb2_ref, xc_ref, xc2_ref, out_ref, gather_ref, link_ref, base_ref, r_ref, a_ref, z_ref, sem):
    core = lax.axis_index("sa")
    pick = lambda zero, one: jnp.where(core == 0, zero, one)
    placed = (
        (own_ref, 0),
        (xd_ref, 4),
        (xa_ref, pick(3, 7)),
        (xa2_ref, pick(7, 3)),
        (xb_ref, pick(1, 5)),
        (xb2_ref, pick(5, 1)),
        (xc_ref, pick(2, 6)),
        (xc2_ref, pick(6, 2)),
    )
    copies = []
    for i, (ref, slot) in enumerate(placed):
        to = gather_ref.at[pl.ds(pl.multiple_of(slot * MESSAGE, 8), MESSAGE), :]
        copies.append(pltpu.make_async_copy(ref, to, sem.at[i]))
        copies[-1].start()
    zero = jnp.zeros((8, 128), jnp.float32)
    for s in range(1, 7):
        for comp in {3: LOWER, 4: UPPER}.get(s, range(24)):
            for dz in range(2):
                r_ref[s, comp, dz] = zero
    for copy in copies:
        copy.wait()

    time = lax.rem(lax.axis_index("ta") + sublane() // 2, 4)
    time_scale = jnp.where(time == 3, -LINK_SCALE, LINK_SCALE).astype(jnp.float32)

    def gathered(comp, dz):
        return gather_ref[pl.ds(dz * 8 * BLOCK + comp, 8, stride=BLOCK), :]

    for dz in range(2):
        for direction in range(4):
            scale = time_scale if direction == 3 else LINK_SCALE
            entry = lambda part, a, b: gathered(direction * 12 + part * 6 + a * 3 + b, dz)
            rows = {(part, a, b): entry(part, a, b) for part in range(2) for a in range(2) for b in range(3)}
            for b in range(3):
                p, q = ((b + 1) % 3, (b + 2) % 3)
                rows[RE, 2, b] = (
                    rows[RE, 0, p] * rows[RE, 1, q] - rows[IM, 0, p] * rows[IM, 1, q]
                    - rows[RE, 0, q] * rows[RE, 1, p] + rows[IM, 0, q] * rows[IM, 1, p]
                )
                rows[IM, 2, b] = (
                    rows[RE, 0, q] * rows[IM, 1, p] + rows[IM, 0, q] * rows[RE, 1, p]
                    - rows[RE, 0, p] * rows[IM, 1, q] - rows[IM, 0, p] * rows[RE, 1, q]
                )
            for a in range(3):
                for b in range(3):
                    real, imag = (rows[RE, a, b] * scale, rows[IM, a, b] * scale)
                    at = direction * 27 + a * 3 + b
                    link_ref[at, dz] = real
                    link_ref[at + 9, dz] = imag
                    link_ref[at + 18, dz] = real + imag
        for comp in range(24):
            r_ref[0, comp, dz] = gathered(SENT + comp, dz) * (1.0 / INNER_SCALE)
            r_ref[7, comp, dz] = gathered(SENT + 24 + comp, dz) * (1.0 / INNER_SCALE)
        for i in range(24):
            base_ref[i, dz] = gathered(SENT + 48 + i, dz)

    def hops(slot, dz, acc):
        def link(direction, at):
            return lambda part, a, b: link_ref[direction * 27 + part * 9 + a * 3 + b, at]

        here = lambda comp: z_ref[slot, comp, dz]
        there = lambda comp: z_ref[slot, comp, 1 - dz]
        for direction, move in ((0, move_x), (1, move_y), (3, move_t)):
            half = {k: move(h, 1) for k, h in half_spinor(here, direction, -1).items()}
            acc = add_hop(acc, link_times_3(link(direction, dz), half, False), direction, -1)
            half = link_times_3(link(direction, dz), half_spinor(here, direction, 1), True)
            acc = add_hop(acc, {k: move(h, -1) for k, h in half.items()}, direction, 1)
        half = half_spinor(there, 2, -1)
        acc = add_hop(acc, link_times_3(link(2, dz), half, False), 2, -1)
        half = link_times_3(link(2, 1 - dz), half_spinor(there, 2, 1), True)
        return add_hop(acc, half, 2, 1)

    for i in range(24):
        out_ref[i] = zero

    def stage(at, carry):
        first = at == 0
        number_f32 = lambda zero, other: jnp.where(first, zero, other).astype(jnp.float32)
        mixed_share = number_f32(MIXED_FIRST, MIXED)
        wall, shift = (number_f32(0.0, -QUARK_MASS * CHI), number_f32(0.0, CHI))
        count = jnp.where(first, 1, at)

        def pair(j, sums):
            low_end = jnp.where(j == 0, wall, shift)
            sides = (
                (j, jnp.where(j == 0, 7, j - 1), j + 1, low_end, shift),
                (7 - j, 6 - j, jnp.where(j == 0, 0, 8 - j), shift, low_end),
            )
            for slot, (s, before, after, low, high) in enumerate(sides):
                for dz in range(2):
                    for comp in range(24):
                        chi = r_ref[before, comp, dz] * low if comp in UPPER else r_ref[after, comp, dz] * high
                        z_ref[slot, comp, dz] = r_ref[s, comp, dz] + chi
            for slot, (s, before, after, low, high) in enumerate(sides):
                for dz in range(2):
                    acc = [r_ref[s, comp, dz] + mixed_share * z_ref[slot, comp, dz] for comp in range(24)]
                    acc = hops(slot, dz, acc)
                    terms = ([], [], [])
                    for i in range(12):
                        ar, ai = (acc[i], acc[i + 12])
                        rr, ri = (r_ref[s, i, dz], r_ref[s, i + 12, dz])
                        terms[0].append(ar * rr + ai * ri)
                        terms[1].append(ar * ri - ai * rr)
                        terms[2].append(ar * ar + ai * ai)
                    sums = tuple(total + tree_sum(part) for total, part in zip(sums, terms))
                    for comp in range(24):
                        a_ref[s, comp, dz] = acc[comp]
            return sums

        real, imag, weight = lax.fori_loop(0, count, pair, (zero, zero, zero))

        @pl.when(first)
        def _():
            for dz in range(2):
                for i in range(12):
                    r_ref[0, LOWER[i], dz] = base_ref[i, dz] - WHOLE * a_ref[0, LOWER[i], dz]
                    r_ref[0, UPPER[i], dz] = zero
                    r_ref[7, UPPER[i], dz] = base_ref[12 + i, dz] - WHOLE * a_ref[7, UPPER[i], dz]
                    r_ref[7, LOWER[i], dz] = zero

        @pl.when(at > 0)
        def _():
            total = lambda x: jnp.sum(x, axis=(0, 1), keepdims=True)
            scale = total(weight) + EPSILON / WHOLE**2
            alpha_real = jnp.broadcast_to(total(real) / scale, (8, 128))
            alpha_imag = jnp.broadcast_to(total(imag) / scale, (8, 128))
            for slot, (s, comps) in enumerate(((0, LOWER), (7, UPPER))):
                for i in range(6):
                    rr, ri = (r_ref[s, comps[i], 0], r_ref[s, comps[i + 6], 0])
                    to = slot * 12 + i
                    out_ref[to] = out_ref[to] + (alpha_real * rr - alpha_imag * ri) * (1.0 / WHOLE)
                    out_ref[to + 6] = out_ref[to + 6] + (alpha_real * ri + alpha_imag * rr) * (1.0 / WHOLE)

            def update(j, c):
                for s in (j, 7 - j):
                    for dz in range(2):
                        for i in range(12):
                            ar, ai = (a_ref[s, i, dz], a_ref[s, i + 12, dz])
                            r_ref[s, i, dz] = r_ref[s, i, dz] - (alpha_real * ar - alpha_imag * ai)
                            r_ref[s, i + 12, dz] = r_ref[s, i + 12, dz] - (alpha_real * ai + alpha_imag * ar)
                return c

            lax.fori_loop(0, jnp.where(at == ITERS, 0, count), update, 0)

        return carry

    lax.fori_loop(0, ITERS + 1, stage, 0)


def final_kernel(own_ref, acc_ref, gauge_ref, up_ref, down_ref, mz_ref, corr_ref, res_out, cor_out, tile_ref, res_ref, cor_ref, sem):
    core = lax.axis_index("sa")
    last_time = lax.axis_index("ta") == lax.axis_size("ta") - 1
    cor_ref[...] = own_ref[...]

    def add_surface(s, comps, first):
        for i, comp in enumerate(comps):
            at = slice(comp * ROWS + 2 * s, comp * ROWS + 2 * s + 2)
            cor_ref[at, :] = cor_ref[at, :] + corr_ref[first + i, 0:2, :]

    pl.when(core == 0)(lambda: add_surface(0, LOWER, 0))
    pl.when(core == 1)(lambda: add_surface(11, UPPER, 12))
    copies = [pltpu.make_async_copy(cor_ref, cor_out, sem.at[3])]
    copies[0].start()
    scaled_links(gauge_ref, tile_ref, 0, 2, -0.5)
    scaled_links(gauge_ref, tile_ref, 1, 3, jnp.where(last_time, 0.5, -0.5).astype(jnp.float32))
    for g in range(3):
        rows = group_rows(g)
        acc = [acc_ref[rows(comp), :] for comp in range(24)]
        acc = add_hop(acc, link_times(tile_link(tile_ref, 0), halves(mz_ref, rows, 0), False), 2, -1)
        acc = add_hop(acc, halves(mz_ref, rows, 288), 2, 1)
        acc = add_hop(acc, link_times(tile_link(tile_ref, 1), halves(down_ref, rows, 0), False), 3, -1)
        acc = add_hop(acc, halves(up_ref, rows, 0), 3, 1)
        for comp in range(24):
            res_ref[g, comp] = -acc[comp]
        copies.append(pltpu.make_async_copy(res_ref.at[g], res_out.at[:, g], sem.at[g]))
        copies[-1].start()
    for copy in copies:
        copy.wait()


def cost(flops, moved):
    return pl.CostEstimate(flops=flops, bytes_accessed=moved, transcendentals=0)


def call(kernel, outs, scratch, in_specs, flops, moved, *args, limit=VMEM_LIMIT, out_space=pltpu.VMEM):
    shapes = [jax.ShapeDtypeStruct(s, jnp.float32) for s in outs]
    return pl.pallas_call(
        kernel,
        out_shape=shapes,
        in_specs=in_specs,
        out_specs=[pl.BlockSpec(memory_space=out_space)] * len(outs),
        scratch_shapes=scratch,
        cost_estimate=cost(flops, moved),
        compiler_params=pltpu.CompilerParams(vmem_limit_bytes=limit),
    )(*args)


def small_body(iterate, source, gauge_links):
    whole = iterate.shape
    own = iterate.reshape(FIELD, 128)
    src = source.reshape(FIELD, 128)
    gauge = gauge_links.reshape(2 * LINKS, 128)
    swap = [(0, 1), (1, 0)]
    oth = lax.ppermute(own, "sa", swap)
    src_oth = lax.ppermute(src, "sa", swap)
    vmem = pl.BlockSpec(memory_space=pltpu.VMEM)
    anywhere = pl.BlockSpec(memory_space=pl.ANY)
    f32 = jnp.float32
    own, src, gauge = call(
        stage_kernel,
        [(FIELD, 128), (FIELD, 128), (2 * LINKS, 128)],
        [pltpu.SemaphoreType.DMA((3,))],
        [pl.BlockSpec(memory_space=pltpu.HBM)] * 3,
        0,
        1_300_000,
        *(pltpu.with_memory_space_constraint(a, pltpu.HBM) for a in (own, src, gauge)),
    )
    up, down, mz, bl, blo = call(
        halo_kernel,
        [(FIELD // 2, 128), (FIELD // 2, 128), (FIELD, 128), (FIELD, 128), (FIELD, 128)],
        [pltpu.VMEM((36, 8, 128), f32)],
        [vmem] * 3,
        4_000_000,
        2_000_000,
        own, oth, gauge,
    )
    blk = call(
        block_kernel,
        [(MESSAGE, 128)],
        [],
        [vmem] * 7,
        100_000,
        300_000,
        own, oth, src, src_oth, gauge, bl, blo,
    )[0]

    def route(where):
        pairs_out = []
        for t in range(4):
            for z in range(2):
                for s in range(2):
                    dt, dz = where(s)
                    to = ((t + dt) % 4) * 4 + ((z + dz) % 2) * 2 + s
                    pairs_out.append((t * 4 + z * 2 + s, to))
        return pairs_out

    axes = ("ta", "gz", "sa")
    xd = lax.ppermute(blk, axes, route(lambda s: (0, 1)))
    xc = lax.ppermute(blk, axes, route(lambda s: (2, s)))
    xb = lax.ppermute(blk, axes, route(lambda s: (-1, s)))
    xa = lax.ppermute(blk, axes, route(lambda s: (1, s)))
    tz = lax.ppermute(mz, axes, route(lambda s: (0, 1)))
    ta = lax.ppermute(up, axes, route(lambda s: (1, 0)))
    tb = lax.ppermute(down, axes, route(lambda s: (-1, 0)))
    acc = call(
        local_kernel,
        [(FIELD, 128)],
        [pltpu.VMEM((36, 8, 128), f32)],
        [vmem] * 4,
        4_000_000,
        3_000_000,
        own, bl, src, gauge,
    )[0]
    xa, xb, xc, xd, acc = lax.optimization_barrier((xa, xb, xc, xd, acc))
    xa2 = lax.ppermute(xa, "sa", swap)
    xb2 = lax.ppermute(xb, "sa", swap)
    xc2 = lax.ppermute(xc, "sa", swap)
    corr = call(
        inner_kernel,
        [(24, 8, 128)],
        [
            pltpu.VMEM((8 * MESSAGE, 128), f32),
            pltpu.VMEM((108, 2, 8, 128), f32),
            pltpu.VMEM((24, 2, 8, 128), f32),
            pltpu.VMEM((8, 24, 2, 8, 128), f32),
            pltpu.VMEM((8, 24, 2, 8, 128), f32),
            pltpu.VMEM((2, 24, 2, 8, 128), f32),
            pltpu.SemaphoreType.DMA((8,)),
        ],
        [anywhere] * 8,
        1_000_000_000,
        1_000_000_000,
        blk, xd, xa, xa2, xb, xb2, xc, xc2,
    )[0]
    residual, corrected = call(
        final_kernel,
        [(24, 3, 8, 128), (FIELD, 128)],
        [
            pltpu.VMEM((36, 8, 128), f32),
            pltpu.VMEM((3, 24, 8, 128), f32),
            pltpu.VMEM((FIELD, 128), f32),
            pltpu.SemaphoreType.DMA((4,)),
        ],
        [vmem] * 7,
        4_000_000,
        3_000_000,
        own, acc, gauge, ta, tb, tz, corr,
        out_space=pltpu.HBM,
    )
    return (residual.reshape(whole), corrected.reshape(whole))


def solution(mesh):
    placed = (
        P("parts", None, None, "sa", "ta", "gz", None),
        P("parts", None, None, "sa", "ta", "gz", None),
        P("parts", None, "ta", "gz", None),
    )
    small = (mesh.shape["ta"], mesh.shape["gz"], mesh.shape["sa"]) == (4, 2, 2)

    def chosen(iterate, source, gauge_links):
        one_block = iterate.shape[3:] == (12, 1, 1, 256)
        return (small_body if small and one_block else body)(iterate, source, gauge_links)

    return jax.shard_map(
        chosen,
        mesh=mesh,
        in_specs=placed,
        out_specs=(
            P("parts", None, None, "sa", "ta", "gz", None),
            P("parts", None, None, "sa", "ta", "gz", None),
        ),
        check_vma=False,
    )
```
